32 devices in a mesh: dp: 16 (over z, x, core), tensor: 2 (over y).
Axes of the slice: x: 2, y: 2, z: 4, core: 2. Of those that a mesh axis runs over, the one named last changes fastest.
Arguments:
- patches: bfloat16 [5440, 768], P(('dp', 'tensor')), may hold values from -6 to 6
- out_grad: bfloat16 [5440, 768], P(('dp', 'tensor')), may hold values from -6 to 6
- score_grad: bfloat16 [320, 65536], P(None, ('dp', 'tensor')), may hold values from -6 to 6
- crop_size: int32 [320], P('dp'), may hold values from 9 to 49, as said below
- frozen: int32 [65536], P(('dp', 'tensor')), may hold values 0 or 1
- attn_gain: float32 [768], replicated, may hold values from 0.5 to 1.5
- attn_shift: float32 [768], replicated, may hold values from -3 to 3
- qkv_weight: bfloat16 [768, 24, 96], P(None, 'tensor'), may hold values from -0.21875 to 0.21875
- qkv_bias: float32 [24, 64], P('tensor'), may hold values from -3 to 3
- rel_table: float32 [24, 169], P('tensor'), may hold values from -4 to 4
- proj_weight: bfloat16 [24, 32, 768], P('tensor'), may hold values from -0.875 to 0.875
- proj_bias: float32 [768], replicated, may hold values from -3 to 3
- mlp_gain: float32 [768], replicated, may hold values from 0.5 to 1.5
- mlp_shift: float32 [768], replicated, may hold values from -3 to 3
- hidden_weight: bfloat16 [768, 3072], P(None, 'tensor'), may hold values from -0.21875 to 0.21875
- hidden_bias: float32 [3072], P('tensor'), may hold values from -3 to 3
- output_weight: bfloat16 [3072, 768], P('tensor'), may hold values from -0.21875 to 0.21875
- output_bias: float32 [768], replicated, may hold values from -3 to 3
- prototypes: bfloat16 [65536, 768], P(('dp', 'tensor')), may hold values from -6 to 6
Outputs:
- block_out: bfloat16 [5440, 768], P(('dp', 'tensor'))
- patch_grad: float32 [5440, 768], P(('dp', 'tensor'))
- attn_gain_grad: float32 [768], replicated
- attn_shift_grad: float32 [768], replicated
- qkv_weight_grad: float32 [768, 24, 96], P(None, 'tensor')
- qkv_bias_grad: float32 [24, 64], P('tensor')
- rel_table_grad: float32 [24, 169], P('tensor')
- proj_weight_grad: float32 [24, 32, 768], P('tensor')
- proj_bias_grad: float32 [768], replicated
- mlp_gain_grad: float32 [768], replicated
- mlp_shift_grad: float32 [768], replicated
- hidden_weight_grad: float32 [768, 3072], P(None, 'tensor')
- hidden_bias_grad: float32 [3072], P('tensor')
- output_weight_grad: float32 [3072, 768], P('tensor')
- output_bias_grad: float32 [768], replicated
- prototype_grad: float32 [65536, 768], P(('dp', 'tensor'))
The draws below stay inside these ranges and needn't reach their ends.
Inputs may be any that keep to these rules, and one draw needn't show every extreme that they name: `crop_size`: each aligned block of 10 entries, the crops of one device, holds exactly 2 entries 49 and the others 9, in an order drawn from the seed, so that its crops fill exactly the 170 rows of that device.
All inputs are finite; a program needn't handle non-finite values. No bound on the sum of `frozen` on one device may be relied on, other than what follows from the above.
Results may differ from the reference program's by a relative error of at most 0.018.
Values may be sent and summed in bfloat16 or wider, within the bound.
No kernel may reach another device: no remote copies, remote signals or barrier semaphores. Data moves between devices by JAX's collectives and lax.ppermute only.
A program may use at most 448 MiB of HBM per device.

```python
import jax
import jax.numpy as jnp
import numpy as np
from jax import lax

D = 768
HEADS = 24
HS = 32
FF = 3072
PROTOS = 65536
IMG_DEV = 1
CROPS_DEV = 10
BLOCK_ROWS = 340
TOKENS = 5440
CROPS = 320
DEVICES = 32


def draw_crop_size(key, part):
    key = jax.random.fold_in(key, 7)
    pattern = jnp.where(jnp.arange(CROPS_DEV) < 2 * IMG_DEV, 49, 9).astype(jnp.int32)
    device_keys = jax.random.split(key, DEVICES)

    def shuffle(subkey):
        return jax.random.permutation(subkey, pattern)
    return jax.vmap(shuffle)(device_keys).reshape(-1).astype(jnp.int32)


def set_ends(entries, rng, smallest, largest):
    extent = entries.shape
    spot = [jax.random.randint(jax.random.fold_in(rng, axis), (), 0, extent[axis]) for axis in range(len(extent))]
    entries = entries.at[tuple(spot)].set(smallest)
    longest = extent.index(max(extent))
    spot[longest] = (spot[longest] + 1) % extent[longest]
    return entries.at[tuple(spot)].set(largest)


def raised(entries, key, source, target, shards_of, factor):
    def block_of(dim):
        return (jnp.arange(entries.shape[dim]) // (entries.shape[dim] // shards_of)).reshape((-1,) + (1,) * (entries.ndim - 1 - dim))

    one_side = jax.random.permutation(key, shards_of)[block_of(target)]
    other_side = (block_of(target) + shards_of // 2) % shards_of
    return jnp.where((block_of(source) == one_side) | (block_of(source) == other_side), factor * entries, entries)


def block_levels(own_key, dims, shards, smallest, top_value):
    factor_of = 1.0
    for axis_at, shards_of in shards:
        steps = jax.random.uniform(jax.random.fold_in(jax.random.fold_in(own_key, 6), axis_at), (shards_of,), jnp.float32, smallest / len(shards), top_value / len(shards))
        factor_of = factor_of * jnp.repeat(jnp.exp(steps), dims[axis_at] // shards_of).reshape((-1,) + (1,) * (len(dims) - 1 - axis_at))
    return factor_of


def noise(own_key, shape, scale, reach, pieces=(), kind=jnp.bfloat16):
    factor_of = block_levels(own_key, shape, pieces, -0.22, 0.18) if pieces else 1.0
    entries = jax.random.normal(own_key, shape, jnp.float32) * scale * factor_of
    return jnp.minimum(jnp.maximum(entries, -reach), reach).astype(kind)


def bell_draw_with(own_key, extent, width, most, pieces, heavy, kind=jnp.bfloat16):
    drawn = width * jax.random.normal(own_key, extent, jnp.float32)
    if pieces:
        drawn = drawn * block_levels(own_key, extent, pieces, -0.22, 0.18)
    return jnp.clip(raised(drawn, jax.random.fold_in(own_key, 3), *heavy), -most, most).astype(kind)


def setup_inputs(seed: int = 0) -> dict:
    seeds = jax.random.split(jax.random.key(seed), 20)
    patches = noise(seeds[0], (TOKENS, D), 1.0, 6.0, ((0, 32),))
    out_grad = noise(seeds[1], (TOKENS, D), 1.0, 6.0, ((0, 32),))
    score_grad = bell_draw_with(seeds[2], (CROPS, PROTOS), 1.0, 6.0, ((1, 32),), (1, 0, 32, 2.75))
    crop_size = draw_crop_size(jax.random.fold_in(seeds[19], 71), 0)
    frozen = set_ends((jax.random.randint(seeds[4], (PROTOS,), 0, 4) < 1).astype(jnp.int32), jax.random.fold_in(seeds[4], 1), 0, 1)
    attn_gain = jnp.clip(1.0 + 0.1 * jax.random.normal(seeds[5], (D,), jnp.float32), 0.5, 1.5)
    attn_shift = noise(seeds[6], (D,), 0.5, 3.0, (), jnp.float32)
    qkv_weight = noise(seeds[7], (D, HEADS, 3 * HS), D ** -0.5, 0.21875, ((1, 2),))
    qkv_bias = noise(seeds[8], (HEADS, 2 * HS), 0.5, 3.0, ((0, 2),), jnp.float32)
    rel_table = noise(seeds[9], (HEADS, 169), 1.0, 4.0, ((0, 2),), jnp.float32)
    proj_weight = noise(seeds[10], (HEADS, HS, D), (D // 16) ** -0.5, 0.875, ((0, 2),))
    proj_bias = noise(seeds[11], (D,), 0.5, 3.0, (), jnp.float32)
    mlp_gain = jnp.clip(1.0 + 0.1 * jax.random.normal(seeds[12], (D,), jnp.float32), 0.5, 1.5)
    mlp_shift = noise(seeds[13], (D,), 0.5, 3.0, (), jnp.float32)
    hidden_weight = noise(seeds[14], (D, FF), D ** -0.5, 0.21875, ((1, 2),))
    hidden_bias = noise(seeds[15], (FF,), 0.5, 3.0, ((0, 2),), jnp.float32)
    output_weight = noise(seeds[16], (FF, D), (FF // 4) ** -0.5, 0.21875, ((0, 2),))
    output_bias = noise(seeds[17], (D,), 0.5, 3.0, (), jnp.float32)
    prototypes = noise(seeds[18], (PROTOS, D), 1.0, 6.0, ((0, 32),))
    return {"patches": patches, "out_grad": out_grad, "score_grad": score_grad, "crop_size": crop_size, "frozen": frozen, "attn_gain": attn_gain, "attn_shift": attn_shift, "qkv_weight": qkv_weight, "qkv_bias": qkv_bias, "rel_table": rel_table, "proj_weight": proj_weight, "proj_bias": proj_bias, "mlp_gain": mlp_gain, "mlp_shift": mlp_shift, "hidden_weight": hidden_weight, "hidden_bias": hidden_bias, "output_weight": output_weight, "output_bias": output_bias, "prototypes": prototypes}


@jax.custom_vjp
def low(v):
    return lax.optimization_barrier(v.astype(jnp.bfloat16)).astype(jnp.float32)

@jax.custom_vjp
def low_back(v):
    return v

def low_keep(v):
    return (low(v), None)

def low_pass(kept, grad):
    return (grad,)

def back_keep(v):
    return (v, None)

def back_low(kept, grad):
    return (low(grad),)
low.defvjp(low_keep, low_pass)
low_back.defvjp(back_keep, back_low)
HIGH = lax.Precision.HIGHEST
EPS = 1e-05

def layer_norm(values, norm_gain, norm_shift):
    center = values - lax.optimization_barrier(jnp.mean(values, axis=-1, keepdims=True))
    spread = lax.optimization_barrier(jnp.mean(center * center, axis=-1, keepdims=True))
    return center * lax.rsqrt(spread + EPS) * norm_gain + norm_shift

def offset_table():
    places = np.arange(49)
    across = places // 7
    inside = places % 7
    relative = (across[:, None] - across[None, :] + 6) * 13 + (inside[:, None] - inside[None, :] + 6)
    return (relative.reshape(-1)[:, None] == np.arange(169)[None, :]).astype(np.float32)

def crop_layout(crop_sizes, row_count):
    crop_ends = jnp.cumsum(crop_sizes).astype(jnp.int32)
    starts = (crop_ends - crop_sizes).astype(jnp.int32)
    position = jnp.arange(row_count, dtype=jnp.int32)
    segment = jnp.searchsorted(crop_ends, position, side='right').astype(jnp.int32)
    crop_first = starts[segment]
    crop_side = jnp.where(crop_sizes[segment] == 49, 7, 3).astype(jnp.int32)
    offset = position - crop_first
    return (segment, offset // crop_side * 7 + offset % crop_side)

def window_attention(queries, keys_all, values_all, rel_table, segment, crop_place):
    halo_rows = 48
    score_scale = HS ** (-0.5)
    bias_table = jnp.dot(rel_table, jnp.asarray(offset_table()).T, precision=HIGH).reshape(HEADS, 49, 49)
    key_pad = jnp.pad(keys_all, ((halo_rows, halo_rows), (0, 0), (0, 0)))
    value_pad = jnp.pad(values_all, ((halo_rows, halo_rows), (0, 0), (0, 0)))
    segment_pad = jnp.pad(segment, (halo_rows, halo_rows), constant_values=-1)
    place_pad = jnp.pad(crop_place, (halo_rows, halo_rows))
    key_rows = BLOCK_ROWS + 2 * halo_rows

    def one_block(block_index):
        first_row = block_index * BLOCK_ROWS
        block_query = lax.dynamic_slice_in_dim(queries, first_row, BLOCK_ROWS, 0)
        block_keys = lax.dynamic_slice_in_dim(key_pad, first_row, key_rows, 0)
        block_values = lax.dynamic_slice_in_dim(value_pad, first_row, key_rows, 0)
        query_seg = lax.dynamic_slice_in_dim(segment, first_row, BLOCK_ROWS, 0)
        key_seg = lax.dynamic_slice_in_dim(segment_pad, first_row, key_rows, 0)
        query_place = lax.dynamic_slice_in_dim(crop_place, first_row, BLOCK_ROWS, 0)
        key_place = lax.dynamic_slice_in_dim(place_pad, first_row, key_rows, 0)
        scores = jnp.einsum('qhd,khd->hqk', block_query, block_keys, precision=HIGH) * score_scale
        scores = scores + bias_table[:, query_place[:, None], key_place[None, :]]
        same_crop = query_seg[:, None] == key_seg[None, :]
        scores = low_back(jnp.where(same_crop[None], scores, -jnp.inf))
        weights_low = low(jax.nn.softmax(scores, axis=-1))
        return jnp.einsum('hqk,khd->qhd', weights_low, block_values, precision=HIGH)
    blocks = TOKENS // BLOCK_ROWS
    outputs = lax.map(jax.checkpoint(one_block), jnp.arange(blocks, dtype=jnp.int32))
    return outputs.reshape(TOKENS, HEADS, HS)

def block_forward(patches, attn_gain, attn_shift, qkv_weight, qkv_bias, rel_table, proj_weight, proj_bias, mlp_gain, mlp_shift, hidden_weight, hidden_bias, output_weight, output_bias, prototypes, segment, crop_place, crop_sizes):
    normed = low(layer_norm(patches, attn_gain, attn_shift))
    mixed = jnp.dot(normed, qkv_weight.reshape(D, HEADS * 3 * HS), precision=HIGH).reshape(TOKENS, HEADS, 3 * HS)
    middle_zero = jnp.zeros((HEADS, HS), jnp.float32)
    full_bias = jnp.concatenate([qkv_bias[:, :HS], middle_zero.astype(qkv_bias.dtype), qkv_bias[:, HS:]], axis=1)
    mixed = low(low_back(mixed + full_bias))
    attended = window_attention(mixed[:, :, :HS], mixed[:, :, HS:2 * HS], mixed[:, :, 2 * HS:], rel_table, segment, crop_place)
    attended = low(low_back(attended))
    branch = low_back(jnp.dot(attended.reshape(TOKENS, D), proj_weight.reshape(D, D), precision=HIGH))
    middle = patches + branch + proj_bias
    normed_two = low(layer_norm(middle, mlp_gain, mlp_shift))
    before = low_back(jnp.dot(normed_two, hidden_weight, precision=HIGH) + hidden_bias)
    active = low(jax.nn.gelu(before, approximate=False))
    update = low_back(jnp.dot(active, output_weight, precision=HIGH))
    result = middle + update + output_bias
    pooled = low(jax.ops.segment_sum(result, segment, num_segments=CROPS) / crop_sizes[:, None])
    unit = prototypes * lax.rsqrt(lax.optimization_barrier(jnp.sum(prototypes * prototypes, axis=1, keepdims=True)) + 1e-06)
    logits = jnp.dot(pooled, low(unit).T, precision=HIGH)
    return (result, logits)

def reference(patches, out_grad, score_grad, crop_size, frozen, attn_gain, attn_shift, qkv_weight, qkv_bias, rel_table, proj_weight, proj_bias, mlp_gain, mlp_shift, hidden_weight, hidden_bias, output_weight, output_bias, prototypes):
    segment, crop_place = crop_layout(crop_size, TOKENS)
    crop_sizes = crop_size.astype(jnp.float32)
    floats = (patches.astype(jnp.float32), attn_gain, attn_shift, qkv_weight.astype(jnp.float32), qkv_bias, rel_table, proj_weight.astype(jnp.float32), proj_bias, mlp_gain, mlp_shift, hidden_weight.astype(jnp.float32), hidden_bias, output_weight.astype(jnp.float32), output_bias, prototypes.astype(jnp.float32))

    def forward(*params):
        return block_forward(*params, segment, crop_place, crop_sizes)
    (result, logits), pullback = jax.vjp(forward, *floats)
    grads = pullback((out_grad.astype(jnp.float32), score_grad.astype(jnp.float32)))
    keep = (1 - frozen).astype(jnp.float32)[:, None]
    return (result.astype(jnp.bfloat16), grads[0], grads[1], grads[2], grads[3], grads[4], grads[5], grads[6], grads[7], grads[8], grads[9], grads[10], grads[11], grads[12], grads[13], grads[14] * keep)
```

```python
import functools

import jax
import jax.numpy as jnp
import numpy as np
from jax import lax
from jax.experimental import pallas as pl
from jax.experimental.pallas import tpu as pltpu
from jax.sharding import PartitionSpec as P

EPS = 1e-05
BF = jnp.bfloat16
F32 = jnp.float32
HIGH = lax.Precision.HIGHEST
SIDE = 7
PLACES = SIDE * SIDE
OFFSETS = 2 * SIDE - 1
LAST = (SIDE - 1) * (OFFSETS + 1)
SLOTS = 96
LANES = 128
COST = 0.01


def nn(a, b):
    return jnp.dot(a, b, preferred_element_type=F32)


def nt(a, b):
    return lax.dot_general(a, b, (((1,), (1,)), ((), ())), preferred_element_type=F32)


def split(v):
    high = v.astype(BF)
    return high, (v - high.astype(F32)).astype(BF)


def line(ref):
    return ref[...].reshape(1, -1)


def normalize(v):
    center = v - jnp.mean(v, axis=-1, keepdims=True)
    spread = jnp.mean(center * center, axis=-1, keepdims=True)
    inverse = lax.rsqrt(spread + EPS)
    return center * inverse, inverse


def norm_back(hat, inverse, gain, grad):
    scaled = grad * gain
    first = jnp.mean(scaled, axis=-1, keepdims=True)
    second = jnp.mean(scaled * hat, axis=-1, keepdims=True)
    return (scaled - first - hat * second) * inverse


def row_layout(sizes_ref, base, crops, rows, padded, axis):
    shape = (padded, 1) if axis == 0 else (1, padded)
    position = lax.broadcasted_iota(jnp.int32, shape, axis)
    start = jnp.int32(0)
    segment = jnp.zeros(shape, jnp.int32)
    first = jnp.zeros(shape, jnp.int32)
    length = jnp.zeros(shape, jnp.int32)
    for crop in range(crops):
        size = sizes_ref[base + crop]
        reached = position >= start
        segment = jnp.where(reached, crop, segment)
        first = jnp.where(reached, start, first)
        length = jnp.where(reached, size, length)
        start = start + size
    offset = position - first
    by_seven = offset + ((offset * 37) >> 8) * (OFFSETS - SIDE)
    by_three = offset + ((offset * 11) >> 5) * (OFFSETS - 3)
    place = jnp.where(length == PLACES, by_seven, by_three)
    real = position < rows
    segment = jnp.where(real, segment, crops)
    place = jnp.where(real, place, 2 * LANES)
    return segment, place, jnp.where(real, length, 1).astype(F32)


def call(body, grid, ins, outs, scratch, prefetch, args, name, flops, vmem):
    moved = sum(int(np.prod(a.shape)) * a.dtype.itemsize for a in args)
    moved += sum(int(np.prod(s.shape)) * s.dtype.itemsize for s, _ in outs)
    return pl.pallas_call(
        body,
        grid_spec=pltpu.PrefetchScalarGridSpec(
            num_scalar_prefetch=prefetch,
            grid=grid,
            in_specs=ins,
            out_specs=[spec for _, spec in outs],
            scratch_shapes=scratch,
        ),
        out_shape=[shape for shape, _ in outs],
        compiler_params=pltpu.CompilerParams(
            dimension_semantics=("arbitrary",) * len(grid), vmem_limit_bytes=vmem * 2**20
        ),
        cost_estimate=pl.CostEstimate(
            flops=int(flops * COST), bytes_accessed=int(moved * COST), transcendentals=0
        ),
        name=name,
    )(*args)


def whole(shape):
    zeros = (0,) * len(shape)
    return pl.BlockSpec(tuple(shape), lambda *_: zeros)


def sds(shape, dtype):
    return jax.ShapeDtypeStruct(tuple(shape), dtype)


def crop_grad_kernel(groups, crops, bits, ids, score, proto, keep, send, total):
    step = pl.program_id(0)

    @pl.when(step == 0)
    def _():
        total[...] = jnp.zeros_like(total)

    p = proto[...].astype(F32)
    unit = p * lax.rsqrt(jnp.sum(p * p, axis=1, keepdims=True) + 1e-06)
    total[...] += nn(score[...], unit.astype(BF))

    @pl.when(step == pl.num_programs(0) - 1)
    def _():
        odd = (ids[1] & 1) == 1
        for pair in range(groups // 2):
            at = 0
            for bit in bits:
                at = 2 * at + (((pair ^ (ids[1] >> 1)) >> (bit.bit_length() - 2)) & 1)
            first = total[2 * pair * crops : (2 * pair + 1) * crops, :]
            second = total[(2 * pair + 1) * crops : (2 * pair + 2) * crops, :]
            keep[at, 0:crops, :] = jnp.where(odd, second, first)
            send[at, 0:crops, :] = jnp.where(odd, first, second)
            if keep.shape[1] > crops:
                tail = jnp.zeros((keep.shape[1] - crops, keep.shape[2]), F32)
                keep[at, crops:, :] = tail
                send[at, crops:, :] = tail


def table_kernel(heads, scale, ids, rel, tables):
    for h in range(heads):
        line = jnp.concatenate(
            [rel[h : h + 1, :], jnp.zeros((1, 2 * LANES - rel.shape[1]), F32)], axis=1
        )
        line = jnp.broadcast_to(line * scale, (8, 2 * LANES))
        line = pltpu.roll(line, 2 * LANES - LAST % 8, 1)
        line = jnp.broadcast_to(line[0:1, :], (SLOTS, 2 * LANES))
        slid = pltpu.roll(line, 2 * LANES - LAST // 8 * 8, 1, stride=1, stride_axis=0)
        high, low = split(slid[:, 0:LANES])
        tables[2 * h * SLOTS : (2 * h + 1) * SLOTS, :] = high
        tables[(2 * h + 1) * SLOTS : (2 * h + 2) * SLOTS, :] = low


def attend_kernel(
    dims, ids, sizes, x0, gain, shift, w, bias, tables, wp, xo, ho, qo, po, oo, ao, xs, rr, hide
):
    first, rows, padded, heads, head_size, crops, unroll = dims
    wide = 3 * head_size
    step = pl.program_id(0)
    base = ((first + step) ^ ids[0]) * crops
    tail = padded - 8
    xs[tail:padded, :] = jnp.zeros((padded - tail, xs.shape[1]), F32)
    xs[0:rows, :] = x0[0].astype(F32)
    x = xs[...]
    xo[0] = x.astype(BF)
    hat, _ = normalize(x)
    h1 = (hat * line(gain) + line(shift)).astype(BF)
    ho[0] = h1
    mixed = nt(w[...], h1)
    bias_cols = jnp.transpose(bias[...])
    for h in range(heads):
        low = h * wide
        qo[0, low : low + head_size, :] = (
            mixed[low : low + head_size] + bias_cols[0:head_size, h : h + 1]
        ).astype(BF)
        qo[0, low + head_size : low + 2 * head_size, :] = mixed[
            low + head_size : low + 2 * head_size
        ].astype(BF)
        qo[0, low + 2 * head_size : low + wide, :] = (
            mixed[low + 2 * head_size : low + wide] + bias_cols[head_size : 2 * head_size, h : h + 1]
        ).astype(BF)
    seg_row, place_row, _ = row_layout(sizes, base, crops, rows, padded, 1)
    seg_col, place_col, _ = row_layout(sizes, base, crops, rows, padded, 0)
    hide[...] = jnp.where(seg_col == seg_row, 0.0, -jnp.inf).astype(F32)
    lane = lax.broadcasted_iota(jnp.int32, (padded, LANES), 1)
    hot = (lane == place_col).astype(F32).astype(BF)
    slot = lax.broadcasted_iota(jnp.int32, (LANES, padded), 0)
    hot_t = (slot == place_row).astype(F32).astype(BF)

    rr[...] = nn(tables[...], hot_t).astype(BF)
    zeros = jnp.zeros((2 * LANES - 2 * SLOTS - head_size, padded), BF)

    def some_heads(i, carry):
        for u in range(unroll):
            h = i * unroll + u
            slab = qo[0, pl.ds(pl.multiple_of(h * wide, 32), wide), :]
            q = slab[0:head_size]
            v = slab[2 * head_size : wide]
            k = slab[head_size : 2 * head_size]
            left_t = jnp.transpose(jnp.concatenate([k, hot_t[0:SLOTS]], axis=0))
            left = jnp.concatenate([left_t, hot], axis=1)
            biases = rr[pl.ds(pl.multiple_of(h * 2 * SLOTS, 64), 2 * SLOTS), :]
            right = jnp.concatenate([q, biases, zeros], axis=0)
            s = nn(left, right) * (head_size**-0.5) + hide[...]
            e = jnp.exp(s - jnp.max(s, axis=0, keepdims=True))
            p = (e * (1.0 / jnp.sum(e, axis=0, keepdims=True))).astype(BF)
            po[0, h] = p
            oo[0, pl.ds(pl.multiple_of(h * head_size, 32), head_size), :] = nn(v, p).astype(BF)
        return carry

    lax.fori_loop(0, heads // unroll, some_heads, 0)
    ao[0] = nn(jnp.transpose(oo[0]), wp[...]).astype(BF)


def hidden_kernel(
    dims, ids, sizes, x0, x1, a0, a1, b0, b1, g0, g1, *rest,
):
    parts, rows, padded, crops, group_crops = dims
    terms, rest = rest[: 2 * parts], rest[2 * parts :]
    pb, gain, shift, w1, bias1, w2 = rest[:6]
    y1o, gyo, h2o, gzo, mo, guo, gh0, gh1, obo, hbo, gs, cs, total = rest[6:]
    step = pl.program_id(0)

    @pl.when(step == 0)
    def _():
        cs[...] = jnp.zeros_like(cs)
        cs[0 : terms[0].shape[1], :] = sum(term[0] for term in terms)
        high, low = split(cs[...])
        bias_sum = jnp.zeros((1, gs.shape[1]), F32)
        tail, half = padded - 8, parts // 2
        for r in range(parts):
            x, own, other, g = (x0, a0, b1, g0) if r < half else (x1, a1, b0, g1)
            k = r % half
            y1 = x[k].astype(F32) + (own[k].astype(F32) + other[k].astype(F32)) + line(pb)
            y1o[r] = y1
            hat, _ = normalize(y1)
            h2o[r * padded : (r + 1) * padded, :] = (hat * line(gain) + line(shift)).astype(BF)
            base = (ids[0] ^ r) * crops
            segment, _, length = row_layout(sizes, base, crops, rows, padded, 0)
            lane = lax.broadcasted_iota(jnp.int32, (padded, cs.shape[0]), 1)
            mine = (lane == segment + base) & (segment < crops)
            hot = mine.astype(F32).astype(BF)
            gs[tail:padded, :] = jnp.zeros((padded - tail, gs.shape[1]), F32)
            gs[0:rows, :] = g[k].astype(F32)
            gy = gs[...] + (nn(hot, high) + nn(hot, low)) / length
            gyo[r] = gy
            gzo[r * padded : (r + 1) * padded, :] = gy.astype(BF)
            bias_sum = bias_sum + jnp.sum(gy, axis=0, keepdims=True)
        obo[...] = bias_sum
        total[...] = jnp.zeros_like(total)

    u = nn(h2o[...], w1[...]) + bias1[...]
    spread = 0.5 * (1.0 + lax.erf(u * np.float32(np.sqrt(0.5))))
    mo[...] = (u * spread).astype(BF)
    slope = spread + u * (jnp.exp(-0.5 * u * u) * np.float32(1.0 / np.sqrt(2.0 * np.pi)))
    gu = (nt(gzo[...], w2[...]) * slope).astype(BF)
    guo[...] = gu
    hbo[...] = jnp.sum(gu.astype(F32), axis=0, keepdims=True)
    total[...] += nt(gu, w1[...])

    @pl.when(step == pl.num_programs(0) - 1)
    def _():
        half = parts // 2
        for r in range(parts):
            gho = gh0 if r < half else gh1
            gho[r % half] = total[r * padded : (r + 1) * padded, :].astype(BF)


def spot(pair, mine, core, orders):
    spots = []
    for order in orders:
        at = 0
        for bit in order:
            source = pair if bit == order[-1] else pair ^ mine
            at = 2 * at + ((source >> (bit.bit_length() - 2)) & 1)
        spots.append(at)
    return jnp.where(core == 1, spots[1], spots[0])


def put_chunk(keep, send, spots, odd, first, second, at):
    rows = pl.ds(at, first.shape[0])
    keep[spots[0], rows, :] = jnp.where(odd, second, first).astype(BF)
    send[spots[1], rows, :] = jnp.where(odd, first, second).astype(BF)


def pair_spots(pair, rank, orders):
    core, mine = rank & 1, rank >> 1
    return spot(pair, mine, core, orders), spot(pair, mine, 1 - core, orders)


def hidden_grad_kernel(dims, ids, h2, gz, m, gu, keep, send, h2t):
    chunks, chunks_step, wide, orders = dims
    step = pl.program_id(0)
    rank = ids[1] & (chunks - 1)
    odd = (rank & 1) == 1

    @pl.when(step == 0)
    def _():
        h2t[...] = jnp.transpose(h2[...])

    d1 = nn(h2t[...], gu[...])
    n1 = d1.shape[0] // chunks
    steps = d1.shape[1] // wide
    for pair in range(chunks // 2):
        spots = pair_spots(pair, rank, orders)
        for part in range(steps):
            piece = d1[2 * pair * n1 : (2 * pair + 2) * n1, part * wide : (part + 1) * wide]
            at = pl.multiple_of((step * steps + part) * n1, 16)
            put_chunk(keep, send, spots, odd, piece[:n1], piece[n1:], at)
    d2 = nn(jnp.transpose(m[...]), gz[...])
    n2 = d2.shape[0] // chunks_step
    base = keep.shape[1] - d2.shape[1] // wide * n2
    for pair in range(chunks_step // 2):
        spots = pair_spots(step * (chunks_step // 2) + pair, rank, orders)
        for part in range(d2.shape[1] // wide):
            piece = d2[2 * pair * n2 : (2 * pair + 2) * n2, part * wide : (part + 1) * wide]
            put_chunk(keep, send, spots, odd, piece[:n2], piece[n2:], base + part * n2)


def share_kernel(parts, padded, m, w2, zo, total):
    step = pl.program_id(0)

    @pl.when(step == 0)
    def _():
        total[...] = jnp.zeros_like(total)

    total[...] += nn(m[...], w2[...])

    @pl.when(step == pl.num_programs(0) - 1)
    def _():
        for r in range(parts):
            zo[r] = total[r * padded : (r + 1) * padded, :].astype(BF)


def result_kernel(dims, ids, sizes, y1, z0, z1, bias, out, pooled):
    rows, padded, crops = dims
    y = y1[0] + (z0[0].astype(F32) + z1[0].astype(F32)) + line(bias)
    out[...] = y[0:rows, :].astype(BF)
    segment, _, _ = row_layout(sizes, ids[0] * crops, crops, rows, padded, 1)
    crop = lax.broadcasted_iota(jnp.int32, (pooled.shape[1], padded), 0)
    member = ((crop == segment) & (crop < crops)).astype(F32)
    high, low = split(y)
    hot = member.astype(BF)
    count = jnp.maximum(jnp.sum(member, axis=1, keepdims=True), 1.0)
    pooled[0] = ((nn(hot, high) + nn(hot, low)) / count).astype(BF)


def attend_back_kernel(
    dims, ids, sizes, y1, gy, e0, e1, gain, x, qkv, pt, wp, w, g1o, gho, gao, gqo, sums, qb, tt, go, by
):
    first, rows, padded, heads, head_size, crops, unroll = dims
    wide = 3 * head_size
    step = pl.program_id(0)
    base = ((first + step) ^ ids[0]) * crops

    @pl.when(step == 0)
    def _():
        sums[...] = jnp.zeros_like(sums)
        qb[...] = jnp.zeros_like(qb)
        tt[...] = jnp.zeros_like(tt)

    hat2, inv2 = normalize(y1[0])
    grad2 = e0[0].astype(F32) + e1[0].astype(F32)
    gy1 = gy[0] + norm_back(hat2, inv2, line(gain), grad2)
    g1o[0] = gy1
    ga = gy1.astype(BF)
    gao[0] = ga
    sums[2:3, :] += jnp.sum(grad2 * hat2, axis=0, keepdims=True)
    sums[3:4, :] += jnp.sum(grad2, axis=0, keepdims=True)
    sums[4:5, :] += jnp.sum(gy1, axis=0, keepdims=True)
    go[...] = nt(wp[...], ga).astype(BF)
    _, place_row, _ = row_layout(sizes, base, crops, rows, padded, 1)
    _, place_col, _ = row_layout(sizes, base, crops, rows, padded, 0)
    slot = lax.broadcasted_iota(jnp.int32, (SLOTS, padded), 0)
    hot_t = (slot == LAST - place_row).astype(F32).astype(BF)
    lane = lax.broadcasted_iota(jnp.int32, (padded, LANES), 1)
    hot = (lane == place_col).astype(F32).astype(BF)
    zeros_a = jnp.zeros((LANES - wide, padded), BF)
    zeros_b = jnp.zeros((2 * head_size, padded), BF)
    scale = head_size**-0.5

    def some_heads(i, carry):
        for u in range(unroll):
            h = i * unroll + u
            at = pl.multiple_of(h * wide, 32)
            slab = qkv[0, pl.ds(at, wide), :]
            q = slab[0:head_size]
            k = slab[head_size : 2 * head_size]
            goh = go[pl.ds(pl.multiple_of(h * head_size, 32), head_size), :]
            p = pt[0, h]
            slab_t = jnp.transpose(jnp.concatenate([slab, zeros_a], axis=0))
            gp = nn(slab_t, jnp.concatenate([zeros_b, goh, zeros_a], axis=0))
            pf = p.astype(F32)
            both = pf * gp
            gs = (both - pf * jnp.sum(both, axis=0, keepdims=True)).astype(BF)
            gv = nt(goh, p)
            gk = nt(q, gs)
            gqe = nn(jnp.concatenate([k, hot_t], axis=0), gs)
            gqo[0, pl.ds(at, head_size), :] = (gqe[0:head_size] * scale).astype(BF)
            gqo[0, pl.ds(at + head_size, head_size), :] = (gk * scale).astype(BF)
            gqo[0, pl.ds(at + 2 * head_size, head_size), :] = gv.astype(BF)
            by[pl.ds(pl.multiple_of(h * SLOTS, 32), SLOTS), :] = gqe[head_size:]
        return carry

    lax.fori_loop(0, heads // unroll, some_heads, 0)
    high, low = split(by[...])
    tt[...] += nn(high, hot) + nn(low, hot)
    g = gqo[0]
    qb[...] += nt(jnp.ones((8, padded), BF), g)
    gh1 = nn(jnp.transpose(g), w[...])
    gho[0] = gh1.astype(BF)
    hat1, _ = normalize(x[0].astype(F32))
    sums[0:1, :] += jnp.sum(gh1 * hat1, axis=0, keepdims=True)
    sums[1:2, :] += jnp.sum(gh1, axis=0, keepdims=True)


def attend_grad_kernel(
    dims, ids, o0, o1, ga0, ga1, gq0, gq1, h0, h1, u0, u1, q0, q1, t0, t1, ob, hb, keep, send, small, dp, dq
):
    parts, heads, chunks, orders = dims
    half = parts // 2
    dp[...] = jnp.zeros_like(dp)
    dq[...] = jnp.zeros_like(dq)
    for r in range(parts):
        o, ga, gq, h = (o0, ga0, gq0, h0) if r < half else (o1, ga1, gq1, h1)
        dp[...] += nn(o[r % half], ga[r % half])
        dq[...] += nn(gq[r % half], h[r % half])
    n = (dp.shape[0] + dq.shape[0]) // chunks
    edge = dp.shape[0] // n
    rank = ids[1] & (chunks - 1)
    for pair in range(chunks // 2):
        source, at = (dp, 2 * pair * n) if 2 * pair < edge else (dq, (2 * pair - edge) * n)
        put_chunk(
            keep, send, pair_spots(pair, rank, orders), (rank & 1) == 1,
            source[at : at + n, :], source[at + n : at + 2 * n, :], 0,
        )
    width = small.shape[1]
    small[...] = jnp.zeros_like(small)
    small[0:5, :] = u0[0:5, :] + u1[0:5, :]
    small[5:6, :] = ob[...]
    at = 6
    for line in (q0[0:1, :] + q1[0:1, :], hb[...]):
        for low in range(0, line.shape[1], width):
            high = min(low + width, line.shape[1])
            small[at : at + 1, 0 : high - low] = line[:, low:high]
            at += 1
    held = width // (2 * LANES)
    for h in range(heads):
        block = t0[h * SLOTS : (h + 1) * SLOTS, :] + t1[h * SLOTS : (h + 1) * SLOTS, :]
        block = jnp.concatenate([block, jnp.zeros((SLOTS, LANES), F32)], axis=1)
        slid = pltpu.roll(block, 0, 1, stride=1, stride_axis=0)
        low = h % held * 2 * LANES
        small[at + h // held : at + h // held + 1, low : low + 2 * LANES] = jnp.sum(
            slid, axis=0, keepdims=True
        )


def patch_grad_kernel(rows, g1, e0, e1, x, gain, out):
    hat, inv = normalize(x[0].astype(F32))
    grad = g1[0] + norm_back(hat, inv, line(gain), e0[0].astype(F32) + e1[0].astype(F32))
    out[...] = grad[0:rows, :]


def proto_grad_kernel(dims, ids, score, pooled, proto, frozen, out, ordered):
    crops, slots, weights = dims

    @pl.when(pl.program_id(0) == 0)
    def _():
        count = pooled.shape[0]
        column = lax.broadcasted_iota(jnp.int32, (1, count), 1)
        block = column // slots
        device = jnp.zeros((1, count), jnp.int32)
        for k, weight in enumerate(weights):
            device = device + ((block >> k) & 1) * weight
        inside = column - block * slots
        target = jnp.where(inside < crops, (device ^ ids[2]) * crops + inside, -1)
        row = lax.broadcasted_iota(jnp.int32, (ordered.shape[0], count), 0)
        hot = (row == target).astype(F32).astype(BF)
        ordered[...] = nn(hot, pooled[...]).astype(BF)

    keep = (1 - frozen[...]).astype(F32).astype(BF)
    grad = nn(jnp.transpose(score[...] * keep), ordered[...])
    p = proto[...].astype(F32)
    inverse = lax.rsqrt(jnp.sum(p * p, axis=1, keepdims=True) + 1e-06)
    unit = p * inverse
    out[...] = (grad - unit * jnp.sum(unit * grad, axis=1, keepdims=True)) * inverse


def unpack_kernel(layout, group, places, own, other, *outs):
    odd = places[0] == 1
    step = pl.program_id(0)
    pairs, _, wide = own.shape
    for out, first, last, at, n, parts in layout:
        for flag, a, b, c, d in ((False, own, other, 1, 1 + pairs), (True, other, own, 1 + pairs, 1)):

            @pl.when((odd == flag) & (step >= first) & (step < last))
            def _():
                for g in range(group):
                    pair = step * group + g
                    for part in range(parts):
                        rows = slice(at + part * n, at + (part + 1) * n)
                        columns = slice(part * wide, (part + 1) * wide)
                        low = 2 * g * n
                        outs[out][low : low + n, columns] = a[places[c + pair], rows, :].astype(F32)
                        outs[out][low + n : low + 2 * n, columns] = b[
                            places[d + pair], rows, :
                        ].astype(F32)


def tie(v, *after):
    return lax.optimization_barrier((v, *after))[0]


def rounds(threads):
    done, waiting = {}, {name: next(thread) for name, thread in threads.items()}
    while waiting:
        ready = lax.optimization_barrier(waiting)
        waiting = {}
        for name, value in ready.items():
            try:
                waiting[name] = threads[name].send(value)
            except StopIteration as stop:
                done[name] = stop.value
    return done


def finish_kernel(dims, small, *outs):
    heads, head_size, hidden = dims
    width = small.shape[1]
    wide = 3 * head_size
    for i in range(6):
        outs[i][...] = small[i, :]
    at = 6
    for h in range(heads):
        row, low = at + h * wide // width, h * wide % width
        line = small[row : row + 1, low : low + wide]
        outs[6][h : h + 1, 0:head_size] = line[:, 0:head_size]
        outs[6][h : h + 1, head_size:] = line[:, 2 * head_size :]
    at += -(-heads * wide // width)
    for low in range(0, hidden, width):
        high = min(low + width, hidden)
        outs[8][low:high] = small[at, 0 : high - low]
        at += 1
    held = width // (2 * LANES)
    for h in range(heads):
        low = h % held * 2 * LANES
        row = at + h // held
        outs[7][h : h + 1, :] = small[row : row + 1, low : low + outs[7].shape[1]]


def partner(axis, bit):
    return [(i, i ^ bit) for i in range(lax.axis_size(axis))]


def swap(v, axis, bit):
    return lax.ppermute(v, axis, partner(axis, bit))


def bits_of(count):
    return [1 << i for i in range(count.bit_length() - 1)]


def add_low(a, b):
    return (a.astype(F32) + b.astype(F32)).astype(a.dtype)


def gather_halves(v, axis):
    held = v[None]
    bits = bits_of(lax.axis_size(axis))
    for bit in bits[:-1]:
        held = jnp.concatenate([held, swap(held, axis, bit)], axis=0)
    return held, swap(held, axis, bits[-1])


def sum_halves(v, axis):
    bits = bits_of(lax.axis_size(axis))
    for bit in bits[:-1]:
        other = swap(v, axis, bit)
        shape = other.shape
        other = other.reshape((shape[0] // (2 * bit), 2, bit) + shape[1:])[:, ::-1].reshape(shape)
        v = add_low(v, other)
    return v, swap(v, axis, bits[-1])


def scatter_halves(v, axis, count=None):
    bits = bits_of(count or lax.axis_size(axis))
    for bit in bits[:0:-1]:
        v = add_low(v[:bit], swap(v[bit:], axis, bit))
    return v[:1], swap(v[1:], axis, 1)


def gather_all(v, steps):
    for axis, bit in steps:
        v = jnp.concatenate([v, swap(v, axis, bit)], axis=0)
    return v


def mixed_swap(v, bits):
    size = lax.axis_size("dp")
    return lax.ppermute(v, "dp", [(i, i ^ bits[i & 1]) for i in range(size)])


def add_halves(kept, other):
    half = kept.shape[0] // 2
    return add_low(kept[:half], other[:half]), add_low(kept[half:], other[half:])


def unpack(places, own, other, layout, group, outs, name):
    return call(
        functools.partial(unpack_kernel, layout, group),
        (own.shape[0] // group,),
        [whole(own.shape), whole(own.shape)],
        outs,
        [],
        1,
        (places, own, other),
        name,
        0,
        30,
    )


def largest(count, most):
    return max(n for n in range(1, most + 1) if count % n == 0)


def per_device(
    patches,
    out_grad,
    score_grad,
    crop_size,
    frozen,
    attn_gain,
    attn_shift,
    qkv_weight,
    qkv_bias,
    rel_table,
    proj_weight,
    proj_bias,
    mlp_gain,
    mlp_shift,
    hidden_weight,
    hidden_bias,
    output_weight,
    output_bias,
    prototypes,
):
    rows, width = patches.shape
    padded = -(-rows // 16) * 16
    parts = lax.axis_size("tensor")
    groups = lax.axis_size("dp")
    heads = qkv_weight.shape[1]
    head_size = qkv_weight.shape[2] // 3
    hidden = hidden_weight.shape[1]
    inner = heads * head_size
    group_crops = crop_size.shape[0]
    crops = group_crops // parts
    slots = -(-crops // 16) * 16
    protos = prototypes.shape[0]
    all_rows = parts * padded
    half = parts // 2
    tensor_rank, dp_rank = lax.axis_index("tensor"), lax.axis_index("dp")
    ids = jnp.stack([tensor_rank, dp_rank, dp_rank * parts + tensor_rank]).astype(jnp.int32)
    chunks = groups
    while (width // chunks) % 16 or (hidden // chunks) % 16 or (4 * inner // chunks) % 16:
        chunks //= 2
    pairs = chunks // 2
    scatter = [b for b in bits_of(chunks) if b > 1]
    rest_bits = [b for b in bits_of(groups) if b >= chunks]
    orders_a = (scatter, scatter[1:2] + scatter[:1] + scatter[2:])
    orders_b = orders_a
    vector = whole((width,))

    x0, x1 = gather_halves(patches, "tensor")

    proto_step = min(512, protos)
    crop_bits = bits_of(groups)[1:]
    crop_rows = -(-group_crops // 8) * 8
    crop_shape = (groups // 2, crop_rows, width)
    def crop_step(kept, other, bit, *after):
        kept, other = (lax.optimization_barrier((v, after))[0] for v in (kept, other))
        half = kept.shape[0] // 2
        return kept[:half] + other[:half], swap(kept[half:] + other[half:], "dp", bit)

    tables = call(
        functools.partial(table_kernel, heads, head_size**0.5),
        (1,),
        [whole(rel_table.shape)],
        [(sds((heads * 2 * SLOTS, LANES), BF), whole((heads * 2 * SLOTS, LANES)))],
        [],
        1,
        (ids, rel_table),
        "tables",
        0,
        24,
    )[0]
    w_t = jnp.transpose(qkv_weight, (1, 2, 0)).reshape(3 * inner, width)
    wp = proj_weight.reshape(inner, width)
    unroll = largest(heads, 12)
    block3 = lambda a, b: pl.BlockSpec((1, a, b), lambda i, *_: (i, 0, 0))
    halves3 = lambda a, b, dtype: (sds((half, a, b), dtype), block3(a, b))

    def attend(first, x, ids):
        dims = (first, rows, padded, heads, head_size, crops, unroll)
        return call(
            functools.partial(attend_kernel, dims),
            (half,),
            [
                block3(rows, width),
                vector,
                vector,
                whole(w_t.shape),
                whole(qkv_bias.shape),
                whole(tables.shape),
                whole(wp.shape),
            ],
            [
                halves3(padded, width, BF),
                halves3(padded, width, BF),
                halves3(3 * inner, padded, BF),
                (
                    sds((half, heads, padded, padded), BF),
                    pl.BlockSpec((1, heads, padded, padded), lambda i, *_: (i, 0, 0, 0)),
                ),
                halves3(inner, padded, BF),
                halves3(padded, width, BF),
            ],
            [
                pltpu.VMEM((padded, width), F32),
                pltpu.VMEM((heads * 2 * SLOTS, padded), BF),
                pltpu.VMEM((padded, padded), F32),
            ],
            2,
            (ids, crop_size, x, attn_gain, attn_shift, w_t, qkv_bias, tables, wp),
            "attend",
            all_rows * 4 * inner * width,
            20,
        )

    crop_keep, crop_send = call(
        functools.partial(crop_grad_kernel, groups, group_crops, crop_bits),
        (protos // proto_step,),
        [
            pl.BlockSpec((score_grad.shape[0], proto_step), lambda i, s: (0, i)),
            pl.BlockSpec((proto_step, width), lambda i, s: (i, 0)),
        ],
        [(sds(crop_shape, F32), whole(crop_shape)), (sds(crop_shape, F32), whole(crop_shape))],
        [pltpu.VMEM((score_grad.shape[0], width), F32)],
        1,
        (tie(ids, tables), score_grad, prototypes),
        "crop_grads",
        2 * score_grad.shape[0] * protos * width,
        16,
    )
    crop_other = swap(tie(crop_send, x1), "dp", 1)
    g0, g1 = gather_halves(tie(out_grad, x1), "tensor")
    xf0, h1_0, qkv0, pt0, ot0, a0 = attend(0, x0, tie(ids, crop_send))
    a0, g1 = lax.optimization_barrier((a0, g1))
    b0 = swap(a0, "tensor", 1)
    crop_held = crop_step(crop_keep, crop_other, crop_bits[0], a0)
    xf1, h1_1, qkv1, pt1, ot1, a1 = attend(half, x1, tie(ids, crop_held[0]))
    b1 = swap(tie(a1, b0, g1), "tensor", 1)
    if parts > 2:
        a_all, b_all = sum_halves(jnp.concatenate([a0, a1]), "tensor")
        a0, a1, b0, b1 = a_all[:half], a_all[half:], b_all[:half], b_all[half:]
    for bit in crop_bits[1:-1]:
        crop_held = crop_step(*crop_held, bit, a1)
    kept, other = (tie(v, a1) for v in crop_held)
    kept, sent = kept[:1] + other[:1], kept[1:] + other[1:]
    far = crop_bits[-1] * parts
    crop_terms = [kept, swap(sent, ("dp", "tensor"), far)]
    for move in range(1, parts):
        crop_terms += [
            swap(kept, ("dp", "tensor"), move),
            swap(sent, ("dp", "tensor"), far + move),
        ]

    hidden_step = 768 if hidden % 768 == 0 else hidden
    hidden_steps = hidden // hidden_step
    crops_slots = -(-group_crops // 16) * 16
    full = whole((parts, padded, width))
    columns = lambda a: pl.BlockSpec((a, hidden_step), lambda i, *_: (0, i))
    y1, gy, h2, gz, m, gu, gh2_near, gh2_far, ob, hb = call(
        functools.partial(hidden_kernel, (parts, rows, padded, crops, group_crops)),
        (hidden_steps,),
        [
            *[whole((half, padded, width))] * 6,
            whole(g0.shape),
            whole(g1.shape),
            *[whole(kept.shape)] * len(crop_terms),
            vector,
            vector,
            vector,
            columns(width),
            columns(1),
            pl.BlockSpec((hidden_step, width), lambda i, *_: (i, 0)),
        ],
        [
            (sds((parts, padded, width), F32), full),
            (sds((parts, padded, width), F32), full),
            (sds((all_rows, width), BF), whole((all_rows, width))),
            (sds((all_rows, width), BF), whole((all_rows, width))),
            (sds((all_rows, hidden), BF), columns(all_rows)),
            (sds((all_rows, hidden), BF), columns(all_rows)),
            (sds((half, padded, width), BF), whole((half, padded, width))),
            (sds((half, padded, width), BF), whole((half, padded, width))),
            (sds((1, width), F32), whole((1, width))),
            (sds((1, hidden), F32), columns(1)),
        ],
        [
            pltpu.VMEM((padded, width), F32),
            pltpu.VMEM((crops_slots, width), F32),
            pltpu.VMEM((all_rows, width), F32),
        ],
        2,
        (
            ids, crop_size, xf0, xf1, a0, a1, b0, b1, g0, g1, *crop_terms, proj_bias, mlp_gain, mlp_shift,
            hidden_weight, hidden_bias.reshape(1, hidden), output_weight,
        ),
        "hidden",
        6 * all_rows * hidden * width,
        34,
    )
    near_other = swap(gh2_near, "tensor", half)

    chunks_step = chunks // hidden_steps
    wide = min(hidden, width)
    n1, n2 = width // chunks, hidden // chunks
    rows_a = (n1 * hidden + n2 * width) // wide
    chunk_a = whole((pairs, rows_a, wide))
    keep_a, send_a = call(
        functools.partial(hidden_grad_kernel, (chunks, chunks_step, wide, orders_a)),
        (hidden_steps,),
        [
            whole((all_rows, width)),
            whole((all_rows, width)),
            pl.BlockSpec((all_rows, hidden_step), lambda i, s: (0, i)),
            pl.BlockSpec((all_rows, hidden_step), lambda i, s: (0, i)),
        ],
        [
            (sds((pairs, rows_a, wide), BF), chunk_a),
            (sds((pairs, rows_a, wide), BF), chunk_a),
        ],
        [pltpu.VMEM((width, all_rows), BF)],
        1,
        (ids, h2, gz, m, gu),
        "hidden_grads",
        4 * all_rows * hidden * width,
        30,
    )
    if parts > 2:
        e_all, f_all = sum_halves(jnp.concatenate([gh2_near, gh2_far]), "tensor")
        gh2_near, gh2_far = e_all[:half], e_all[half:]
        near_other, far_other = f_all[:half], f_all[half:]
    else:
        far_other = swap(tie(gh2_far, near_other), "tensor", half)
    core_a = swap(tie(send_a, near_other), "dp", 1)

    n_b = 4 * inner // chunks
    chunk_b = whole((pairs, n_b, width))

    def attend_back(first, e0, e1, xf, qkv, pt, ids):
        dims = (first, rows, padded, heads, head_size, crops, unroll)
        at = lambda a, b: pl.BlockSpec((1, a, b), lambda i, *_: (first + i, 0, 0))
        return call(
            functools.partial(attend_back_kernel, dims),
            (half,),
            [
                at(padded, width),
                at(padded, width),
                block3(padded, width),
                block3(padded, width),
                vector,
                block3(padded, width),
                block3(3 * inner, padded),
                pl.BlockSpec((1, heads, padded, padded), lambda i, *_: (i, 0, 0, 0)),
                whole(wp.shape),
                whole(w_t.shape),
            ],
            [
                (sds((half, padded, width), F32), block3(padded, width)),
                (sds((half, padded, width), BF), block3(padded, width)),
                (sds((half, padded, width), BF), block3(padded, width)),
                (sds((half, 3 * inner, padded), BF), block3(3 * inner, padded)),
                (sds((8, width), F32), whole((8, width))),
                (sds((8, 3 * inner), F32), whole((8, 3 * inner))),
                (sds((heads * SLOTS, LANES), F32), whole((heads * SLOTS, LANES))),
            ],
            [pltpu.VMEM((inner, padded), BF), pltpu.VMEM((heads * SLOTS, padded), F32)],
            2,
            (ids, crop_size, y1, gy, e0, e1, mlp_gain, xf, qkv, pt, wp, w_t),
            "attend_back",
            2 * all_rows * 4 * inner * width,
            22,
        )

    z_part = call(
        functools.partial(share_kernel, parts, padded),
        (hidden_steps,),
        [
            pl.BlockSpec((all_rows, hidden_step), lambda i: (0, i)),
            pl.BlockSpec((hidden_step, width), lambda i: (i, 0)),
        ],
        [(sds((parts, padded, width), BF), full)],
        [pltpu.VMEM((all_rows, width), F32)],
        0,
        (tie(m, keep_a), output_weight),
        "share",
        2 * all_rows * hidden * width,
        16,
    )[0]
    kept_a, sent_a = add_halves(tie(keep_a, z_part), tie(core_a, z_part))
    other_a = mixed_swap(sent_a, list(zip(*orders_a))[0])
    _, gh1_far, ga1, gq1, sums1, qb1, tt1 = attend_back(
        half, gh2_far, near_other, xf1, qkv1, pt1, tie(ids, sent_a)
    )
    gh1_far, far_other = lax.optimization_barrier((gh1_far, far_other))
    z0, z1 = scatter_halves(tie(z_part, gh1_far), "tensor")
    g_own, gh1_near, ga0, gq0, sums0, qb0, tt0 = attend_back(
        0, gh2_near, far_other, xf0, qkv0, pt0, tie(ids, gh1_far)
    )
    small_rows = 6 + -(-3 * inner // width) + -(-hidden // width) + -(-heads // (width // (2 * LANES)))
    small_rows = -(-small_rows // 8) * 8
    args = (ot0, ot1, ga0, ga1, gq0, gq1, h1_0, h1_1, sums0, sums1, qb0, qb1, tt0, tt1, ob, hb)
    keep_b, send_b, small = call(
        functools.partial(attend_grad_kernel, (parts, heads, chunks, orders_b)),
        (1,),
        [whole(v.shape) for v in args],
        [
            (sds((pairs, n_b, width), BF), chunk_b),
            (sds((pairs, n_b, width), BF), chunk_b),
            (sds((small_rows, width), F32), whole((small_rows, width))),
        ],
        [pltpu.VMEM((inner, width), F32), pltpu.VMEM((3 * inner, width), F32)],
        1,
        (tie(ids, other_a, z1), *args),
        "attend_grads",
        2 * all_rows * 4 * inner * width,
        30,
    )

    one = whole((1, padded, width))

    def places_of(orders):
        spots = pair_spots(jnp.arange(pairs, dtype=jnp.int32), dp_rank & (chunks - 1), orders)
        return jnp.concatenate([(dp_rank & 1)[None], *spots]).astype(jnp.int32)

    def all_sum(kept, other, orders, begin, cuts):
        stages = list(zip(*orders))
        for stage in stages[begin:-1]:
            kept, sent = add_halves(kept, other)
            kept, other = yield kept, mixed_swap(sent, stage)
        held = add_low(kept, other)
        for bits in [stages[-1], *[(bit, bit) for bit in rest_bits]]:
            size = held.shape[0] // cuts
            pieces = [held[i * size : (i + 1) * size] for i in range(cuts)]
            for i in range(cuts):
                pieces[i], pieces[i + 1 :], other = yield (
                    pieces[i],
                    pieces[i + 1 :],
                    mixed_swap(pieces[i], bits),
                )
                pieces[i] = add_low(pieces[i], other)
            held = jnp.concatenate(pieces, axis=0) if cuts > 1 else pieces[0]
        for stage in stages[-2::-1]:
            held = jnp.concatenate((yield held, mixed_swap(held, stage)), axis=0)
        return held, swap(held, "dp", 1)

    def hidden_sum():
        kept, other = yield kept_a, other_a
        held, other = yield from all_sum(kept, other, orders_a, 1, 2)
        group = 2 - pairs % 2
        layout = (
            (0, 0, pairs, 0, n1, hidden // wide),
            (1, 0, pairs, rows_a - n2 * width // wide, n2, width // wide),
        )
        outs = [
            (sds((width, hidden), F32), pl.BlockSpec((2 * group * n1, hidden), lambda i, s: (i, 0))),
            (sds((hidden, width), F32), pl.BlockSpec((2 * group * n2, width), lambda i, s: (i, 0))),
        ]
        return (yield unpack(places_of(orders_a), held, other, layout, group, outs, "unpack_hidden"))

    def attend_sum():
        kept, sent = yield keep_b, send_b
        kept, other = yield kept, swap(sent, "dp", 1)
        held, other = yield from all_sum(kept, other, orders_b, 0, 1)
        edge = inner // (2 * n_b)
        group = 2 - edge % 2
        edge = edge // group
        layout = ((0, 0, edge, 0, n_b, 1), (1, edge, pairs, 0, n_b, 1))
        shape = (2 * group * n_b, width)
        early = pl.BlockSpec(shape, lambda i, s: (jnp.minimum(i, edge - 1), 0))
        late = pl.BlockSpec(shape, lambda i, s: (jnp.maximum(i - edge, 0), 0))
        outs = [(sds((inner, width), F32), early), (sds((3 * inner, width), F32), late)]
        return unpack(places_of(orders_b), held, other, layout, group, outs, "unpack_attend")

    def patch():
        yield ()
        near, far = gh1_near, gh1_far
        if half > 1:
            near, far = yield near, swap(far, "tensor", half)
            near, far = scatter_halves(add_low(near, far), "tensor", half)
        else:
            far = swap(far, "tensor", 1)
        near, far = yield near, far
        return (yield call(
            functools.partial(patch_grad_kernel, rows),
            (1,),
            [one, one, one, one, vector],
            [(sds((rows, width), F32), whole((rows, width)))],
            [],
            0,
            (g_own, near, far, xf0, attn_gain),
            "patch_grads",
            0,
            24,
        )[0])

    def head():
        own, other, held = yield z0, z1, small
        block_out, pooled = call(
            functools.partial(result_kernel, (rows, padded, crops)),
            (1,),
            [one, one, one, vector],
            [
                (sds((rows, width), BF), whole((rows, width))),
                (sds((1, slots, width), BF), whole((1, slots, width))),
            ],
            [],
            2,
            (ids, crop_size, y1, own, other, output_bias),
            "result",
            0,
            24,
        )
        steps = [[b * parts] for b in bits_of(groups)[:0:-1]]
        steps += [[1, parts]] if parts == 2 else [[b] for b in [*bits_of(parts), parts]]
        weights = [weight for step in steps for weight in step]
        pooled = pooled[0]
        first = lax.broadcasted_iota(jnp.int32, (small_rows, 1), 0) < 2
        for step in steps:
            count = pooled.shape[0]
            high = lax.reduce_precision(held, 8, 7)
            payload = jnp.concatenate([pooled, high.astype(BF), (held - high).astype(BF)], axis=0)
            moves = [sum(w for k, w in enumerate(step) if i >> k & 1) for i in range(1, 2 ** len(step))]
            pooled, held, *others = yield (
                pooled,
                held,
                *[swap(payload, ("dp", "tensor"), move) for move in moves],
            )
            for move, other in zip(moves, others):
                high = other[count : count + small_rows].astype(F32)
                part = high + other[count + small_rows :].astype(F32)
                held = held + (jnp.where(first, part, 0.0) if move % parts else part)
            pooled = jnp.concatenate([pooled, *[other[:count] for other in others]], axis=0)
        step_spec = pl.BlockSpec((proto_step, width), lambda i, s: (i, 0))
        prototype_grad = call(
            functools.partial(proto_grad_kernel, (crops, slots, weights)),
            (protos // proto_step,),
            [
                pl.BlockSpec((score_grad.shape[0], proto_step), lambda i, s: (0, i)),
                whole(pooled.shape),
                step_spec,
                pl.BlockSpec((1, proto_step), lambda i, s: (0, i)),
            ],
            [(sds((protos, width), F32), step_spec)],
            [pltpu.VMEM((score_grad.shape[0], width), BF)],
            1,
            (ids, score_grad, pooled, prototypes, frozen.reshape(1, protos)),
            "proto_grads",
            2 * score_grad.shape[0] * protos * width,
            40,
        )[0]
        finished = call(
            functools.partial(finish_kernel, (heads, head_size, hidden)),
            (1,),
            [whole(held.shape)],
            [
                *[(sds((width,), F32), whole((width,)))] * 6,
                (sds((heads, 2 * head_size), F32), whole((heads, 2 * head_size))),
                (sds(rel_table.shape, F32), whole(rel_table.shape)),
                (sds((hidden,), F32), whole((hidden,))),
            ],
            [],
            0,
            (held,),
            "finish",
            0,
            8,
        )
        prototype_grad, finished = yield prototype_grad, finished
        return block_out, prototype_grad, finished

    threads = {"A": hidden_sum(), "B": attend_sum(), "H": head(), "P": patch()}
    done = rounds(threads)
    out_w1, out_w2 = done["A"]
    proj_weight_grad, qkv_weight_grad = done["B"]
    block_out, prototype_grad, (*small, qb, rel, hb) = done["H"]
    return (
        block_out,
        done["P"],
        small[0],
        small[1],
        jnp.transpose(qkv_weight_grad.reshape(heads, 3 * head_size, width), (2, 0, 1)),
        qb,
        rel,
        proj_weight_grad.reshape(heads, head_size, width),
        small[4],
        small[2],
        small[3],
        out_w1,
        hb,
        out_w2,
        small[5],
        prototype_grad,
    )


def solution(mesh):
    both = ("dp", "tensor")
    return jax.shard_map(
        per_device,
        mesh=mesh,
        in_specs=(
            P(both, None),
            P(both, None),
            P(None, both),
            P("dp"),
            P(both),
            P(),
            P(),
            P(None, "tensor", None),
            P("tensor", None),
            P("tensor", None),
            P("tensor", None, None),
            P(),
            P(),
            P(),
            P(None, "tensor"),
            P("tensor"),
            P("tensor", None),
            P(),
            P(both, None),
        ),
        out_specs=(
            P(both, None),
            P(both, None),
            P(),
            P(),
            P(None, "tensor", None),
            P("tensor", None),
            P("tensor", None),
            P("tensor", None, None),
            P(),
            P(),
            P(),
            P(None, "tensor"),
            P("tensor"),
            P("tensor", None),
            P(),
            P(both, None),
        ),
        check_vma=False,
    )
```

```python
import functools

import jax
import jax.numpy as jnp
import numpy as np
from jax import lax
from jax.experimental import pallas as pl
from jax.experimental.pallas import tpu as pltpu
from jax.sharding import PartitionSpec as P

EPS = 1e-05
BF = jnp.bfloat16
F32 = jnp.float32
HIGH = lax.Precision.HIGHEST
SIDE = 7
PLACES = SIDE * SIDE
OFFSETS = 2 * SIDE - 1
LAST = (SIDE - 1) * (OFFSETS + 1)
SLOTS = 96
LANES = 128
COST = 0.01


def nn(a, b):
    return jnp.dot(a, b, preferred_element_type=F32)


def nt(a, b):
    return lax.dot_general(a, b, (((1,), (1,)), ((), ())), preferred_element_type=F32)


def split(v):
    high = v.astype(BF)
    return high, (v - high.astype(F32)).astype(BF)


def line(ref):
    return ref[...].reshape(1, -1)


def normalize(v):
    center = v - jnp.mean(v, axis=-1, keepdims=True)
    spread = jnp.mean(center * center, axis=-1, keepdims=True)
    inverse = lax.rsqrt(spread + EPS)
    return center * inverse, inverse


def norm_back(hat, inverse, gain, grad):
    scaled = grad * gain
    first = jnp.mean(scaled, axis=-1, keepdims=True)
    second = jnp.mean(scaled * hat, axis=-1, keepdims=True)
    return (scaled - first - hat * second) * inverse


def row_layout(sizes_ref, base, crops, rows, padded, axis):
    shape = (padded, 1) if axis == 0 else (1, padded)
    position = lax.broadcasted_iota(jnp.int32, shape, axis)
    start = jnp.int32(0)
    segment = jnp.zeros(shape, jnp.int32)
    first = jnp.zeros(shape, jnp.int32)
    length = jnp.zeros(shape, jnp.int32)
    for crop in range(crops):
        size = sizes_ref[base + crop]
        reached = position >= start
        segment = jnp.where(reached, crop, segment)
        first = jnp.where(reached, start, first)
        length = jnp.where(reached, size, length)
        start = start + size
    offset = position - first
    by_seven = offset + ((offset * 37) >> 8) * (OFFSETS - SIDE)
    by_three = offset + ((offset * 11) >> 5) * (OFFSETS - 3)
    place = jnp.where(length == PLACES, by_seven, by_three)
    real = position < rows
    segment = jnp.where(real, segment, crops)
    place = jnp.where(real, place, 2 * LANES)
    return segment, place, jnp.where(real, length, 1).astype(F32)


def call(body, grid, ins, outs, scratch, prefetch, args, name, flops, vmem):
    moved = sum(int(np.prod(a.shape)) * a.dtype.itemsize for a in args)
    moved += sum(int(np.prod(s.shape)) * s.dtype.itemsize for s, _ in outs)
    return pl.pallas_call(
        body,
        grid_spec=pltpu.PrefetchScalarGridSpec(
            num_scalar_prefetch=prefetch,
            grid=grid,
            in_specs=ins,
            out_specs=[spec for _, spec in outs],
            scratch_shapes=scratch,
        ),
        out_shape=[shape for shape, _ in outs],
        compiler_params=pltpu.CompilerParams(
            dimension_semantics=("arbitrary",) * len(grid), vmem_limit_bytes=vmem * 2**20
        ),
        cost_estimate=pl.CostEstimate(
            flops=int(flops * COST), bytes_accessed=int(moved * COST), transcendentals=0
        ),
        name=name,
    )(*args)


def whole(shape):
    zeros = (0,) * len(shape)
    return pl.BlockSpec(tuple(shape), lambda *_: zeros)


def sds(shape, dtype):
    return jax.ShapeDtypeStruct(tuple(shape), dtype)


def crop_grad_kernel(groups, crops, bits, ids, score, proto, keep, send, total):
    step = pl.program_id(0)

    @pl.when(step == 0)
    def _():
        total[...] = jnp.zeros_like(total)

    p = proto[...].astype(F32)
    unit = p * lax.rsqrt(jnp.sum(p * p, axis=1, keepdims=True) + 1e-06)
    total[...] += nn(score[...], unit.astype(BF))

    @pl.when(step == pl.num_programs(0) - 1)
    def _():
        odd = (ids[1] & 1) == 1
        for pair in range(groups // 2):
            at = 0
            for bit in bits:
                at = 2 * at + (((pair ^ (ids[1] >> 1)) >> (bit.bit_length() - 2)) & 1)
            first = total[2 * pair * crops : (2 * pair + 1) * crops, :]
            second = total[(2 * pair + 1) * crops : (2 * pair + 2) * crops, :]
            keep[at, 0:crops, :] = jnp.where(odd, second, first)
            send[at, 0:crops, :] = jnp.where(odd, first, second)
            if keep.shape[1] > crops:
                tail = jnp.zeros((keep.shape[1] - crops, keep.shape[2]), F32)
                keep[at, crops:, :] = tail
                send[at, crops:, :] = tail


def table_kernel(heads, scale, ids, rel, tables):
    for h in range(heads):
        line = jnp.concatenate(
            [rel[h : h + 1, :], jnp.zeros((1, 2 * LANES - rel.shape[1]), F32)], axis=1
        )
        line = jnp.broadcast_to(line * scale, (8, 2 * LANES))
        line = pltpu.roll(line, 2 * LANES - LAST % 8, 1)
        line = jnp.broadcast_to(line[0:1, :], (SLOTS, 2 * LANES))
        slid = pltpu.roll(line, 2 * LANES - LAST // 8 * 8, 1, stride=1, stride_axis=0)
        high, low = split(slid[:, 0:LANES])
        tables[2 * h * SLOTS : (2 * h + 1) * SLOTS, :] = high
        tables[(2 * h + 1) * SLOTS : (2 * h + 2) * SLOTS, :] = low


def attend_kernel(
    dims, ids, sizes, x0, gain, shift, w, bias, tables, wp, xo, ho, qo, po, oo, ao, xs, rr, hide
):
    first, rows, padded, heads, head_size, crops, unroll = dims
    wide = 3 * head_size
    step = pl.program_id(0)
    base = ((first + step) ^ ids[0]) * crops
    tail = padded - 8
    xs[tail:padded, :] = jnp.zeros((padded - tail, xs.shape[1]), F32)
    xs[0:rows, :] = x0[0].astype(F32)
    x = xs[...]
    xo[0] = x.astype(BF)
    hat, _ = normalize(x)
    h1 = (hat * line(gain) + line(shift)).astype(BF)
    ho[0] = h1
    mixed = nt(w[...], h1)
    bias_cols = jnp.transpose(bias[...])
    for h in range(heads):
        low = h * wide
        qo[0, low : low + head_size, :] = (
            mixed[low : low + head_size] + bias_cols[0:head_size, h : h + 1]
        ).astype(BF)
        qo[0, low + head_size : low + 2 * head_size, :] = mixed[
            low + head_size : low + 2 * head_size
        ].astype(BF)
        qo[0, low + 2 * head_size : low + wide, :] = (
            mixed[low + 2 * head_size : low + wide] + bias_cols[head_size : 2 * head_size, h : h + 1]
        ).astype(BF)
    seg_row, place_row, _ = row_layout(sizes, base, crops, rows, padded, 1)
    seg_col, place_col, _ = row_layout(sizes, base, crops, rows, padded, 0)
    hide[...] = jnp.where(seg_col == seg_row, 0.0, -jnp.inf).astype(F32)
    lane = lax.broadcasted_iota(jnp.int32, (padded, LANES), 1)
    hot = (lane == place_col).astype(F32).astype(BF)
    slot = lax.broadcasted_iota(jnp.int32, (LANES, padded), 0)
    hot_t = (slot == place_row).astype(F32).astype(BF)

    rr[...] = nn(tables[...], hot_t).astype(BF)
    zeros = jnp.zeros((2 * LANES - 2 * SLOTS - head_size, padded), BF)

    def some_heads(i, carry):
        for u in range(unroll):
            h = i * unroll + u
            slab = qo[0, pl.ds(pl.multiple_of(h * wide, 32), wide), :]
            q = slab[0:head_size]
            v = slab[2 * head_size : wide]
            k = slab[head_size : 2 * head_size]
            left_t = jnp.transpose(jnp.concatenate([k, hot_t[0:SLOTS]], axis=0))
            left = jnp.concatenate([left_t, hot], axis=1)
            biases = rr[pl.ds(pl.multiple_of(h * 2 * SLOTS, 64), 2 * SLOTS), :]
            right = jnp.concatenate([q, biases, zeros], axis=0)
            s = nn(left, right) * (head_size**-0.5) + hide[...]
            e = jnp.exp(s - jnp.max(s, axis=0, keepdims=True))
            p = (e * (1.0 / jnp.sum(e, axis=0, keepdims=True))).astype(BF)
            po[0, h] = p
            oo[0, pl.ds(pl.multiple_of(h * head_size, 32), head_size), :] = nn(v, p).astype(BF)
        return carry

    lax.fori_loop(0, heads // unroll, some_heads, 0)
    ao[0] = nn(jnp.transpose(oo[0]), wp[...]).astype(BF)


def hidden_kernel(
    dims, ids, sizes, x0, x1, a0, a1, b0, b1, g0, g1, *rest,
):
    parts, rows, padded, crops, group_crops = dims
    terms, rest = rest[: 2 * parts], rest[2 * parts :]
    pb, gain, shift, w1, bias1, w2 = rest[:6]
    y1o, gyo, h2o, gzo, mo, guo, gh0, gh1, obo, hbo, gs, cs, total = rest[6:]
    step = pl.program_id(0)

    @pl.when(step == 0)
    def _():
        cs[...] = jnp.zeros_like(cs)
        cs[0 : terms[0].shape[1], :] = sum(term[0].astype(F32) for term in terms)
        high, low = split(cs[...])
        bias_sum = jnp.zeros((1, gs.shape[1]), F32)
        tail, half = padded - 8, parts // 2
        for r in range(parts):
            x, own, other, g = (x0, a0, b1, g0) if r < half else (x1, a1, b0, g1)
            k = r % half
            y1 = x[k].astype(F32) + (own[k].astype(F32) + other[k].astype(F32)) + line(pb)
            y1o[r] = y1
            hat, _ = normalize(y1)
            h2o[r * padded : (r + 1) * padded, :] = (hat * line(gain) + line(shift)).astype(BF)
            base = (ids[0] ^ r) * crops
            segment, _, length = row_layout(sizes, base, crops, rows, padded, 0)
            lane = lax.broadcasted_iota(jnp.int32, (padded, cs.shape[0]), 1)
            mine = (lane == segment + base) & (segment < crops)
            hot = mine.astype(F32).astype(BF)
            gs[tail:padded, :] = jnp.zeros((padded - tail, gs.shape[1]), F32)
            gs[0:rows, :] = g[k].astype(F32)
            gy = gs[...] + (nn(hot, high) + nn(hot, low)) / length
            gyo[r] = gy
            gzo[r * padded : (r + 1) * padded, :] = gy.astype(BF)
            bias_sum = bias_sum + jnp.sum(gy, axis=0, keepdims=True)
        obo[...] = bias_sum
        total[...] = jnp.zeros_like(total)

    u = nn(h2o[...], w1[...]) + bias1[...]
    spread = 0.5 * (1.0 + lax.erf(u * np.float32(np.sqrt(0.5))))
    mo[...] = (u * spread).astype(BF)
    slope = spread + u * (jnp.exp(-0.5 * u * u) * np.float32(1.0 / np.sqrt(2.0 * np.pi)))
    gu = (nt(gzo[...], w2[...]) * slope).astype(BF)
    guo[...] = gu
    hbo[...] = jnp.sum(gu.astype(F32), axis=0, keepdims=True)
    total[...] += nt(gu, w1[...])

    @pl.when(step == pl.num_programs(0) - 1)
    def _():
        half = parts // 2
        for r in range(parts):
            gho = gh0 if r < half else gh1
            gho[r % half] = total[r * padded : (r + 1) * padded, :].astype(BF)


def spot(pair, mine, core, orders):
    spots = []
    for order in orders:
        at = 0
        for bit in order:
            source = pair if bit == order[-1] else pair ^ mine
            at = 2 * at + ((source >> (bit.bit_length() - 2)) & 1)
        spots.append(at)
    return jnp.where(core == 1, spots[1], spots[0])


def put_chunk(keep, send, spots, odd, first, second, at):
    rows = pl.ds(at, first.shape[0])
    keep[spots[0], rows, :] = jnp.where(odd, second, first).astype(BF)
    send[spots[1], rows, :] = jnp.where(odd, first, second).astype(BF)


def pair_spots(pair, rank, orders):
    core, mine = rank & 1, rank >> 1
    return spot(pair, mine, core, orders), spot(pair, mine, 1 - core, orders)


def hidden_grad_kernel(dims, ids, h2, gz, m, gu, keep, send, h2t):
    chunks, chunks_step, wide, orders = dims
    step = pl.program_id(0)
    rank = ids[1] & (chunks - 1)
    odd = (rank & 1) == 1

    @pl.when(step == 0)
    def _():
        h2t[...] = jnp.transpose(h2[...])

    d1 = nn(h2t[...], gu[...])
    n1 = d1.shape[0] // chunks
    steps = d1.shape[1] // wide
    for pair in range(chunks // 2):
        spots = pair_spots(pair, rank, orders)
        for part in range(steps):
            piece = d1[2 * pair * n1 : (2 * pair + 2) * n1, part * wide : (part + 1) * wide]
            at = pl.multiple_of((step * steps + part) * n1, 16)
            put_chunk(keep, send, spots, odd, piece[:n1], piece[n1:], at)
    d2 = nn(jnp.transpose(m[...]), gz[...])
    n2 = d2.shape[0] // chunks_step
    base = keep.shape[1] - d2.shape[1] // wide * n2
    for pair in range(chunks_step // 2):
        spots = pair_spots(step * (chunks_step // 2) + pair, rank, orders)
        for part in range(d2.shape[1] // wide):
            piece = d2[2 * pair * n2 : (2 * pair + 2) * n2, part * wide : (part + 1) * wide]
            put_chunk(keep, send, spots, odd, piece[:n2], piece[n2:], base + part * n2)


def share_kernel(parts, padded, m, w2, zo, total):
    step = pl.program_id(0)

    @pl.when(step == 0)
    def _():
        total[...] = jnp.zeros_like(total)

    total[...] += nn(m[...], w2[...])

    @pl.when(step == pl.num_programs(0) - 1)
    def _():
        for r in range(parts):
            zo[r] = total[r * padded : (r + 1) * padded, :].astype(BF)


def result_kernel(dims, ids, sizes, y1, z0, z1, bias, out, pooled):
    rows, padded, crops = dims
    y = y1[0] + (z0[0].astype(F32) + z1[0].astype(F32)) + line(bias)
    out[...] = y[0:rows, :].astype(BF)
    segment, _, _ = row_layout(sizes, ids[0] * crops, crops, rows, padded, 1)
    crop = lax.broadcasted_iota(jnp.int32, (pooled.shape[1], padded), 0)
    member = ((crop == segment) & (crop < crops)).astype(F32)
    high, low = split(y)
    hot = member.astype(BF)
    count = jnp.maximum(jnp.sum(member, axis=1, keepdims=True), 1.0)
    pooled[0] = ((nn(hot, high) + nn(hot, low)) / count).astype(BF)


def attend_back_kernel(
    dims, ids, sizes, y1, gy, e0, e1, gain, x, qkv, pt, wp, w, g1o, gho, gao, gqo, sums, qb, tt, go, by
):
    first, rows, padded, heads, head_size, crops, unroll = dims
    wide = 3 * head_size
    step = pl.program_id(0)
    base = ((first + step) ^ ids[0]) * crops

    @pl.when(step == 0)
    def _():
        sums[...] = jnp.zeros_like(sums)
        qb[...] = jnp.zeros_like(qb)
        tt[...] = jnp.zeros_like(tt)

    hat2, inv2 = normalize(y1[0])
    grad2 = e0[0].astype(F32) + e1[0].astype(F32)
    gy1 = gy[0] + norm_back(hat2, inv2, line(gain), grad2)
    g1o[0] = gy1
    ga = gy1.astype(BF)
    gao[0] = ga
    sums[2:3, :] += jnp.sum(grad2 * hat2, axis=0, keepdims=True)
    sums[3:4, :] += jnp.sum(grad2, axis=0, keepdims=True)
    sums[4:5, :] += jnp.sum(gy1, axis=0, keepdims=True)
    go[...] = nt(wp[...], ga).astype(BF)
    _, place_row, _ = row_layout(sizes, base, crops, rows, padded, 1)
    _, place_col, _ = row_layout(sizes, base, crops, rows, padded, 0)
    slot = lax.broadcasted_iota(jnp.int32, (SLOTS, padded), 0)
    hot_t = (slot == LAST - place_row).astype(F32).astype(BF)
    lane = lax.broadcasted_iota(jnp.int32, (padded, LANES), 1)
    hot = (lane == place_col).astype(F32).astype(BF)
    zeros_a = jnp.zeros((LANES - wide, padded), BF)
    zeros_b = jnp.zeros((2 * head_size, padded), BF)
    scale = head_size**-0.5

    def some_heads(i, carry):
        for u in range(unroll):
            h = i * unroll + u
            at = pl.multiple_of(h * wide, 32)
            slab = qkv[0, pl.ds(at, wide), :]
            q = slab[0:head_size]
            k = slab[head_size : 2 * head_size]
            goh = go[pl.ds(pl.multiple_of(h * head_size, 32), head_size), :]
            p = pt[0, h]
            slab_t = jnp.transpose(jnp.concatenate([slab, zeros_a], axis=0))
            gp = nn(slab_t, jnp.concatenate([zeros_b, goh, zeros_a], axis=0))
            pf = p.astype(F32)
            both = pf * gp
            gs = (both - pf * jnp.sum(both, axis=0, keepdims=True)).astype(BF)
            gv = nt(goh, p)
            gk = nt(q, gs)
            gqe = nn(jnp.concatenate([k, hot_t], axis=0), gs)
            gqo[0, pl.ds(at, head_size), :] = (gqe[0:head_size] * scale).astype(BF)
            gqo[0, pl.ds(at + head_size, head_size), :] = (gk * scale).astype(BF)
            gqo[0, pl.ds(at + 2 * head_size, head_size), :] = gv.astype(BF)
            by[pl.ds(pl.multiple_of(h * SLOTS, 32), SLOTS), :] = gqe[head_size:]
        return carry

    lax.fori_loop(0, heads // unroll, some_heads, 0)
    high, low = split(by[...])
    tt[...] += nn(high, hot) + nn(low, hot)
    g = gqo[0]
    qb[...] += nt(jnp.ones((8, padded), BF), g)
    gh1 = nn(jnp.transpose(g), w[...])
    gho[0] = gh1.astype(BF)
    hat1, _ = normalize(x[0].astype(F32))
    sums[0:1, :] += jnp.sum(gh1 * hat1, axis=0, keepdims=True)
    sums[1:2, :] += jnp.sum(gh1, axis=0, keepdims=True)


def attend_grad_kernel(
    dims, ids, o0, o1, ga0, ga1, gq0, gq1, h0, h1, u0, u1, q0, q1, t0, t1, ob, hb, keep, send, small, dp, dq
):
    parts, heads, chunks, orders = dims
    half = parts // 2
    dp[...] = jnp.zeros_like(dp)
    dq[...] = jnp.zeros_like(dq)
    for r in range(parts):
        o, ga, gq, h = (o0, ga0, gq0, h0) if r < half else (o1, ga1, gq1, h1)
        dp[...] += nn(o[r % half], ga[r % half])
        dq[...] += nn(gq[r % half], h[r % half])
    n = (dp.shape[0] + dq.shape[0]) // chunks
    edge = dp.shape[0] // n
    rank = ids[1] & (chunks - 1)
    for pair in range(chunks // 2):
        source, at = (dp, 2 * pair * n) if 2 * pair < edge else (dq, (2 * pair - edge) * n)
        put_chunk(
            keep, send, pair_spots(pair, rank, orders), (rank & 1) == 1,
            source[at : at + n, :], source[at + n : at + 2 * n, :], 0,
        )
    width = small.shape[1]
    small[...] = jnp.zeros_like(small)
    small[0:5, :] = u0[0:5, :] + u1[0:5, :]
    small[5:6, :] = ob[...]
    at = 6
    for line in (q0[0:1, :] + q1[0:1, :], hb[...]):
        for low in range(0, line.shape[1], width):
            high = min(low + width, line.shape[1])
            small[at : at + 1, 0 : high - low] = line[:, low:high]
            at += 1
    held = width // (2 * LANES)
    for h in range(heads):
        block = t0[h * SLOTS : (h + 1) * SLOTS, :] + t1[h * SLOTS : (h + 1) * SLOTS, :]
        block = jnp.concatenate([block, jnp.zeros((SLOTS, LANES), F32)], axis=1)
        slid = pltpu.roll(block, 0, 1, stride=1, stride_axis=0)
        low = h % held * 2 * LANES
        small[at + h // held : at + h // held + 1, low : low + 2 * LANES] = jnp.sum(
            slid, axis=0, keepdims=True
        )


def patch_grad_kernel(rows, g1, e0, e1, x, gain, out):
    hat, inv = normalize(x[0].astype(F32))
    grad = g1[0] + norm_back(hat, inv, line(gain), e0[0].astype(F32) + e1[0].astype(F32))
    out[...] = grad[0:rows, :]


def proto_grad_kernel(dims, ids, score, pooled, proto, frozen, out, ordered):
    crops, slots, weights = dims

    @pl.when(pl.program_id(0) == 0)
    def _():
        count = pooled.shape[0]
        column = lax.broadcasted_iota(jnp.int32, (1, count), 1)
        block = column // slots
        device = jnp.zeros((1, count), jnp.int32)
        for k, weight in enumerate(weights):
            device = device + ((block >> k) & 1) * weight
        inside = column - block * slots
        target = jnp.where(inside < crops, (device ^ ids[2]) * crops + inside, -1)
        row = lax.broadcasted_iota(jnp.int32, (ordered.shape[0], count), 0)
        hot = (row == target).astype(F32).astype(BF)
        ordered[...] = nn(hot, pooled[...]).astype(BF)

    keep = (1 - frozen[...]).astype(F32).astype(BF)
    grad = nn(jnp.transpose(score[...] * keep), ordered[...])
    p = proto[...].astype(F32)
    inverse = lax.rsqrt(jnp.sum(p * p, axis=1, keepdims=True) + 1e-06)
    unit = p * inverse
    out[...] = (grad - unit * jnp.sum(unit * grad, axis=1, keepdims=True)) * inverse


def unpack_kernel(layout, own, places, held, *refs):
    count = len(layout)
    outs, wides, sems = refs[-2 * count - 1 : -count - 1], refs[-count - 1 : -1], refs[-1]
    pairs, _, wide = held.shape
    core = places[0] if own else 1 - places[0]
    copies = []
    for pair in range(pairs):
        at = places[(1 if own else 1 + pairs) + pair]
        for k, (first, last, low, n, parts) in enumerate(layout):
            if not first <= pair < last:
                continue
            buffer = wides[k].at[pair - first]
            for part in range(parts):
                rows = slice(low + part * n, low + (part + 1) * n)
                buffer[:, part * wide : (part + 1) * wide] = held[at, rows, :].astype(F32)
            start = pl.multiple_of((2 * (pair - first) + core) * n, n)
            copies.append(
                pltpu.make_async_copy(buffer, outs[k].at[pl.ds(start, n), :], sems.at[k, pair])
            )
            copies[-1].start()
    for copy in copies:
        copy.wait()


def tie(v, *after):
    return lax.optimization_barrier((v, *after))[0]


def rounds(threads):
    done, waiting = {}, {name: next(thread) for name, thread in threads.items()}
    while waiting:
        ready = lax.optimization_barrier(waiting)
        waiting = {}
        for name, value in ready.items():
            try:
                waiting[name] = threads[name].send(value)
            except StopIteration as stop:
                done[name] = stop.value
    return done


def finish_kernel(dims, small, *outs):
    heads, head_size, hidden = dims
    width = small.shape[1]
    wide = 3 * head_size
    for i in range(6):
        outs[i][...] = small[i, :]
    at = 6
    for h in range(heads):
        row, low = at + h * wide // width, h * wide % width
        line = small[row : row + 1, low : low + wide]
        outs[6][h : h + 1, 0:head_size] = line[:, 0:head_size]
        outs[6][h : h + 1, head_size:] = line[:, 2 * head_size :]
    at += -(-heads * wide // width)
    for low in range(0, hidden, width):
        high = min(low + width, hidden)
        outs[8][low:high] = small[at, 0 : high - low]
        at += 1
    held = width // (2 * LANES)
    for h in range(heads):
        low = h % held * 2 * LANES
        row = at + h // held
        outs[7][h : h + 1, :] = small[row : row + 1, low : low + outs[7].shape[1]]


def partner(axis, bit):
    return [(i, i ^ bit) for i in range(lax.axis_size(axis))]


def swap(v, axis, bit):
    return lax.ppermute(v, axis, partner(axis, bit))


def bits_of(count):
    return [1 << i for i in range(count.bit_length() - 1)]


def add_low(a, b):
    return (a.astype(F32) + b.astype(F32)).astype(a.dtype)


def gather_halves(v, axis):
    held = v[None]
    bits = bits_of(lax.axis_size(axis))
    for bit in bits[:-1]:
        held = jnp.concatenate([held, swap(held, axis, bit)], axis=0)
    return held, swap(held, axis, bits[-1])


def sum_halves(v, axis):
    bits = bits_of(lax.axis_size(axis))
    for bit in bits[:-1]:
        other = swap(v, axis, bit)
        shape = other.shape
        other = other.reshape((shape[0] // (2 * bit), 2, bit) + shape[1:])[:, ::-1].reshape(shape)
        v = add_low(v, other)
    return v, swap(v, axis, bits[-1])


def scatter_halves(v, axis, count=None):
    bits = bits_of(count or lax.axis_size(axis))
    for bit in bits[:0:-1]:
        v = add_low(v[:bit], swap(v[bit:], axis, bit))
    return v[:1], swap(v[1:], axis, 1)


def gather_all(v, steps):
    for axis, bit in steps:
        v = jnp.concatenate([v, swap(v, axis, bit)], axis=0)
    return v


def mixed_swap(v, bits):
    size = lax.axis_size("dp")
    return lax.ppermute(v, "dp", [(i, i ^ bits[i & 1]) for i in range(size)])


def add_halves(kept, other):
    half = kept.shape[0] // 2
    return add_low(kept[:half], other[:half]), add_low(kept[half:], other[half:])


def unpack(places, held, before, layout, shapes, name):
    own = not before
    anywhere = pl.BlockSpec(memory_space=pl.ANY)
    return pl.pallas_call(
        functools.partial(unpack_kernel, layout, own),
        grid_spec=pltpu.PrefetchScalarGridSpec(
            num_scalar_prefetch=1,
            grid=(1,),
            in_specs=[whole(held.shape)] + [anywhere] * len(before),
            out_specs=[anywhere] * len(shapes),
            scratch_shapes=[
                *[
                    pltpu.VMEM((last - first, n, shape[1]), F32)
                    for (first, last, _, n, _), shape in zip(layout, shapes)
                ],
                pltpu.SemaphoreType.DMA((len(layout), held.shape[0])),
            ],
        ),
        out_shape=[sds(shape, F32) for shape in shapes],
        input_output_aliases={2 + i: i for i in range(len(before))},
        compiler_params=pltpu.CompilerParams(
            dimension_semantics=("arbitrary",), vmem_limit_bytes=20 * 2**20
        ),
        name=name,
    )(places, held, *before)


def unpack_both(places, own, other, layout, shapes, name):
    first = unpack(places, own, (), layout, shapes, name + "_own")
    return unpack(places, other, tuple(first), layout, shapes, name + "_other")


def largest(count, most):
    return max(n for n in range(1, most + 1) if count % n == 0)


def per_device(
    patches,
    out_grad,
    score_grad,
    crop_size,
    frozen,
    attn_gain,
    attn_shift,
    qkv_weight,
    qkv_bias,
    rel_table,
    proj_weight,
    proj_bias,
    mlp_gain,
    mlp_shift,
    hidden_weight,
    hidden_bias,
    output_weight,
    output_bias,
    prototypes,
):
    rows, width = patches.shape
    padded = -(-rows // 16) * 16
    parts = lax.axis_size("tensor")
    groups = lax.axis_size("dp")
    heads = qkv_weight.shape[1]
    head_size = qkv_weight.shape[2] // 3
    hidden = hidden_weight.shape[1]
    inner = heads * head_size
    group_crops = crop_size.shape[0]
    crops = group_crops // parts
    slots = -(-crops // 16) * 16
    protos = prototypes.shape[0]
    all_rows = parts * padded
    half = parts // 2
    tensor_rank, dp_rank = lax.axis_index("tensor"), lax.axis_index("dp")
    ids = jnp.stack([tensor_rank, dp_rank, dp_rank * parts + tensor_rank]).astype(jnp.int32)
    chunks = groups
    while (width // chunks) % 16 or (hidden // chunks) % 16 or (4 * inner // chunks) % 16:
        chunks //= 2
    pairs = chunks // 2
    scatter = [b for b in bits_of(chunks) if b > 1]
    rest_bits = [b for b in bits_of(groups) if b >= chunks]
    orders_a = (scatter, scatter[1:2] + scatter[:1] + scatter[2:])
    orders_b = orders_a
    vector = whole((width,))

    x0, x1 = gather_halves(patches, "tensor")
    g0, g1 = gather_halves(out_grad, "tensor")

    proto_step = min(512, protos)
    crop_bits = bits_of(groups)[1:]
    crop_rows = -(-group_crops // 8) * 8
    crop_shape = (groups // 2, crop_rows, width)
    def crop_step(kept, other, bit, *after):
        kept, other = (lax.optimization_barrier((v, after))[0] for v in (kept, other))
        half = kept.shape[0] // 2
        total = kept + other.astype(F32)
        return total[:half], swap(total[half:].astype(BF), "dp", bit)

    w_t = jnp.transpose(qkv_weight, (1, 2, 0)).reshape(3 * inner, width)
    wp = proj_weight.reshape(inner, width)
    unroll = largest(heads, 12)
    unroll_first = largest(heads, 6)
    block3 = lambda a, b: pl.BlockSpec((1, a, b), lambda i, *_: (i, 0, 0))
    halves3 = lambda a, b, dtype: (sds((half, a, b), dtype), block3(a, b))

    def attend(first, x, ids):
        dims = (first, rows, padded, heads, head_size, crops, unroll_first)
        return call(
            functools.partial(attend_kernel, dims),
            (half,),
            [
                block3(rows, width),
                vector,
                vector,
                whole(w_t.shape),
                whole(qkv_bias.shape),
                whole(tables.shape),
                whole(wp.shape),
            ],
            [
                halves3(padded, width, BF),
                halves3(padded, width, BF),
                halves3(3 * inner, padded, BF),
                (
                    sds((half, heads, padded, padded), BF),
                    pl.BlockSpec((1, heads, padded, padded), lambda i, *_: (i, 0, 0, 0)),
                ),
                halves3(inner, padded, BF),
                halves3(padded, width, BF),
            ],
            [
                pltpu.VMEM((padded, width), F32),
                pltpu.VMEM((heads * 2 * SLOTS, padded), BF),
                pltpu.VMEM((padded, padded), F32),
            ],
            2,
            (ids, crop_size, x, attn_gain, attn_shift, w_t, qkv_bias, tables, wp),
            "attend",
            all_rows * 4 * inner * width,
            20,
        )

    crop_keep, crop_send = call(
        functools.partial(crop_grad_kernel, groups, group_crops, crop_bits),
        (protos // proto_step,),
        [
            pl.BlockSpec((score_grad.shape[0], proto_step), lambda i, s: (0, i)),
            pl.BlockSpec((proto_step, width), lambda i, s: (i, 0)),
        ],
        [(sds(crop_shape, F32), whole(crop_shape)), (sds(crop_shape, F32), whole(crop_shape))],
        [pltpu.VMEM((score_grad.shape[0], width), F32)],
        1,
        (ids, score_grad, prototypes),
        "crop_grads",
        2 * score_grad.shape[0] * protos * width,
        16,
    )
    crop_other = swap(tie(crop_send, x1), "dp", 1)
    tables = call(
        functools.partial(table_kernel, heads, head_size**0.5),
        (1,),
        [whole(rel_table.shape)],
        [(sds((heads * 2 * SLOTS, LANES), BF), whole((heads * 2 * SLOTS, LANES)))],
        [],
        1,
        (tie(ids, crop_send), rel_table),
        "tables",
        0,
        8,
    )[0]
    crop_held = crop_step(crop_keep, crop_other, crop_bits[0], tables)
    xf0, h1_0, qkv0, pt0, ot0, a0 = attend(0, x0, tie(ids, crop_held[0]))
    a0, g1 = lax.optimization_barrier((a0, g1))
    b0 = swap(a0, "tensor", 1)
    crop_held = crop_step(*crop_held, crop_bits[1], a0)
    xf1, h1_1, qkv1, pt1, ot1, a1 = attend(half, x1, tie(ids, crop_held[0]))
    b1 = swap(tie(a1, b0, g1), "tensor", 1)
    if parts > 2:
        a_all, b_all = sum_halves(jnp.concatenate([a0, a1]), "tensor")
        a0, a1, b0, b1 = a_all[:half], a_all[half:], b_all[:half], b_all[half:]
    for bit in crop_bits[2:-1]:
        crop_held = crop_step(*crop_held, bit, a1)
    kept, other = (tie(v, a1) for v in crop_held)
    total = kept + other.astype(F32)
    kept, sent = total[:1].astype(BF), total[1:].astype(BF)
    far = crop_bits[-1] * parts
    crop_terms = [total[:1], swap(sent, ("dp", "tensor"), far)]
    for move in range(1, parts):
        crop_terms += [
            swap(kept, ("dp", "tensor"), move),
            swap(sent, ("dp", "tensor"), far + move),
        ]

    crops_slots = -(-group_crops // 16) * 16
    full = whole((parts, padded, width))
    columns = lambda a: whole((a, hidden))
    y1, gy, h2, gz, m, gu, gh2_near, gh2_far, ob, hb = call(
        functools.partial(hidden_kernel, (parts, rows, padded, crops, group_crops)),
        (1,),
        [
            *[whole((half, padded, width))] * 6,
            whole(g0.shape),
            whole(g1.shape),
            *[whole(kept.shape)] * len(crop_terms),
            vector,
            vector,
            vector,
            columns(width),
            columns(1),
            whole((hidden, width)),
        ],
        [
            (sds((parts, padded, width), F32), full),
            (sds((parts, padded, width), F32), full),
            (sds((all_rows, width), BF), whole((all_rows, width))),
            (sds((all_rows, width), BF), whole((all_rows, width))),
            (sds((all_rows, hidden), BF), columns(all_rows)),
            (sds((all_rows, hidden), BF), columns(all_rows)),
            (sds((half, padded, width), BF), whole((half, padded, width))),
            (sds((half, padded, width), BF), whole((half, padded, width))),
            (sds((1, width), F32), whole((1, width))),
            (sds((1, hidden), F32), columns(1)),
        ],
        [
            pltpu.VMEM((padded, width), F32),
            pltpu.VMEM((crops_slots, width), F32),
            pltpu.VMEM((all_rows, width), F32),
        ],
        2,
        (
            ids, crop_size, xf0, xf1, a0, a1, b0, b1, g0, g1, *crop_terms, proj_bias, mlp_gain, mlp_shift,
            hidden_weight, hidden_bias.reshape(1, hidden), output_weight,
        ),
        "hidden",
        6 * all_rows * hidden * width,
        40,
    )
    near_other = swap(gh2_near, "tensor", half)

    chunks_step = chunks
    wide = min(hidden, width)
    n1, n2 = width // chunks, hidden // chunks
    rows_a = (n1 * hidden + n2 * width) // wide
    chunk_a = whole((pairs, rows_a, wide))
    keep_a, send_a = call(
        functools.partial(hidden_grad_kernel, (chunks, chunks_step, wide, orders_a)),
        (1,),
        [
            whole((all_rows, width)),
            whole((all_rows, width)),
            pl.BlockSpec((all_rows, hidden), lambda i, s: (0, i)),
            pl.BlockSpec((all_rows, hidden), lambda i, s: (0, i)),
        ],
        [
            (sds((pairs, rows_a, wide), BF), chunk_a),
            (sds((pairs, rows_a, wide), BF), chunk_a),
        ],
        [pltpu.VMEM((width, all_rows), BF)],
        1,
        (ids, h2, gz, m, gu),
        "hidden_grads",
        4 * all_rows * hidden * width,
        30,
    )
    if parts > 2:
        e_all, f_all = sum_halves(jnp.concatenate([gh2_near, gh2_far]), "tensor")
        gh2_near, gh2_far = e_all[:half], e_all[half:]
        near_other, far_other = f_all[:half], f_all[half:]
    else:
        far_other = swap(tie(gh2_far, near_other), "tensor", half)
    send_a = tie(send_a, near_other)
    cut = pairs // 2
    core_high = swap(send_a[cut:], "dp", 1)
    core_low = swap(send_a[:cut], "dp", 1)

    n_b = 4 * inner // chunks
    chunk_b = whole((pairs, n_b, width))

    def attend_back(first, e0, e1, xf, qkv, pt, ids):
        dims = (first, rows, padded, heads, head_size, crops, unroll)
        at = lambda a, b: pl.BlockSpec((1, a, b), lambda i, *_: (first + i, 0, 0))
        return call(
            functools.partial(attend_back_kernel, dims),
            (half,),
            [
                at(padded, width),
                at(padded, width),
                block3(padded, width),
                block3(padded, width),
                vector,
                block3(padded, width),
                block3(3 * inner, padded),
                pl.BlockSpec((1, heads, padded, padded), lambda i, *_: (i, 0, 0, 0)),
                whole(wp.shape),
                whole(w_t.shape),
            ],
            [
                (sds((half, padded, width), F32), block3(padded, width)),
                (sds((half, padded, width), BF), block3(padded, width)),
                (sds((half, padded, width), BF), block3(padded, width)),
                (sds((half, 3 * inner, padded), BF), block3(3 * inner, padded)),
                (sds((8, width), F32), whole((8, width))),
                (sds((8, 3 * inner), F32), whole((8, 3 * inner))),
                (sds((heads * SLOTS, LANES), F32), whole((heads * SLOTS, LANES))),
            ],
            [pltpu.VMEM((inner, padded), BF), pltpu.VMEM((heads * SLOTS, padded), F32)],
            2,
            (ids, crop_size, y1, gy, e0, e1, mlp_gain, xf, qkv, pt, wp, w_t),
            "attend_back",
            2 * all_rows * 4 * inner * width,
            22,
        )

    z_part = call(
        functools.partial(share_kernel, parts, padded),
        (1,),
        [whole((all_rows, hidden)), whole((hidden, width))],
        [(sds((parts, padded, width), BF), full)],
        [pltpu.VMEM((all_rows, width), F32)],
        0,
        (tie(m, keep_a), output_weight),
        "share",
        2 * all_rows * hidden * width,
        16,
    )[0]
    sent_a = add_low(tie(keep_a[cut:], z_part), tie(core_high, z_part))
    other_a = mixed_swap(sent_a, list(zip(*orders_a))[0])
    _, gh1_far, ga1, gq1, sums1, qb1, tt1 = attend_back(
        half, gh2_far, near_other, xf1, qkv1, pt1, tie(ids, sent_a)
    )
    gh1_far, far_other, core_low = lax.optimization_barrier((gh1_far, far_other, core_low))
    kept_a = add_low(tie(keep_a[:cut], gh1_far), core_low)
    z0, z1 = scatter_halves(tie(z_part, gh1_far), "tensor")
    g_own, gh1_near, ga0, gq0, sums0, qb0, tt0 = attend_back(
        0, gh2_near, far_other, xf0, qkv0, pt0, tie(ids, gh1_far)
    )
    small_rows = 6 + -(-3 * inner // width) + -(-hidden // width) + -(-heads // (width // (2 * LANES)))
    small_rows = -(-small_rows // 8) * 8
    args = (ot0, ot1, ga0, ga1, gq0, gq1, h1_0, h1_1, sums0, sums1, qb0, qb1, tt0, tt1, ob, hb)
    keep_b, send_b, small = call(
        functools.partial(attend_grad_kernel, (parts, heads, chunks, orders_b)),
        (1,),
        [whole(v.shape) for v in args],
        [
            (sds((pairs, n_b, width), BF), chunk_b),
            (sds((pairs, n_b, width), BF), chunk_b),
            (sds((small_rows, width), F32), whole((small_rows, width))),
        ],
        [pltpu.VMEM((inner, width), F32), pltpu.VMEM((3 * inner, width), F32)],
        1,
        (tie(ids, other_a), *args),
        "attend_grads",
        2 * all_rows * 4 * inner * width,
        30,
    )

    one = whole((1, padded, width))

    def places_of(orders):
        spots = pair_spots(jnp.arange(pairs, dtype=jnp.int32), dp_rank & (chunks - 1), orders)
        return jnp.concatenate([(dp_rank & 1)[None], *spots]).astype(jnp.int32)

    def all_sum(kept, other, orders, begin, cuts):
        stages = list(zip(*orders))
        for stage in stages[begin:-1]:
            kept, sent = add_halves(kept, other)
            kept, other = yield kept, mixed_swap(sent, stage)
        held = add_low(kept, other)
        for bits in [stages[-1], *[(bit, bit) for bit in rest_bits]]:
            size = held.shape[0] // cuts
            pieces = [held[i * size : (i + 1) * size] for i in range(cuts)]
            for i in range(cuts):
                pieces[i], pieces[i + 1 :], other = yield (
                    pieces[i],
                    pieces[i + 1 :],
                    mixed_swap(pieces[i], bits),
                )
                pieces[i] = add_low(pieces[i], other)
            held = jnp.concatenate(pieces, axis=0) if cuts > 1 else pieces[0]
        for stage in stages[-2::-1]:
            held = jnp.concatenate((yield held, mixed_swap(held, stage)), axis=0)
        return held, swap(held, "dp", 1)

    def hidden_sum():
        kept, other = yield kept_a, other_a
        held, other = yield from all_sum(kept, other, orders_a, 1, 2)
        layout = (
            (0, pairs, 0, n1, hidden // wide),
            (0, pairs, rows_a - n2 * width // wide, n2, width // wide),
        )
        shapes = ((width, hidden), (hidden, width))
        return (yield unpack_both(places_of(orders_a), held, other, layout, shapes, "unpack_hidden"))

    def attend_sum():
        kept, sent = yield keep_b, send_b
        kept, other = yield kept, swap(sent, "dp", 1)
        held, other = yield from all_sum(kept, other, orders_b, 0, 1)
        edge = inner // (2 * n_b)
        layout = ((0, edge, 0, n_b, 1), (edge, pairs, 0, n_b, 1))
        shapes = ((inner, width), (3 * inner, width))
        return unpack_both(places_of(orders_b), held, other, layout, shapes, "unpack_attend")

    def patch():
        yield ()
        near, far = gh1_near, gh1_far
        if half > 1:
            near, far = yield near, swap(far, "tensor", half)
            near, far = scatter_halves(add_low(near, far), "tensor", half)
        else:
            far = swap(far, "tensor", 1)
        near, far = yield near, far
        return (yield call(
            functools.partial(patch_grad_kernel, rows),
            (1,),
            [one, one, one, one, vector],
            [(sds((rows, width), F32), whole((rows, width)))],
            [],
            0,
            (g_own, near, far, xf0, attn_gain),
            "patch_grads",
            0,
            24,
        )[0])

    def head():
        own, other, held = yield z0, z1, small
        block_out, pooled = call(
            functools.partial(result_kernel, (rows, padded, crops)),
            (1,),
            [one, one, one, vector],
            [
                (sds((rows, width), BF), whole((rows, width))),
                (sds((1, slots, width), BF), whole((1, slots, width))),
            ],
            [],
            2,
            (ids, crop_size, y1, own, other, output_bias),
            "result",
            0,
            24,
        )
        steps = [[b * parts] for b in bits_of(groups)[:0:-1]]
        steps += [[1, parts]] if parts == 2 else [[b] for b in [*bits_of(parts), parts]]
        weights = [weight for step in steps for weight in step]
        pooled = pooled[0]
        first = lax.broadcasted_iota(jnp.int32, (small_rows, 1), 0) < 2
        for step in steps:
            count = pooled.shape[0]
            high = lax.reduce_precision(held, 8, 7)
            payload = jnp.concatenate([pooled, high.astype(BF), (held - high).astype(BF)], axis=0)
            moves = [sum(w for k, w in enumerate(step) if i >> k & 1) for i in range(1, 2 ** len(step))]
            pooled, held, *others = yield (
                pooled,
                held,
                *[swap(payload, ("dp", "tensor"), move) for move in moves],
            )
            for move, other in zip(moves, others):
                high = other[count : count + small_rows].astype(F32)
                part = high + other[count + small_rows :].astype(F32)
                held = held + (jnp.where(first, part, 0.0) if move % parts else part)
            pooled = jnp.concatenate([pooled, *[other[:count] for other in others]], axis=0)
        step_spec = pl.BlockSpec((proto_step, width), lambda i, s: (i, 0))
        prototype_grad = call(
            functools.partial(proto_grad_kernel, (crops, slots, weights)),
            (protos // proto_step,),
            [
                pl.BlockSpec((score_grad.shape[0], proto_step), lambda i, s: (0, i)),
                whole(pooled.shape),
                step_spec,
                pl.BlockSpec((1, proto_step), lambda i, s: (0, i)),
            ],
            [(sds((protos, width), F32), step_spec)],
            [pltpu.VMEM((score_grad.shape[0], width), BF)],
            1,
            (ids, score_grad, pooled, prototypes, frozen.reshape(1, protos)),
            "proto_grads",
            2 * score_grad.shape[0] * protos * width,
            40,
        )[0]
        finished = call(
            functools.partial(finish_kernel, (heads, head_size, hidden)),
            (1,),
            [whole(held.shape)],
            [
                *[(sds((width,), F32), whole((width,)))] * 6,
                (sds((heads, 2 * head_size), F32), whole((heads, 2 * head_size))),
                (sds(rel_table.shape, F32), whole(rel_table.shape)),
                (sds((hidden,), F32), whole((hidden,))),
            ],
            [],
            0,
            (held,),
            "finish",
            0,
            8,
        )
        prototype_grad, finished = yield prototype_grad, finished
        return block_out, prototype_grad, finished

    threads = {"A": hidden_sum(), "B": attend_sum(), "H": head(), "P": patch()}
    done = rounds(threads)
    out_w1, out_w2 = done["A"]
    proj_weight_grad, qkv_weight_grad = done["B"]
    block_out, prototype_grad, (*small, qb, rel, hb) = done["H"]
    return (
        block_out,
        done["P"],
        small[0],
        small[1],
        jnp.transpose(qkv_weight_grad.reshape(heads, 3 * head_size, width), (2, 0, 1)),
        qb,
        rel,
        proj_weight_grad.reshape(heads, head_size, width),
        small[4],
        small[2],
        small[3],
        out_w1,
        hb,
        out_w2,
        small[5],
        prototype_grad,
    )


def solution(mesh):
    both = ("dp", "tensor")
    return jax.shard_map(
        per_device,
        mesh=mesh,
        in_specs=(
            P(both, None),
            P(both, None),
            P(None, both),
            P("dp"),
            P(both),
            P(),
            P(),
            P(None, "tensor", None),
            P("tensor", None),
            P("tensor", None),
            P("tensor", None, None),
            P(),
            P(),
            P(),
            P(None, "tensor"),
            P("tensor"),
            P("tensor", None),
            P(),
            P(both, None),
        ),
        out_specs=(
            P(both, None),
            P(both, None),
            P(),
            P(),
            P(None, "tensor", None),
            P("tensor", None),
            P("tensor", None),
            P("tensor", None, None),
            P(),
            P(),
            P(),
            P(None, "tensor"),
            P("tensor"),
            P("tensor", None),
            P(),
            P(both, None),
        ),
        check_vma=False,
    )
```

```python
import functools

import jax
import jax.numpy as jnp
import numpy as np
from jax import lax
from jax.experimental import pallas as pl
from jax.experimental.pallas import tpu as pltpu
from jax.sharding import PartitionSpec as P

EPS = 1e-05
BF = jnp.bfloat16
F32 = jnp.float32
HIGH = lax.Precision.HIGHEST
SIDE = 7
PLACES = SIDE * SIDE
OFFSETS = 2 * SIDE - 1
LAST = (SIDE - 1) * (OFFSETS + 1)
SLOTS = 96
LANES = 128
COST = 0.01


def nn(a, b):
    return jnp.dot(a, b, preferred_element_type=F32)


def nt(a, b):
    return lax.dot_general(a, b, (((1,), (1,)), ((), ())), preferred_element_type=F32)


def split(v):
    high = v.astype(BF)
    return high, (v - high.astype(F32)).astype(BF)


def line(ref):
    return ref[...].reshape(1, -1)


def normalize(v):
    center = v - jnp.mean(v, axis=-1, keepdims=True)
    spread = jnp.mean(center * center, axis=-1, keepdims=True)
    inverse = lax.rsqrt(spread + EPS)
    return center * inverse, inverse


def norm_back(hat, inverse, gain, grad):
    scaled = grad * gain
    first = jnp.mean(scaled, axis=-1, keepdims=True)
    second = jnp.mean(scaled * hat, axis=-1, keepdims=True)
    return (scaled - first - hat * second) * inverse


def row_layout(sizes_ref, base, crops, rows, padded, axis):
    shape = (padded, 1) if axis == 0 else (1, padded)
    position = lax.broadcasted_iota(jnp.int32, shape, axis)
    start = jnp.int32(0)
    segment = jnp.zeros(shape, jnp.int32)
    first = jnp.zeros(shape, jnp.int32)
    length = jnp.zeros(shape, jnp.int32)
    for crop in range(crops):
        size = sizes_ref[base + crop]
        reached = position >= start
        segment = jnp.where(reached, crop, segment)
        first = jnp.where(reached, start, first)
        length = jnp.where(reached, size, length)
        start = start + size
    offset = position - first
    by_seven = offset + ((offset * 37) >> 8) * (OFFSETS - SIDE)
    by_three = offset + ((offset * 11) >> 5) * (OFFSETS - 3)
    place = jnp.where(length == PLACES, by_seven, by_three)
    real = position < rows
    segment = jnp.where(real, segment, crops)
    place = jnp.where(real, place, 2 * LANES)
    return segment, place, jnp.where(real, length, 1).astype(F32)


def call(body, grid, ins, outs, scratch, prefetch, args, name, flops, vmem):
    moved = sum(int(np.prod(a.shape)) * a.dtype.itemsize for a in args)
    moved += sum(int(np.prod(s.shape)) * s.dtype.itemsize for s, _ in outs)
    return pl.pallas_call(
        body,
        grid_spec=pltpu.PrefetchScalarGridSpec(
            num_scalar_prefetch=prefetch,
            grid=grid,
            in_specs=ins,
            out_specs=[spec for _, spec in outs],
            scratch_shapes=scratch,
        ),
        out_shape=[shape for shape, _ in outs],
        compiler_params=pltpu.CompilerParams(
            dimension_semantics=("arbitrary",) * len(grid), vmem_limit_bytes=vmem * 2**20
        ),
        cost_estimate=pl.CostEstimate(
            flops=int(flops * COST), bytes_accessed=int(moved * COST), transcendentals=0
        ),
        name=name,
    )(*args)


def whole(shape):
    zeros = (0,) * len(shape)
    return pl.BlockSpec(tuple(shape), lambda *_: zeros)


def sds(shape, dtype):
    return jax.ShapeDtypeStruct(tuple(shape), dtype)


def crop_grad_kernel(groups, crops, bits, ids, score, proto, keep, send, total):
    step = pl.program_id(0)

    @pl.when(step == 0)
    def _():
        total[...] = jnp.zeros_like(total)

    p = proto[...].astype(F32)
    unit = p * lax.rsqrt(jnp.sum(p * p, axis=1, keepdims=True) + 1e-06)
    total[...] += nn(score[...], unit.astype(BF))

    @pl.when(step == pl.num_programs(0) - 1)
    def _():
        odd = (ids[1] & 1) == 1
        for pair in range(groups // 2):
            at = 0
            for bit in bits:
                at = 2 * at + (((pair ^ (ids[1] >> 1)) >> (bit.bit_length() - 2)) & 1)
            first = total[2 * pair * crops : (2 * pair + 1) * crops, :]
            second = total[(2 * pair + 1) * crops : (2 * pair + 2) * crops, :]
            keep[at, 0:crops, :] = jnp.where(odd, second, first)
            send[at, 0:crops, :] = jnp.where(odd, first, second)
            if keep.shape[1] > crops:
                tail = jnp.zeros((keep.shape[1] - crops, keep.shape[2]), F32)
                keep[at, crops:, :] = tail
                send[at, crops:, :] = tail


def table_kernel(heads, scale, ids, rel, tables):
    for h in range(heads):
        line = jnp.concatenate(
            [rel[h : h + 1, :], jnp.zeros((1, 2 * LANES - rel.shape[1]), F32)], axis=1
        )
        line = jnp.broadcast_to(line * scale, (8, 2 * LANES))
        line = pltpu.roll(line, 2 * LANES - LAST % 8, 1)
        line = jnp.broadcast_to(line[0:1, :], (SLOTS, 2 * LANES))
        slid = pltpu.roll(line, 2 * LANES - LAST // 8 * 8, 1, stride=1, stride_axis=0)
        high, low = split(slid[:, 0:LANES])
        tables[2 * h * SLOTS : (2 * h + 1) * SLOTS, :] = high
        tables[(2 * h + 1) * SLOTS : (2 * h + 2) * SLOTS, :] = low


def attend_kernel(
    dims, ids, sizes, x0, gain, shift, w, bias, tables, wp, xo, ho, qo, po, oo, ao, xs, rr, hide
):
    first, rows, padded, heads, head_size, crops, unroll = dims
    wide = 3 * head_size
    step = pl.program_id(0)
    base = ((first + step) ^ ids[0]) * crops
    tail = padded - 8
    xs[tail:padded, :] = jnp.zeros((padded - tail, xs.shape[1]), F32)
    xs[0:rows, :] = x0[0].astype(F32)
    x = xs[...]
    xo[0] = x.astype(BF)
    hat, _ = normalize(x)
    h1 = (hat * line(gain) + line(shift)).astype(BF)
    ho[0] = h1
    mixed = nt(w[...], h1)
    bias_cols = jnp.transpose(bias[...])
    for h in range(heads):
        low = h * wide
        qo[0, low : low + head_size, :] = (
            mixed[low : low + head_size] + bias_cols[0:head_size, h : h + 1]
        ).astype(BF)
        qo[0, low + head_size : low + 2 * head_size, :] = mixed[
            low + head_size : low + 2 * head_size
        ].astype(BF)
        qo[0, low + 2 * head_size : low + wide, :] = (
            mixed[low + 2 * head_size : low + wide] + bias_cols[head_size : 2 * head_size, h : h + 1]
        ).astype(BF)
    seg_row, place_row, _ = row_layout(sizes, base, crops, rows, padded, 1)
    seg_col, place_col, _ = row_layout(sizes, base, crops, rows, padded, 0)
    hide[...] = jnp.where(seg_col == seg_row, 0.0, -jnp.inf).astype(F32)
    lane = lax.broadcasted_iota(jnp.int32, (padded, LANES), 1)
    hot = (lane == place_col).astype(F32).astype(BF)
    slot = lax.broadcasted_iota(jnp.int32, (LANES, padded), 0)
    hot_t = (slot == place_row).astype(F32).astype(BF)

    rr[...] = nn(tables[...], hot_t).astype(BF)
    zeros = jnp.zeros((2 * LANES - 2 * SLOTS - head_size, padded), BF)

    def some_heads(i, carry):
        for u in range(unroll):
            h = i * unroll + u
            slab = qo[0, pl.ds(pl.multiple_of(h * wide, 32), wide), :]
            q = slab[0:head_size]
            v = slab[2 * head_size : wide]
            k = slab[head_size : 2 * head_size]
            left_t = jnp.transpose(jnp.concatenate([k, hot_t[0:SLOTS]], axis=0))
            left = jnp.concatenate([left_t, hot], axis=1)
            biases = rr[pl.ds(pl.multiple_of(h * 2 * SLOTS, 64), 2 * SLOTS), :]
            right = jnp.concatenate([q, biases, zeros], axis=0)
            s = nn(left, right) * (head_size**-0.5) + hide[...]
            e = jnp.exp(s - jnp.max(s, axis=0, keepdims=True))
            p = (e * (1.0 / jnp.sum(e, axis=0, keepdims=True))).astype(BF)
            po[0, h] = p
            oo[0, pl.ds(pl.multiple_of(h * head_size, 32), head_size), :] = nn(v, p).astype(BF)
        return carry

    lax.fori_loop(0, heads // unroll, some_heads, 0)
    ao[0] = nn(jnp.transpose(oo[0]), wp[...]).astype(BF)


def hidden_kernel(
    dims, ids, sizes, x0, x1, a0, a1, b0, b1, g0, g1, *rest,
):
    parts, rows, padded, crops, group_crops = dims
    terms, rest = rest[: 2 * parts], rest[2 * parts :]
    pb, gain, shift, w1, bias1, w2 = rest[:6]
    y1o, gyo, h2o, gzo, mo, guo, gh0, gh1, obo, hbo, gs, cs, total = rest[6:]
    step = pl.program_id(0)

    @pl.when(step == 0)
    def _():
        cs[...] = jnp.zeros_like(cs)
        cs[0 : terms[0].shape[1], :] = sum(term[0].astype(F32) for term in terms)
        high, low = split(cs[...])
        bias_sum = jnp.zeros((1, gs.shape[1]), F32)
        tail, half = padded - 8, parts // 2
        for r in range(parts):
            x, own, other, g = (x0, a0, b1, g0) if r < half else (x1, a1, b0, g1)
            k = r % half
            y1 = x[k].astype(F32) + (own[k].astype(F32) + other[k].astype(F32)) + line(pb)
            y1o[r] = y1
            hat, _ = normalize(y1)
            h2o[r * padded : (r + 1) * padded, :] = (hat * line(gain) + line(shift)).astype(BF)
            base = (ids[0] ^ r) * crops
            segment, _, length = row_layout(sizes, base, crops, rows, padded, 0)
            lane = lax.broadcasted_iota(jnp.int32, (padded, cs.shape[0]), 1)
            mine = (lane == segment + base) & (segment < crops)
            hot = mine.astype(F32).astype(BF)
            gs[tail:padded, :] = jnp.zeros((padded - tail, gs.shape[1]), F32)
            gs[0:rows, :] = g[k].astype(F32)
            gy = gs[...] + (nn(hot, high) + nn(hot, low)) / length
            gyo[r] = gy
            gzo[r * padded : (r + 1) * padded, :] = gy.astype(BF)
            bias_sum = bias_sum + jnp.sum(gy, axis=0, keepdims=True)
        obo[...] = bias_sum
        total[...] = jnp.zeros_like(total)

    u = nn(h2o[...], w1[...]) + bias1[...]
    spread = 0.5 * (1.0 + lax.erf(u * np.float32(np.sqrt(0.5))))
    mo[...] = (u * spread).astype(BF)
    slope = spread + u * (jnp.exp(-0.5 * u * u) * np.float32(1.0 / np.sqrt(2.0 * np.pi)))
    gu = (nt(gzo[...], w2[...]) * slope).astype(BF)
    guo[...] = gu
    hbo[...] = jnp.sum(gu.astype(F32), axis=0, keepdims=True)
    total[...] += nt(gu, w1[...])

    @pl.when(step == pl.num_programs(0) - 1)
    def _():
        half = parts // 2
        for r in range(parts):
            gho = gh0 if r < half else gh1
            gho[r % half] = total[r * padded : (r + 1) * padded, :].astype(BF)


def spot(pair, mine, core, orders):
    spots = []
    for order in orders:
        at = 0
        for bit in order:
            source = pair if bit == order[-1] else pair ^ mine
            at = 2 * at + ((source >> (bit.bit_length() - 2)) & 1)
        spots.append(at)
    return jnp.where(core == 1, spots[1], spots[0])


def put_chunk(keep, send, spots, odd, first, second, at):
    rows = pl.ds(at, first.shape[0])
    keep[spots[0], rows, :] = jnp.where(odd, second, first).astype(BF)
    send[spots[1], rows, :] = jnp.where(odd, first, second).astype(BF)


def pair_spots(pair, rank, orders):
    core, mine = rank & 1, rank >> 1
    return spot(pair, mine, core, orders), spot(pair, mine, 1 - core, orders)


def hidden_grad_kernel(dims, ids, h2, gz, m, gu, keep, send, h2t):
    chunks, chunks_step, wide, orders = dims
    step = pl.program_id(0)
    rank = ids[1] & (chunks - 1)
    odd = (rank & 1) == 1

    @pl.when(step == 0)
    def _():
        h2t[...] = jnp.transpose(h2[...])

    d1 = nn(h2t[...], gu[...])
    n1 = d1.shape[0] // chunks
    steps = d1.shape[1] // wide
    for pair in range(chunks // 2):
        spots = pair_spots(pair, rank, orders)
        for part in range(steps):
            piece = d1[2 * pair * n1 : (2 * pair + 2) * n1, part * wide : (part + 1) * wide]
            at = pl.multiple_of((step * steps + part) * n1, 16)
            put_chunk(keep, send, spots, odd, piece[:n1], piece[n1:], at)
    d2 = nn(jnp.transpose(m[...]), gz[...])
    n2 = d2.shape[0] // chunks_step
    base = keep.shape[1] - d2.shape[1] // wide * n2
    for pair in range(chunks_step // 2):
        spots = pair_spots(step * (chunks_step // 2) + pair, rank, orders)
        for part in range(d2.shape[1] // wide):
            piece = d2[2 * pair * n2 : (2 * pair + 2) * n2, part * wide : (part + 1) * wide]
            put_chunk(keep, send, spots, odd, piece[:n2], piece[n2:], base + part * n2)


def share_kernel(parts, padded, m, w2, zo, total):
    step = pl.program_id(0)

    @pl.when(step == 0)
    def _():
        total[...] = jnp.zeros_like(total)

    total[...] += nn(m[...], w2[...])

    @pl.when(step == pl.num_programs(0) - 1)
    def _():
        for r in range(parts):
            zo[r] = total[r * padded : (r + 1) * padded, :].astype(BF)


def result_kernel(dims, ids, sizes, y1, z0, z1, bias, out, pooled):
    rows, padded, crops = dims
    y = y1[0] + (z0[0].astype(F32) + z1[0].astype(F32)) + line(bias)
    out[...] = y[0:rows, :].astype(BF)
    segment, _, _ = row_layout(sizes, ids[0] * crops, crops, rows, padded, 1)
    crop = lax.broadcasted_iota(jnp.int32, (pooled.shape[1], padded), 0)
    member = ((crop == segment) & (crop < crops)).astype(F32)
    high, low = split(y)
    hot = member.astype(BF)
    count = jnp.maximum(jnp.sum(member, axis=1, keepdims=True), 1.0)
    pooled[0] = ((nn(hot, high) + nn(hot, low)) / count).astype(BF)


def attend_back_kernel(
    dims, ids, sizes, y1, gy, e0, e1, gain, x, qkv, pt, wp, w, g1o, gho, gao, gqo, sums, qb, tt, go, by
):
    first, rows, padded, heads, head_size, crops, unroll = dims
    wide = 3 * head_size
    step = pl.program_id(0)
    base = ((first + step) ^ ids[0]) * crops

    @pl.when(step == 0)
    def _():
        sums[...] = jnp.zeros_like(sums)
        qb[...] = jnp.zeros_like(qb)
        tt[...] = jnp.zeros_like(tt)

    hat2, inv2 = normalize(y1[0])
    grad2 = e0[0].astype(F32) + e1[0].astype(F32)
    gy1 = gy[0] + norm_back(hat2, inv2, line(gain), grad2)
    g1o[0] = gy1
    ga = gy1.astype(BF)
    gao[0] = ga
    sums[2:3, :] += jnp.sum(grad2 * hat2, axis=0, keepdims=True)
    sums[3:4, :] += jnp.sum(grad2, axis=0, keepdims=True)
    sums[4:5, :] += jnp.sum(gy1, axis=0, keepdims=True)
    go[...] = nt(wp[...], ga).astype(BF)
    _, place_row, _ = row_layout(sizes, base, crops, rows, padded, 1)
    _, place_col, _ = row_layout(sizes, base, crops, rows, padded, 0)
    slot = lax.broadcasted_iota(jnp.int32, (SLOTS, padded), 0)
    hot_t = (slot == LAST - place_row).astype(F32).astype(BF)
    lane = lax.broadcasted_iota(jnp.int32, (padded, LANES), 1)
    hot = (lane == place_col).astype(F32).astype(BF)
    zeros_a = jnp.zeros((LANES - wide, padded), BF)
    zeros_b = jnp.zeros((2 * head_size, padded), BF)
    scale = head_size**-0.5

    def some_heads(i, carry):
        for u in range(unroll):
            h = i * unroll + u
            at = pl.multiple_of(h * wide, 32)
            slab = qkv[0, pl.ds(at, wide), :]
            q = slab[0:head_size]
            k = slab[head_size : 2 * head_size]
            goh = go[pl.ds(pl.multiple_of(h * head_size, 32), head_size), :]
            p = pt[0, h]
            slab_t = jnp.transpose(jnp.concatenate([slab, zeros_a], axis=0))
            gp = nn(slab_t, jnp.concatenate([zeros_b, goh, zeros_a], axis=0))
            pf = p.astype(F32)
            both = pf * gp
            gs = (both - pf * jnp.sum(both, axis=0, keepdims=True)).astype(BF)
            gv = nt(goh, p)
            gk = nt(q, gs)
            gqe = nn(jnp.concatenate([k, hot_t], axis=0), gs)
            gqo[0, pl.ds(at, head_size), :] = (gqe[0:head_size] * scale).astype(BF)
            gqo[0, pl.ds(at + head_size, head_size), :] = (gk * scale).astype(BF)
            gqo[0, pl.ds(at + 2 * head_size, head_size), :] = gv.astype(BF)
            by[pl.ds(pl.multiple_of(h * SLOTS, 32), SLOTS), :] = gqe[head_size:]
        return carry

    lax.fori_loop(0, heads // unroll, some_heads, 0)
    high, low = split(by[...])
    tt[...] += nn(high, hot) + nn(low, hot)
    g = gqo[0]
    qb[...] += nt(jnp.ones((8, padded), BF), g)
    gh1 = nn(jnp.transpose(g), w[...])
    gho[0] = gh1.astype(BF)
    hat1, _ = normalize(x[0].astype(F32))
    sums[0:1, :] += jnp.sum(gh1 * hat1, axis=0, keepdims=True)
    sums[1:2, :] += jnp.sum(gh1, axis=0, keepdims=True)


def attend_grad_kernel(
    dims, ids, o0, o1, ga0, ga1, gq0, gq1, h0, h1, u0, u1, q0, q1, t0, t1, ob, hb, keep, send, small, dp, dq
):
    parts, heads, chunks, orders = dims
    half = parts // 2
    dp[...] = jnp.zeros_like(dp)
    dq[...] = jnp.zeros_like(dq)
    for r in range(parts):
        o, ga, gq, h = (o0, ga0, gq0, h0) if r < half else (o1, ga1, gq1, h1)
        dp[...] += nn(o[r % half], ga[r % half])
        dq[...] += nn(gq[r % half], h[r % half])
    n = (dp.shape[0] + dq.shape[0]) // chunks
    edge = dp.shape[0] // n
    rank = ids[1] & (chunks - 1)
    for pair in range(chunks // 2):
        source, at = (dp, 2 * pair * n) if 2 * pair < edge else (dq, (2 * pair - edge) * n)
        put_chunk(
            keep, send, pair_spots(pair, rank, orders), (rank & 1) == 1,
            source[at : at + n, :], source[at + n : at + 2 * n, :], 0,
        )
    width = small.shape[1]
    small[...] = jnp.zeros_like(small)
    small[0:5, :] = u0[0:5, :] + u1[0:5, :]
    small[5:6, :] = ob[...]
    at = 6
    for line in (q0[0:1, :] + q1[0:1, :], hb[...]):
        for low in range(0, line.shape[1], width):
            high = min(low + width, line.shape[1])
            small[at : at + 1, 0 : high - low] = line[:, low:high]
            at += 1
    held = width // (2 * LANES)
    for h in range(heads):
        block = t0[h * SLOTS : (h + 1) * SLOTS, :] + t1[h * SLOTS : (h + 1) * SLOTS, :]
        block = jnp.concatenate([block, jnp.zeros((SLOTS, LANES), F32)], axis=1)
        slid = pltpu.roll(block, 0, 1, stride=1, stride_axis=0)
        low = h % held * 2 * LANES
        small[at + h // held : at + h // held + 1, low : low + 2 * LANES] = jnp.sum(
            slid, axis=0, keepdims=True
        )


def patch_grad_kernel(rows, g1, e0, e1, x, gain, out):
    hat, inv = normalize(x[0].astype(F32))
    grad = g1[0] + norm_back(hat, inv, line(gain), e0[0].astype(F32) + e1[0].astype(F32))
    out[...] = grad[0:rows, :]


def proto_grad_kernel(dims, ids, score, pooled, proto, frozen, out, ordered):
    crops, slots, weights = dims

    @pl.when(pl.program_id(0) == 0)
    def _():
        count = pooled.shape[0]
        column = lax.broadcasted_iota(jnp.int32, (1, count), 1)
        block = column // slots
        device = jnp.zeros((1, count), jnp.int32)
        for k, weight in enumerate(weights):
            device = device + ((block >> k) & 1) * weight
        inside = column - block * slots
        target = jnp.where(inside < crops, (device ^ ids[2]) * crops + inside, -1)
        row = lax.broadcasted_iota(jnp.int32, (ordered.shape[0], count), 0)
        hot = (row == target).astype(F32).astype(BF)
        ordered[...] = nn(hot, pooled[...]).astype(BF)

    keep = (1 - frozen[...]).astype(F32).astype(BF)
    grad = nn(jnp.transpose(score[...] * keep), ordered[...])
    p = proto[...].astype(F32)
    inverse = lax.rsqrt(jnp.sum(p * p, axis=1, keepdims=True) + 1e-06)
    unit = p * inverse
    out[...] = (grad - unit * jnp.sum(unit * grad, axis=1, keepdims=True)) * inverse


def unpack_kernel(layout, own, places, held, *refs):
    count = len(layout)
    outs, wides, sems = refs[-2 * count - 1 : -count - 1], refs[-count - 1 : -1], refs[-1]
    pairs, _, wide = held.shape
    core = places[0] if own else 1 - places[0]
    copies = []
    for pair in range(pairs):
        at = places[(1 if own else 1 + pairs) + pair]
        for k, (first, last, low, n, parts) in enumerate(layout):
            if not first <= pair < last:
                continue
            buffer = wides[k].at[pair - first]
            for part in range(parts):
                rows = slice(low + part * n, low + (part + 1) * n)
                buffer[:, part * wide : (part + 1) * wide] = held[at, rows, :].astype(F32)
            start = pl.multiple_of((2 * (pair - first) + core) * n, n)
            copies.append(
                pltpu.make_async_copy(buffer, outs[k].at[pl.ds(start, n), :], sems.at[k, pair])
            )
            copies[-1].start()
    for copy in copies:
        copy.wait()


def tie(v, *after):
    return lax.optimization_barrier((v, *after))[0]


def rounds(threads):
    done, waiting = {}, {name: next(thread) for name, thread in threads.items()}
    while waiting:
        ready = lax.optimization_barrier(waiting)
        waiting = {}
        for name, value in ready.items():
            try:
                waiting[name] = threads[name].send(value)
            except StopIteration as stop:
                done[name] = stop.value
    return done


def finish_kernel(dims, small, *outs):
    heads, head_size, hidden = dims
    width = small.shape[1]
    wide = 3 * head_size
    for i in range(6):
        outs[i][...] = small[i, :]
    at = 6
    for h in range(heads):
        row, low = at + h * wide // width, h * wide % width
        line = small[row : row + 1, low : low + wide]
        outs[6][h : h + 1, 0:head_size] = line[:, 0:head_size]
        outs[6][h : h + 1, head_size:] = line[:, 2 * head_size :]
    at += -(-heads * wide // width)
    for low in range(0, hidden, width):
        high = min(low + width, hidden)
        outs[8][low:high] = small[at, 0 : high - low]
        at += 1
    held = width // (2 * LANES)
    for h in range(heads):
        low = h % held * 2 * LANES
        row = at + h // held
        outs[7][h : h + 1, :] = small[row : row + 1, low : low + outs[7].shape[1]]


def partner(axis, bit):
    return [(i, i ^ bit) for i in range(lax.axis_size(axis))]


def swap(v, axis, bit):
    return lax.ppermute(v, axis, partner(axis, bit))


def bits_of(count):
    return [1 << i for i in range(count.bit_length() - 1)]


def add_low(a, b):
    return (a.astype(F32) + b.astype(F32)).astype(a.dtype)


def gather_halves(v, axis):
    held = v[None]
    bits = bits_of(lax.axis_size(axis))
    for bit in bits[:-1]:
        held = jnp.concatenate([held, swap(held, axis, bit)], axis=0)
    return held, swap(held, axis, bits[-1])


def sum_halves(v, axis):
    bits = bits_of(lax.axis_size(axis))
    for bit in bits[:-1]:
        other = swap(v, axis, bit)
        shape = other.shape
        other = other.reshape((shape[0] // (2 * bit), 2, bit) + shape[1:])[:, ::-1].reshape(shape)
        v = add_low(v, other)
    return v, swap(v, axis, bits[-1])


def scatter_halves(v, axis, count=None):
    bits = bits_of(count or lax.axis_size(axis))
    for bit in bits[:0:-1]:
        v = add_low(v[:bit], swap(v[bit:], axis, bit))
    return v[:1], swap(v[1:], axis, 1)


def gather_all(v, steps):
    for axis, bit in steps:
        v = jnp.concatenate([v, swap(v, axis, bit)], axis=0)
    return v


def mixed_swap(v, bits):
    size = lax.axis_size("dp")
    return lax.ppermute(v, "dp", [(i, i ^ bits[i & 1]) for i in range(size)])


def add_halves(kept, other):
    half = kept.shape[0] // 2
    return add_low(kept[:half], other[:half]), add_low(kept[half:], other[half:])


def unpack(places, held, before, layout, shapes, name):
    own = not before
    anywhere = pl.BlockSpec(memory_space=pl.ANY)
    return pl.pallas_call(
        functools.partial(unpack_kernel, layout, own),
        grid_spec=pltpu.PrefetchScalarGridSpec(
            num_scalar_prefetch=1,
            grid=(1,),
            in_specs=[whole(held.shape)] + [anywhere] * len(before),
            out_specs=[anywhere] * len(shapes),
            scratch_shapes=[
                *[
                    pltpu.VMEM((last - first, n, shape[1]), F32)
                    for (first, last, _, n, _), shape in zip(layout, shapes)
                ],
                pltpu.SemaphoreType.DMA((len(layout), held.shape[0])),
            ],
        ),
        out_shape=[sds(shape, F32) for shape in shapes],
        input_output_aliases={2 + i: i for i in range(len(before))},
        compiler_params=pltpu.CompilerParams(
            dimension_semantics=("arbitrary",), vmem_limit_bytes=20 * 2**20
        ),
        name=name,
    )(places, held, *before)


def unpack_both(places, own, other, layout, shapes, name):
    first = unpack(places, own, (), layout, shapes, name + "_own")
    return unpack(places, other, tuple(first), layout, shapes, name + "_other")


def largest(count, most):
    return max(n for n in range(1, most + 1) if count % n == 0)


def per_device(
    patches,
    out_grad,
    score_grad,
    crop_size,
    frozen,
    attn_gain,
    attn_shift,
    qkv_weight,
    qkv_bias,
    rel_table,
    proj_weight,
    proj_bias,
    mlp_gain,
    mlp_shift,
    hidden_weight,
    hidden_bias,
    output_weight,
    output_bias,
    prototypes,
):
    rows, width = patches.shape
    padded = -(-rows // 16) * 16
    parts = lax.axis_size("tensor")
    groups = lax.axis_size("dp")
    heads = qkv_weight.shape[1]
    head_size = qkv_weight.shape[2] // 3
    hidden = hidden_weight.shape[1]
    inner = heads * head_size
    group_crops = crop_size.shape[0]
    crops = group_crops // parts
    slots = -(-crops // 16) * 16
    protos = prototypes.shape[0]
    all_rows = parts * padded
    half = parts // 2
    tensor_rank, dp_rank = lax.axis_index("tensor"), lax.axis_index("dp")
    ids = jnp.stack([tensor_rank, dp_rank, dp_rank * parts + tensor_rank]).astype(jnp.int32)
    chunks = groups
    while (width // chunks) % 16 or (hidden // chunks) % 16 or (4 * inner // chunks) % 16:
        chunks //= 2
    pairs = chunks // 2
    scatter = [b for b in bits_of(chunks) if b > 1]
    rest_bits = [b for b in bits_of(groups) if b >= chunks]
    orders_a = (scatter, scatter[1:2] + scatter[:1] + scatter[2:])
    orders_b = orders_a
    vector = whole((width,))

    x0, x1 = gather_halves(patches, "tensor")
    g0, g1 = gather_halves(out_grad, "tensor")

    proto_step = min(1024, protos)
    crop_bits = bits_of(groups)[1:]
    crop_rows = -(-group_crops // 8) * 8
    crop_shape = (groups // 2, crop_rows, width)
    def crop_step(kept, other, bit, *after):
        kept, other = (lax.optimization_barrier((v, after))[0] for v in (kept, other))
        half = kept.shape[0] // 2
        total = kept + other.astype(F32)
        return total[:half], swap(total[half:].astype(BF), "dp", bit)

    w_t = jnp.transpose(qkv_weight, (1, 2, 0)).reshape(3 * inner, width)
    wp = proj_weight.reshape(inner, width)
    unroll = largest(heads, 12)
    unroll_first = largest(heads, 6)
    block3 = lambda a, b: pl.BlockSpec((1, a, b), lambda i, *_: (i, 0, 0))
    halves3 = lambda a, b, dtype: (sds((half, a, b), dtype), block3(a, b))

    def attend(first, x, ids):
        dims = (first, rows, padded, heads, head_size, crops, unroll_first)
        return call(
            functools.partial(attend_kernel, dims),
            (half,),
            [
                block3(rows, width),
                vector,
                vector,
                whole(w_t.shape),
                whole(qkv_bias.shape),
                whole(tables.shape),
                whole(wp.shape),
            ],
            [
                halves3(padded, width, BF),
                halves3(padded, width, BF),
                halves3(3 * inner, padded, BF),
                (
                    sds((half, heads, padded, padded), BF),
                    pl.BlockSpec((1, heads, padded, padded), lambda i, *_: (i, 0, 0, 0)),
                ),
                halves3(inner, padded, BF),
                halves3(padded, width, BF),
            ],
            [
                pltpu.VMEM((padded, width), F32),
                pltpu.VMEM((heads * 2 * SLOTS, padded), BF),
                pltpu.VMEM((padded, padded), F32),
            ],
            2,
            (ids, crop_size, x, attn_gain, attn_shift, w_t, qkv_bias, tables, wp),
            "attend",
            all_rows * 4 * inner * width,
            20,
        )

    crop_keep, crop_send = call(
        functools.partial(crop_grad_kernel, groups, group_crops, crop_bits),
        (protos // proto_step,),
        [
            pl.BlockSpec((score_grad.shape[0], proto_step), lambda i, s: (0, i)),
            pl.BlockSpec((proto_step, width), lambda i, s: (i, 0)),
        ],
        [(sds(crop_shape, F32), whole(crop_shape)), (sds(crop_shape, F32), whole(crop_shape))],
        [pltpu.VMEM((score_grad.shape[0], width), F32)],
        1,
        (ids, score_grad, prototypes),
        "crop_grads",
        2 * score_grad.shape[0] * protos * width,
        24,
    )
    crop_other = swap(tie(crop_send, x1), "dp", 1)
    tables = call(
        functools.partial(table_kernel, heads, head_size**0.5),
        (1,),
        [whole(rel_table.shape)],
        [(sds((heads * 2 * SLOTS, LANES), BF), whole((heads * 2 * SLOTS, LANES)))],
        [],
        1,
        (tie(ids, crop_send), rel_table),
        "tables",
        0,
        8,
    )[0]
    crop_held = crop_step(crop_keep, crop_other, crop_bits[0], tables)
    xf0, h1_0, qkv0, pt0, ot0, a0 = attend(0, x0, tie(ids, crop_held[0]))
    a0, g1 = lax.optimization_barrier((a0, g1))
    b0 = swap(a0, "tensor", 1)
    crop_held = crop_step(*crop_held, crop_bits[1], a0)
    xf1, h1_1, qkv1, pt1, ot1, a1 = attend(half, x1, tie(ids, crop_held[0]))
    b1 = swap(a1, "tensor", 1)
    if parts > 2:
        a_all, b_all = sum_halves(jnp.concatenate([a0, a1]), "tensor")
        a0, a1, b0, b1 = a_all[:half], a_all[half:], b_all[:half], b_all[half:]
    for bit in crop_bits[2:-1]:
        crop_held = crop_step(*crop_held, bit, a1)
    kept, other = (tie(v, a1) for v in crop_held)
    total = kept + other.astype(F32)
    kept, sent = total[:1].astype(BF), total[1:].astype(BF)
    far = crop_bits[-1] * parts
    crop_terms = [total[:1], swap(sent, ("dp", "tensor"), far)]
    for move in range(1, parts):
        crop_terms += [
            swap(kept, ("dp", "tensor"), move),
            swap(sent, ("dp", "tensor"), far + move),
        ]

    crops_slots = -(-group_crops // 16) * 16
    full = whole((parts, padded, width))
    columns = lambda a: whole((a, hidden))
    y1, gy, h2, gz, m, gu, gh2_near, gh2_far, ob, hb = call(
        functools.partial(hidden_kernel, (parts, rows, padded, crops, group_crops)),
        (1,),
        [
            *[whole((half, padded, width))] * 6,
            whole(g0.shape),
            whole(g1.shape),
            *[whole(kept.shape)] * len(crop_terms),
            vector,
            vector,
            vector,
            columns(width),
            columns(1),
            whole((hidden, width)),
        ],
        [
            (sds((parts, padded, width), F32), full),
            (sds((parts, padded, width), F32), full),
            (sds((all_rows, width), BF), whole((all_rows, width))),
            (sds((all_rows, width), BF), whole((all_rows, width))),
            (sds((all_rows, hidden), BF), columns(all_rows)),
            (sds((all_rows, hidden), BF), columns(all_rows)),
            (sds((half, padded, width), BF), whole((half, padded, width))),
            (sds((half, padded, width), BF), whole((half, padded, width))),
            (sds((1, width), F32), whole((1, width))),
            (sds((1, hidden), F32), columns(1)),
        ],
        [
            pltpu.VMEM((padded, width), F32),
            pltpu.VMEM((crops_slots, width), F32),
            pltpu.VMEM((all_rows, width), F32),
        ],
        2,
        (
            ids, crop_size, xf0, xf1, a0, a1, b0, b1, g0, g1, *crop_terms, proj_bias, mlp_gain, mlp_shift,
            hidden_weight, hidden_bias.reshape(1, hidden), output_weight,
        ),
        "hidden",
        6 * all_rows * hidden * width,
        40,
    )
    near_other = swap(gh2_near, "tensor", half)

    chunks_step = chunks
    wide = min(hidden, width)
    n1, n2 = width // chunks, hidden // chunks
    rows_a = (n1 * hidden + n2 * width) // wide
    chunk_a = whole((pairs, rows_a, wide))
    keep_a, send_a = call(
        functools.partial(hidden_grad_kernel, (chunks, chunks_step, wide, orders_a)),
        (1,),
        [
            whole((all_rows, width)),
            whole((all_rows, width)),
            pl.BlockSpec((all_rows, hidden), lambda i, s: (0, i)),
            pl.BlockSpec((all_rows, hidden), lambda i, s: (0, i)),
        ],
        [
            (sds((pairs, rows_a, wide), BF), chunk_a),
            (sds((pairs, rows_a, wide), BF), chunk_a),
        ],
        [pltpu.VMEM((width, all_rows), BF)],
        1,
        (ids, h2, gz, m, gu),
        "hidden_grads",
        4 * all_rows * hidden * width,
        30,
    )
    if parts > 2:
        e_all, f_all = sum_halves(jnp.concatenate([gh2_near, gh2_far]), "tensor")
        gh2_near, gh2_far = e_all[:half], e_all[half:]
        near_other, far_other = f_all[:half], f_all[half:]
    else:
        far_other = swap(tie(gh2_far, near_other), "tensor", half)
    send_a = tie(send_a, near_other)
    cut = pairs // 2
    core_high = swap(send_a[cut:], "dp", 1)
    core_low = swap(send_a[:cut], "dp", 1)

    n_b = 4 * inner // chunks
    chunk_b = whole((pairs, n_b, width))

    def attend_back(first, e0, e1, xf, qkv, pt, ids):
        dims = (first, rows, padded, heads, head_size, crops, unroll)
        at = lambda a, b: pl.BlockSpec((1, a, b), lambda i, *_: (first + i, 0, 0))
        return call(
            functools.partial(attend_back_kernel, dims),
            (half,),
            [
                at(padded, width),
                at(padded, width),
                block3(padded, width),
                block3(padded, width),
                vector,
                block3(padded, width),
                block3(3 * inner, padded),
                pl.BlockSpec((1, heads, padded, padded), lambda i, *_: (i, 0, 0, 0)),
                whole(wp.shape),
                whole(w_t.shape),
            ],
            [
                (sds((half, padded, width), F32), block3(padded, width)),
                (sds((half, padded, width), BF), block3(padded, width)),
                (sds((half, padded, width), BF), block3(padded, width)),
                (sds((half, 3 * inner, padded), BF), block3(3 * inner, padded)),
                (sds((8, width), F32), whole((8, width))),
                (sds((8, 3 * inner), F32), whole((8, 3 * inner))),
                (sds((heads * SLOTS, LANES), F32), whole((heads * SLOTS, LANES))),
            ],
            [pltpu.VMEM((inner, padded), BF), pltpu.VMEM((heads * SLOTS, padded), F32)],
            2,
            (ids, crop_size, y1, gy, e0, e1, mlp_gain, xf, qkv, pt, wp, w_t),
            "attend_back",
            2 * all_rows * 4 * inner * width,
            22,
        )

    z_part = call(
        functools.partial(share_kernel, parts, padded),
        (1,),
        [whole((all_rows, hidden)), whole((hidden, width))],
        [(sds((parts, padded, width), BF), full)],
        [pltpu.VMEM((all_rows, width), F32)],
        0,
        (tie(m, keep_a), output_weight),
        "share",
        2 * all_rows * hidden * width,
        16,
    )[0]
    sent_a = add_low(keep_a[cut:], core_high)
    other_a = mixed_swap(sent_a, list(zip(*orders_a))[0])
    _, gh1_far, ga1, gq1, sums1, qb1, tt1 = attend_back(
        half, gh2_far, near_other, xf1, qkv1, pt1, tie(ids, sent_a)
    )
    gh1_far, core_low = lax.optimization_barrier((gh1_far, core_low))
    kept_a = add_low(tie(keep_a[:cut], gh1_far), core_low)
    z0, z1 = scatter_halves(tie(z_part, gh1_far), "tensor")
    g_own, gh1_near, ga0, gq0, sums0, qb0, tt0 = attend_back(
        0, gh2_near, far_other, xf0, qkv0, pt0, tie(ids, gh1_far)
    )
    small_rows = 6 + -(-3 * inner // width) + -(-hidden // width) + -(-heads // (width // (2 * LANES)))
    small_rows = -(-small_rows // 8) * 8
    args = (ot0, ot1, ga0, ga1, gq0, gq1, h1_0, h1_1, sums0, sums1, qb0, qb1, tt0, tt1, ob, hb)
    keep_b, send_b, small = call(
        functools.partial(attend_grad_kernel, (parts, heads, chunks, orders_b)),
        (1,),
        [whole(v.shape) for v in args],
        [
            (sds((pairs, n_b, width), BF), chunk_b),
            (sds((pairs, n_b, width), BF), chunk_b),
            (sds((small_rows, width), F32), whole((small_rows, width))),
        ],
        [pltpu.VMEM((inner, width), F32), pltpu.VMEM((3 * inner, width), F32)],
        1,
        (tie(ids, other_a), *args),
        "attend_grads",
        2 * all_rows * 4 * inner * width,
        30,
    )

    one = whole((1, padded, width))

    def places_of(orders):
        spots = pair_spots(jnp.arange(pairs, dtype=jnp.int32), dp_rank & (chunks - 1), orders)
        return jnp.concatenate([(dp_rank & 1)[None], *spots]).astype(jnp.int32)

    def all_sum(kept, other, orders, begin, cuts):
        stages = list(zip(*orders))
        for stage in stages[begin:-1]:
            kept, sent = add_halves(kept, other)
            kept, other = yield kept, mixed_swap(sent, stage)
        held = add_low(kept, other)
        for bits in [stages[-1], *[(bit, bit) for bit in rest_bits]]:
            size = held.shape[0] // cuts
            pieces = [held[i * size : (i + 1) * size] for i in range(cuts)]
            for i in range(cuts):
                pieces[i], pieces[i + 1 :], other = yield (
                    pieces[i],
                    pieces[i + 1 :],
                    mixed_swap(pieces[i], bits),
                )
                pieces[i] = add_low(pieces[i], other)
            held = jnp.concatenate(pieces, axis=0) if cuts > 1 else pieces[0]
        for stage in stages[-2::-1]:
            held = jnp.concatenate((yield held, mixed_swap(held, stage)), axis=0)
        return held, swap(held, "dp", 1)

    def hidden_sum():
        kept, other = yield kept_a, other_a
        held, other = yield from all_sum(kept, other, orders_a, 1, 2)
        layout = (
            (0, pairs, 0, n1, hidden // wide),
            (0, pairs, rows_a - n2 * width // wide, n2, width // wide),
        )
        shapes = ((width, hidden), (hidden, width))
        return (yield unpack_both(places_of(orders_a), held, other, layout, shapes, "unpack_hidden"))

    def attend_sum():
        kept, sent = yield keep_b, send_b
        kept, other = yield kept, swap(sent, "dp", 1)
        held, other = yield from all_sum(kept, other, orders_b, 0, 1)
        edge = inner // (2 * n_b)
        layout = ((0, edge, 0, n_b, 1), (edge, pairs, 0, n_b, 1))
        shapes = ((inner, width), (3 * inner, width))
        return unpack_both(places_of(orders_b), held, other, layout, shapes, "unpack_attend")

    def patch():
        yield ()
        near, far = gh1_near, gh1_far
        if half > 1:
            near, far = yield near, swap(far, "tensor", half)
            near, far = scatter_halves(add_low(near, far), "tensor", half)
        else:
            far = swap(far, "tensor", 1)
        near, far = yield near, far
        return (yield call(
            functools.partial(patch_grad_kernel, rows),
            (1,),
            [one, one, one, one, vector],
            [(sds((rows, width), F32), whole((rows, width)))],
            [],
            0,
            (g_own, near, far, xf0, attn_gain),
            "patch_grads",
            0,
            24,
        )[0])

    def head():
        own, other, held = yield z0, z1, small
        block_out, pooled = call(
            functools.partial(result_kernel, (rows, padded, crops)),
            (1,),
            [one, one, one, vector],
            [
                (sds((rows, width), BF), whole((rows, width))),
                (sds((1, slots, width), BF), whole((1, slots, width))),
            ],
            [],
            2,
            (ids, crop_size, y1, own, other, output_bias),
            "result",
            0,
            24,
        )
        steps = [[b * parts] for b in (bits_of(groups)[:2:-1] + bits_of(groups)[1:3])]
        steps += [[1, parts]] if parts == 2 else [[b] for b in [*bits_of(parts), parts]]
        weights = [weight for step in steps for weight in step]
        pooled = pooled[0]
        first = lax.broadcasted_iota(jnp.int32, (small_rows, 1), 0) < 2
        for step in steps:
            count = pooled.shape[0]
            high = lax.reduce_precision(held, 8, 7)
            payload = jnp.concatenate([pooled, high.astype(BF), (held - high).astype(BF)], axis=0)
            moves = [sum(w for k, w in enumerate(step) if i >> k & 1) for i in range(1, 2 ** len(step))]
            pooled, held, *others = yield (
                pooled,
                held,
                *[swap(payload, ("dp", "tensor"), move) for move in moves],
            )
            for move, other in zip(moves, others):
                high = other[count : count + small_rows].astype(F32)
                part = high + other[count + small_rows :].astype(F32)
                held = held + (jnp.where(first, part, 0.0) if move % parts else part)
            pooled = jnp.concatenate([pooled, *[other[:count] for other in others]], axis=0)
        step_spec = pl.BlockSpec((proto_step, width), lambda i, s: (i, 0))
        prototype_grad = call(
            functools.partial(proto_grad_kernel, (crops, slots, weights)),
            (protos // proto_step,),
            [
                pl.BlockSpec((score_grad.shape[0], proto_step), lambda i, s: (0, i)),
                whole(pooled.shape),
                step_spec,
                pl.BlockSpec((1, proto_step), lambda i, s: (0, i)),
            ],
            [(sds((protos, width), F32), step_spec)],
            [pltpu.VMEM((score_grad.shape[0], width), BF)],
            1,
            (ids, score_grad, pooled, prototypes, frozen.reshape(1, protos)),
            "proto_grads",
            2 * score_grad.shape[0] * protos * width,
            40,
        )[0]
        finished = call(
            functools.partial(finish_kernel, (heads, head_size, hidden)),
            (1,),
            [whole(held.shape)],
            [
                *[(sds((width,), F32), whole((width,)))] * 6,
                (sds((heads, 2 * head_size), F32), whole((heads, 2 * head_size))),
                (sds(rel_table.shape, F32), whole(rel_table.shape)),
                (sds((hidden,), F32), whole((hidden,))),
            ],
            [],
            0,
            (held,),
            "finish",
            0,
            8,
        )
        prototype_grad, finished = yield prototype_grad, finished
        return block_out, prototype_grad, finished

    threads = {"A": hidden_sum(), "B": attend_sum(), "H": head(), "P": patch()}
    done = rounds(threads)
    out_w1, out_w2 = done["A"]
    proj_weight_grad, qkv_weight_grad = done["B"]
    block_out, prototype_grad, (*small, qb, rel, hb) = done["H"]
    return (
        block_out,
        done["P"],
        small[0],
        small[1],
        jnp.transpose(qkv_weight_grad.reshape(heads, 3 * head_size, width), (2, 0, 1)),
        qb,
        rel,
        proj_weight_grad.reshape(heads, head_size, width),
        small[4],
        small[2],
        small[3],
        out_w1,
        hb,
        out_w2,
        small[5],
        prototype_grad,
    )


def solution(mesh):
    both = ("dp", "tensor")
    return jax.shard_map(
        per_device,
        mesh=mesh,
        in_specs=(
            P(both, None),
            P(both, None),
            P(None, both),
            P("dp"),
            P(both),
            P(),
            P(),
            P(None, "tensor", None),
            P("tensor", None),
            P("tensor", None),
            P("tensor", None, None),
            P(),
            P(),
            P(),
            P(None, "tensor"),
            P("tensor"),
            P("tensor", None),
            P(),
            P(both, None),
        ),
        out_specs=(
            P(both, None),
            P(both, None),
            P(),
            P(),
            P(None, "tensor", None),
            P("tensor", None),
            P("tensor", None),
            P("tensor", None, None),
            P(),
            P(),
            P(),
            P(None, "tensor"),
            P("tensor"),
            P("tensor", None),
            P(),
            P(both, None),
        ),
        check_vma=False,
    )
```

```python
import functools

import jax
import jax.numpy as jnp
import numpy as np
from jax import lax
from jax.experimental import pallas as pl
from jax.experimental.pallas import tpu as pltpu
from jax.sharding import PartitionSpec as P

EPS = 1e-05
BF = jnp.bfloat16
F32 = jnp.float32
HIGH = lax.Precision.HIGHEST
SIDE = 7
PLACES = SIDE * SIDE
OFFSETS = 2 * SIDE - 1
LAST = (SIDE - 1) * (OFFSETS + 1)
SLOTS = 96
LANES = 128
COST = 0.01


def nn(a, b):
    return jnp.dot(a, b, preferred_element_type=F32)


def nt(a, b):
    return lax.dot_general(a, b, (((1,), (1,)), ((), ())), preferred_element_type=F32)


def split(v):
    high = v.astype(BF)
    return high, (v - high.astype(F32)).astype(BF)


def line(ref):
    return ref[...].reshape(1, -1)


def normalize(v):
    center = v - jnp.mean(v, axis=-1, keepdims=True)
    spread = jnp.mean(center * center, axis=-1, keepdims=True)
    inverse = lax.rsqrt(spread + EPS)
    return center * inverse, inverse


def norm_back(hat, inverse, gain, grad):
    scaled = grad * gain
    first = jnp.mean(scaled, axis=-1, keepdims=True)
    second = jnp.mean(scaled * hat, axis=-1, keepdims=True)
    return (scaled - first - hat * second) * inverse


def row_layout(sizes_ref, base, crops, rows, padded, axis):
    shape = (padded, 1) if axis == 0 else (1, padded)
    position = lax.broadcasted_iota(jnp.int32, shape, axis)
    start = jnp.int32(0)
    segment = jnp.zeros(shape, jnp.int32)
    first = jnp.zeros(shape, jnp.int32)
    length = jnp.zeros(shape, jnp.int32)
    for crop in range(crops):
        size = sizes_ref[base + crop]
        reached = position >= start
        segment = jnp.where(reached, crop, segment)
        first = jnp.where(reached, start, first)
        length = jnp.where(reached, size, length)
        start = start + size
    offset = position - first
    by_seven = offset + ((offset * 37) >> 8) * (OFFSETS - SIDE)
    by_three = offset + ((offset * 11) >> 5) * (OFFSETS - 3)
    place = jnp.where(length == PLACES, by_seven, by_three)
    real = position < rows
    segment = jnp.where(real, segment, crops)
    place = jnp.where(real, place, 2 * LANES)
    return segment, place, jnp.where(real, length, 1).astype(F32)


def call(body, grid, ins, outs, scratch, prefetch, args, name, flops, vmem):
    moved = sum(int(np.prod(a.shape)) * a.dtype.itemsize for a in args)
    moved += sum(int(np.prod(s.shape)) * s.dtype.itemsize for s, _ in outs)
    return pl.pallas_call(
        body,
        grid_spec=pltpu.PrefetchScalarGridSpec(
            num_scalar_prefetch=prefetch,
            grid=grid,
            in_specs=ins,
            out_specs=[spec for _, spec in outs],
            scratch_shapes=scratch,
        ),
        out_shape=[shape for shape, _ in outs],
        compiler_params=pltpu.CompilerParams(
            dimension_semantics=("arbitrary",) * len(grid), vmem_limit_bytes=vmem * 2**20
        ),
        cost_estimate=pl.CostEstimate(
            flops=int(flops * COST), bytes_accessed=int(moved * COST), transcendentals=0
        ),
        name=name,
    )(*args)


def whole(shape):
    zeros = (0,) * len(shape)
    return pl.BlockSpec(tuple(shape), lambda *_: zeros)


def sds(shape, dtype):
    return jax.ShapeDtypeStruct(tuple(shape), dtype)


def crop_grad_kernel(groups, crops, bits, ids, score, proto, keep, send, total):
    step = pl.program_id(0)

    @pl.when(step == 0)
    def _():
        total[...] = jnp.zeros_like(total)

    p = proto[...].astype(F32)
    unit = p * lax.rsqrt(jnp.sum(p * p, axis=1, keepdims=True) + 1e-06)
    total[...] += nn(score[...], unit.astype(BF))

    @pl.when(step == pl.num_programs(0) - 1)
    def _():
        odd = (ids[1] & 1) == 1
        for pair in range(groups // 2):
            at = 0
            for bit in bits:
                at = 2 * at + (((pair ^ (ids[1] >> 1)) >> (bit.bit_length() - 2)) & 1)
            first = total[2 * pair * crops : (2 * pair + 1) * crops, :]
            second = total[(2 * pair + 1) * crops : (2 * pair + 2) * crops, :]
            keep[at, 0:crops, :] = jnp.where(odd, second, first)
            send[at, 0:crops, :] = jnp.where(odd, first, second)
            if keep.shape[1] > crops:
                tail = jnp.zeros((keep.shape[1] - crops, keep.shape[2]), F32)
                keep[at, crops:, :] = tail
                send[at, crops:, :] = tail


def table_kernel(heads, scale, ids, rel, tables):
    for h in range(heads):
        line = jnp.concatenate(
            [rel[h : h + 1, :], jnp.zeros((1, 2 * LANES - rel.shape[1]), F32)], axis=1
        )
        line = jnp.broadcast_to(line * scale, (8, 2 * LANES))
        line = pltpu.roll(line, 2 * LANES - LAST % 8, 1)
        line = jnp.broadcast_to(line[0:1, :], (SLOTS, 2 * LANES))
        slid = pltpu.roll(line, 2 * LANES - LAST // 8 * 8, 1, stride=1, stride_axis=0)
        high, low = split(slid[:, 0:LANES])
        tables[2 * h * SLOTS : (2 * h + 1) * SLOTS, :] = high
        tables[(2 * h + 1) * SLOTS : (2 * h + 2) * SLOTS, :] = low


def attend_kernel(
    dims, ids, sizes, x0, gain, shift, w, bias, tables, wp, xo, ho, qo, po, oo, ao, xs, rr, hide
):
    first, rows, padded, heads, head_size, crops, unroll = dims
    wide = 3 * head_size
    step = pl.program_id(0)
    base = ((first + step) ^ ids[0]) * crops
    tail = padded - 8
    xs[tail:padded, :] = jnp.zeros((padded - tail, xs.shape[1]), F32)
    xs[0:rows, :] = x0[0].astype(F32)
    x = xs[...]
    xo[0] = x.astype(BF)
    hat, _ = normalize(x)
    h1 = (hat * line(gain) + line(shift)).astype(BF)
    ho[0] = h1
    mixed = nt(w[...], h1)
    bias_cols = jnp.transpose(bias[...])
    for h in range(heads):
        low = h * wide
        qo[0, low : low + head_size, :] = (
            mixed[low : low + head_size] + bias_cols[0:head_size, h : h + 1]
        ).astype(BF)
        qo[0, low + head_size : low + 2 * head_size, :] = mixed[
            low + head_size : low + 2 * head_size
        ].astype(BF)
        qo[0, low + 2 * head_size : low + wide, :] = (
            mixed[low + 2 * head_size : low + wide] + bias_cols[head_size : 2 * head_size, h : h + 1]
        ).astype(BF)
    seg_row, place_row, _ = row_layout(sizes, base, crops, rows, padded, 1)
    seg_col, place_col, _ = row_layout(sizes, base, crops, rows, padded, 0)
    hide[...] = jnp.where(seg_col == seg_row, 0.0, -jnp.inf).astype(F32)
    lane = lax.broadcasted_iota(jnp.int32, (padded, LANES), 1)
    hot = (lane == place_col).astype(F32).astype(BF)
    slot = lax.broadcasted_iota(jnp.int32, (LANES, padded), 0)
    hot_t = (slot == place_row).astype(F32).astype(BF)

    rr[...] = nn(tables[...], hot_t).astype(BF)
    zeros = jnp.zeros((2 * LANES - 2 * SLOTS - head_size, padded), BF)

    def some_heads(i, carry):
        for u in range(unroll):
            h = i * unroll + u
            slab = qo[0, pl.ds(pl.multiple_of(h * wide, 32), wide), :]
            q = slab[0:head_size]
            v = slab[2 * head_size : wide]
            k = slab[head_size : 2 * head_size]
            left_t = jnp.transpose(jnp.concatenate([k, hot_t[0:SLOTS]], axis=0))
            left = jnp.concatenate([left_t, hot], axis=1)
            biases = rr[pl.ds(pl.multiple_of(h * 2 * SLOTS, 64), 2 * SLOTS), :]
            right = jnp.concatenate([q, biases, zeros], axis=0)
            s = nn(left, right) * (head_size**-0.5) + hide[...]
            e = jnp.exp(s - jnp.max(s, axis=0, keepdims=True))
            p = (e * (1.0 / jnp.sum(e, axis=0, keepdims=True))).astype(BF)
            po[0, h] = p
            oo[0, pl.ds(pl.multiple_of(h * head_size, 32), head_size), :] = nn(v, p).astype(BF)
        return carry

    lax.fori_loop(0, heads // unroll, some_heads, 0)
    ao[0] = nn(jnp.transpose(oo[0]), wp[...]).astype(BF)


def hidden_kernel(
    dims, ids, sizes, x0, x1, a0, a1, b0, b1, g0, g1, *rest,
):
    parts, rows, padded, crops, group_crops = dims
    terms, rest = rest[: 2 * parts], rest[2 * parts :]
    pb, gain, shift, w1, bias1, w2 = rest[:6]
    y1o, gyo, h2o, gzo, mo, guo, gh0, gh1, obo, hbo, gs, cs, total = rest[6:]
    step = pl.program_id(0)

    @pl.when(step == 0)
    def _():
        cs[...] = jnp.zeros_like(cs)
        cs[0 : terms[0].shape[1], :] = sum(term[0].astype(F32) for term in terms)
        high, low = split(cs[...])
        bias_sum = jnp.zeros((1, gs.shape[1]), F32)
        tail, half = padded - 8, parts // 2
        for r in range(parts):
            x, own, other, g = (x0, a0, b1, g0) if r < half else (x1, a1, b0, g1)
            k = r % half
            y1 = x[k].astype(F32) + (own[k].astype(F32) + other[k].astype(F32)) + line(pb)
            y1o[r] = y1
            hat, _ = normalize(y1)
            h2o[r * padded : (r + 1) * padded, :] = (hat * line(gain) + line(shift)).astype(BF)
            base = (ids[0] ^ r) * crops
            segment, _, length = row_layout(sizes, base, crops, rows, padded, 0)
            lane = lax.broadcasted_iota(jnp.int32, (padded, cs.shape[0]), 1)
            mine = (lane == segment + base) & (segment < crops)
            hot = mine.astype(F32).astype(BF)
            gs[tail:padded, :] = jnp.zeros((padded - tail, gs.shape[1]), F32)
            gs[0:rows, :] = g[k].astype(F32)
            gy = gs[...] + (nn(hot, high) + nn(hot, low)) / length
            gyo[r] = gy
            gzo[r * padded : (r + 1) * padded, :] = gy.astype(BF)
            bias_sum = bias_sum + jnp.sum(gy, axis=0, keepdims=True)
        obo[...] = bias_sum
        total[...] = jnp.zeros_like(total)

    u = nn(h2o[...], w1[...]) + bias1[...]
    spread = 0.5 * (1.0 + lax.erf(u * np.float32(np.sqrt(0.5))))
    mo[...] = (u * spread).astype(BF)
    slope = spread + u * (jnp.exp(-0.5 * u * u) * np.float32(1.0 / np.sqrt(2.0 * np.pi)))
    gu = (nt(gzo[...], w2[...]) * slope).astype(BF)
    guo[...] = gu
    hbo[...] = jnp.sum(gu.astype(F32), axis=0, keepdims=True)
    total[...] += nt(gu, w1[...])

    @pl.when(step == pl.num_programs(0) - 1)
    def _():
        half = parts // 2
        for r in range(parts):
            gho = gh0 if r < half else gh1
            gho[r % half] = total[r * padded : (r + 1) * padded, :].astype(BF)


def spot(pair, mine, core, orders):
    spots = []
    for order in orders:
        at = 0
        for bit in order:
            source = pair if bit == order[-1] else pair ^ mine
            at = 2 * at + ((source >> (bit.bit_length() - 2)) & 1)
        spots.append(at)
    return jnp.where(core == 1, spots[1], spots[0])


def put_chunk(keep, send, spots, odd, first, second, at):
    rows = pl.ds(at, first.shape[0])
    keep[spots[0], rows, :] = jnp.where(odd, second, first).astype(BF)
    send[spots[1], rows, :] = jnp.where(odd, first, second).astype(BF)


def pair_spots(pair, rank, orders):
    core, mine = rank & 1, rank >> 1
    return spot(pair, mine, core, orders), spot(pair, mine, 1 - core, orders)


def hidden_grad_kernel(dims, ids, h2, gz, m, gu, keep, send, h2t):
    chunks, chunks_step, wide, orders = dims
    step = pl.program_id(0)
    rank = ids[1] & (chunks - 1)
    odd = (rank & 1) == 1

    @pl.when(step == 0)
    def _():
        h2t[...] = jnp.transpose(h2[...])

    d1 = nn(h2t[...], gu[...])
    n1 = d1.shape[0] // chunks
    steps = d1.shape[1] // wide
    for pair in range(chunks // 2):
        spots = pair_spots(pair, rank, orders)
        for part in range(steps):
            piece = d1[2 * pair * n1 : (2 * pair + 2) * n1, part * wide : (part + 1) * wide]
            at = pl.multiple_of((step * steps + part) * n1, 16)
            put_chunk(keep, send, spots, odd, piece[:n1], piece[n1:], at)
    d2 = nn(jnp.transpose(m[...]), gz[...])
    n2 = d2.shape[0] // chunks_step
    base = keep.shape[1] - d2.shape[1] // wide * n2
    for pair in range(chunks_step // 2):
        spots = pair_spots(step * (chunks_step // 2) + pair, rank, orders)
        for part in range(d2.shape[1] // wide):
            piece = d2[2 * pair * n2 : (2 * pair + 2) * n2, part * wide : (part + 1) * wide]
            put_chunk(keep, send, spots, odd, piece[:n2], piece[n2:], base + part * n2)


def share_kernel(parts, padded, m, w2, zo, total):
    step = pl.program_id(0)

    @pl.when(step == 0)
    def _():
        total[...] = jnp.zeros_like(total)

    total[...] += nn(m[...], w2[...])

    @pl.when(step == pl.num_programs(0) - 1)
    def _():
        for r in range(parts):
            zo[r] = total[r * padded : (r + 1) * padded, :].astype(BF)


def result_kernel(dims, ids, sizes, y1, z0, z1, bias, out, pooled):
    rows, padded, crops = dims
    y = y1[0] + (z0[0].astype(F32) + z1[0].astype(F32)) + line(bias)
    out[...] = y[0:rows, :].astype(BF)
    segment, _, _ = row_layout(sizes, ids[0] * crops, crops, rows, padded, 1)
    crop = lax.broadcasted_iota(jnp.int32, (pooled.shape[1], padded), 0)
    member = ((crop == segment) & (crop < crops)).astype(F32)
    high, low = split(y)
    hot = member.astype(BF)
    count = jnp.maximum(jnp.sum(member, axis=1, keepdims=True), 1.0)
    pooled[0] = ((nn(hot, high) + nn(hot, low)) / count).astype(BF)


def attend_back_kernel(
    dims, ids, sizes, y1, gy, e0, e1, gain, x, qkv, pt, wp, w, g1o, gho, gao, gqo, sums, qb, tt, go, by
):
    first, rows, padded, heads, head_size, crops, unroll = dims
    wide = 3 * head_size
    step = pl.program_id(0)
    base = ((first + step) ^ ids[0]) * crops

    @pl.when(step == 0)
    def _():
        sums[...] = jnp.zeros_like(sums)
        qb[...] = jnp.zeros_like(qb)
        tt[...] = jnp.zeros_like(tt)

    hat2, inv2 = normalize(y1[0])
    grad2 = e0[0].astype(F32) + e1[0].astype(F32)
    gy1 = gy[0] + norm_back(hat2, inv2, line(gain), grad2)
    g1o[0] = gy1
    ga = gy1.astype(BF)
    gao[0] = ga
    sums[2:3, :] += jnp.sum(grad2 * hat2, axis=0, keepdims=True)
    sums[3:4, :] += jnp.sum(grad2, axis=0, keepdims=True)
    sums[4:5, :] += jnp.sum(gy1, axis=0, keepdims=True)
    go[...] = nt(wp[...], ga).astype(BF)
    _, place_row, _ = row_layout(sizes, base, crops, rows, padded, 1)
    _, place_col, _ = row_layout(sizes, base, crops, rows, padded, 0)
    slot = lax.broadcasted_iota(jnp.int32, (SLOTS, padded), 0)
    hot_t = (slot == LAST - place_row).astype(F32).astype(BF)
    lane = lax.broadcasted_iota(jnp.int32, (padded, LANES), 1)
    hot = (lane == place_col).astype(F32).astype(BF)
    zeros_a = jnp.zeros((LANES - wide, padded), BF)
    zeros_b = jnp.zeros((2 * head_size, padded), BF)
    scale = head_size**-0.5

    def some_heads(i, carry):
        for u in range(unroll):
            h = i * unroll + u
            at = pl.multiple_of(h * wide, 32)
            slab = qkv[0, pl.ds(at, wide), :]
            q = slab[0:head_size]
            k = slab[head_size : 2 * head_size]
            goh = go[pl.ds(pl.multiple_of(h * head_size, 32), head_size), :]
            p = pt[0, h]
            slab_t = jnp.transpose(jnp.concatenate([slab, zeros_a], axis=0))
            gp = nn(slab_t, jnp.concatenate([zeros_b, goh, zeros_a], axis=0))
            pf = p.astype(F32)
            both = pf * gp
            gs = (both - pf * jnp.sum(both, axis=0, keepdims=True)).astype(BF)
            gv = nt(goh, p)
            gk = nt(q, gs)
            gqe = nn(jnp.concatenate([k, hot_t], axis=0), gs)
            gqo[0, pl.ds(at, head_size), :] = (gqe[0:head_size] * scale).astype(BF)
            gqo[0, pl.ds(at + head_size, head_size), :] = (gk * scale).astype(BF)
            gqo[0, pl.ds(at + 2 * head_size, head_size), :] = gv.astype(BF)
            by[pl.ds(pl.multiple_of(h * SLOTS, 32), SLOTS), :] = gqe[head_size:]
        return carry

    lax.fori_loop(0, heads // unroll, some_heads, 0)
    high, low = split(by[...])
    tt[...] += nn(high, hot) + nn(low, hot)
    g = gqo[0]
    qb[...] += nt(jnp.ones((8, padded), BF), g)
    gh1 = nn(jnp.transpose(g), w[...])
    gho[0] = gh1.astype(BF)
    hat1, _ = normalize(x[0].astype(F32))
    sums[0:1, :] += jnp.sum(gh1 * hat1, axis=0, keepdims=True)
    sums[1:2, :] += jnp.sum(gh1, axis=0, keepdims=True)


def attend_grad_kernel(
    dims, ids, o0, o1, ga0, ga1, gq0, gq1, h0, h1, u0, u1, q0, q1, t0, t1, ob, hb, keep, send, small, dp, dq
):
    parts, heads, chunks, orders = dims
    half = parts // 2
    dp[...] = jnp.zeros_like(dp)
    dq[...] = jnp.zeros_like(dq)
    for r in range(parts):
        o, ga, gq, h = (o0, ga0, gq0, h0) if r < half else (o1, ga1, gq1, h1)
        dp[...] += nn(o[r % half], ga[r % half])
        dq[...] += nn(gq[r % half], h[r % half])
    n = (dp.shape[0] + dq.shape[0]) // chunks
    edge = dp.shape[0] // n
    rank = ids[1] & (chunks - 1)
    for pair in range(chunks // 2):
        source, at = (dp, 2 * pair * n) if 2 * pair < edge else (dq, (2 * pair - edge) * n)
        put_chunk(
            keep, send, pair_spots(pair, rank, orders), (rank & 1) == 1,
            source[at : at + n, :], source[at + n : at + 2 * n, :], 0,
        )
    width = small.shape[1]
    small[...] = jnp.zeros_like(small)
    small[0:5, :] = u0[0:5, :] + u1[0:5, :]
    small[5:6, :] = ob[...]
    at = 6
    for line in (q0[0:1, :] + q1[0:1, :], hb[...]):
        for low in range(0, line.shape[1], width):
            high = min(low + width, line.shape[1])
            small[at : at + 1, 0 : high - low] = line[:, low:high]
            at += 1
    held = width // (2 * LANES)
    for h in range(heads):
        block = t0[h * SLOTS : (h + 1) * SLOTS, :] + t1[h * SLOTS : (h + 1) * SLOTS, :]
        block = jnp.concatenate([block, jnp.zeros((SLOTS, LANES), F32)], axis=1)
        slid = pltpu.roll(block, 0, 1, stride=1, stride_axis=0)
        low = h % held * 2 * LANES
        small[at + h // held : at + h // held + 1, low : low + 2 * LANES] = jnp.sum(
            slid, axis=0, keepdims=True
        )


def patch_grad_kernel(rows, g1, e0, e1, x, gain, out):
    hat, inv = normalize(x[0].astype(F32))
    grad = g1[0] + norm_back(hat, inv, line(gain), e0[0].astype(F32) + e1[0].astype(F32))
    out[...] = grad[0:rows, :]


def proto_grad_kernel(dims, ids, score, pooled, proto, frozen, out, ordered):
    crops, slots, weights = dims

    @pl.when(pl.program_id(0) == 0)
    def _():
        count = pooled.shape[0]
        column = lax.broadcasted_iota(jnp.int32, (1, count), 1)
        block = column // slots
        device = jnp.zeros((1, count), jnp.int32)
        for k, weight in enumerate(weights):
            device = device + ((block >> k) & 1) * weight
        inside = column - block * slots
        target = jnp.where(inside < crops, (device ^ ids[2]) * crops + inside, -1)
        row = lax.broadcasted_iota(jnp.int32, (ordered.shape[0], count), 0)
        hot = (row == target).astype(F32).astype(BF)
        ordered[...] = nn(hot, pooled[...]).astype(BF)

    keep = (1 - frozen[...]).astype(F32).astype(BF)
    grad = nn(jnp.transpose(score[...] * keep), ordered[...])
    p = proto[...].astype(F32)
    inverse = lax.rsqrt(jnp.sum(p * p, axis=1, keepdims=True) + 1e-06)
    unit = p * inverse
    out[...] = (grad - unit * jnp.sum(unit * grad, axis=1, keepdims=True)) * inverse


def unpack_kernel(layout, own, places, held, *refs):
    count = len(layout)
    outs, wides, sems = refs[-2 * count - 1 : -count - 1], refs[-count - 1 : -1], refs[-1]
    pairs, _, wide = held.shape
    core = places[0] if own else 1 - places[0]
    copies = []
    for pair in range(pairs):
        at = places[(1 if own else 1 + pairs) + pair]
        for k, (first, last, low, n, parts) in enumerate(layout):
            if not first <= pair < last:
                continue
            buffer = wides[k].at[pair - first]
            for part in range(parts):
                rows = slice(low + part * n, low + (part + 1) * n)
                buffer[:, part * wide : (part + 1) * wide] = held[at, rows, :].astype(F32)
            start = pl.multiple_of((2 * (pair - first) + core) * n, n)
            copies.append(
                pltpu.make_async_copy(buffer, outs[k].at[pl.ds(start, n), :], sems.at[k, pair])
            )
            copies[-1].start()
    for copy in copies:
        copy.wait()


def tie(v, *after):
    return lax.optimization_barrier((v, *after))[0]


def rounds(threads):
    done, waiting = {}, {name: next(thread) for name, thread in threads.items()}
    while waiting:
        ready = lax.optimization_barrier(waiting)
        waiting = {}
        for name, value in ready.items():
            try:
                waiting[name] = threads[name].send(value)
            except StopIteration as stop:
                done[name] = stop.value
    return done


def finish_kernel(dims, small, *outs):
    heads, head_size, hidden = dims
    width = small.shape[1]
    wide = 3 * head_size
    for i in range(6):
        outs[i][...] = small[i, :]
    at = 6
    for h in range(heads):
        row, low = at + h * wide // width, h * wide % width
        line = small[row : row + 1, low : low + wide]
        outs[6][h : h + 1, 0:head_size] = line[:, 0:head_size]
        outs[6][h : h + 1, head_size:] = line[:, 2 * head_size :]
    at += -(-heads * wide // width)
    for low in range(0, hidden, width):
        high = min(low + width, hidden)
        outs[8][low:high] = small[at, 0 : high - low]
        at += 1
    held = width // (2 * LANES)
    for h in range(heads):
        low = h % held * 2 * LANES
        row = at + h // held
        outs[7][h : h + 1, :] = small[row : row + 1, low : low + outs[7].shape[1]]


def partner(axis, bit):
    return [(i, i ^ bit) for i in range(lax.axis_size(axis))]


def swap(v, axis, bit):
    return lax.ppermute(v, axis, partner(axis, bit))


def bits_of(count):
    return [1 << i for i in range(count.bit_length() - 1)]


def add_low(a, b):
    return (a.astype(F32) + b.astype(F32)).astype(a.dtype)


def gather_halves(v, axis):
    held = v[None]
    bits = bits_of(lax.axis_size(axis))
    for bit in bits[:-1]:
        held = jnp.concatenate([held, swap(held, axis, bit)], axis=0)
    return held, swap(held, axis, bits[-1])


def sum_halves(v, axis):
    bits = bits_of(lax.axis_size(axis))
    for bit in bits[:-1]:
        other = swap(v, axis, bit)
        shape = other.shape
        other = other.reshape((shape[0] // (2 * bit), 2, bit) + shape[1:])[:, ::-1].reshape(shape)
        v = add_low(v, other)
    return v, swap(v, axis, bits[-1])


def scatter_halves(v, axis, count=None):
    bits = bits_of(count or lax.axis_size(axis))
    for bit in bits[:0:-1]:
        v = add_low(v[:bit], swap(v[bit:], axis, bit))
    return v[:1], swap(v[1:], axis, 1)


def gather_all(v, steps):
    for axis, bit in steps:
        v = jnp.concatenate([v, swap(v, axis, bit)], axis=0)
    return v


def mixed_swap(v, bits):
    size = lax.axis_size("dp")
    return lax.ppermute(v, "dp", [(i, i ^ bits[i & 1]) for i in range(size)])


def add_halves(kept, other):
    half = kept.shape[0] // 2
    return add_low(kept[:half], other[:half]), add_low(kept[half:], other[half:])


def unpack(places, held, before, layout, shapes, name):
    own = not before
    anywhere = pl.BlockSpec(memory_space=pl.ANY)
    return pl.pallas_call(
        functools.partial(unpack_kernel, layout, own),
        grid_spec=pltpu.PrefetchScalarGridSpec(
            num_scalar_prefetch=1,
            grid=(1,),
            in_specs=[whole(held.shape)] + [anywhere] * len(before),
            out_specs=[anywhere] * len(shapes),
            scratch_shapes=[
                *[
                    pltpu.VMEM((last - first, n, shape[1]), F32)
                    for (first, last, _, n, _), shape in zip(layout, shapes)
                ],
                pltpu.SemaphoreType.DMA((len(layout), held.shape[0])),
            ],
        ),
        out_shape=[sds(shape, F32) for shape in shapes],
        input_output_aliases={2 + i: i for i in range(len(before))},
        compiler_params=pltpu.CompilerParams(
            dimension_semantics=("arbitrary",), vmem_limit_bytes=20 * 2**20
        ),
        name=name,
    )(places, held, *before)


def unpack_both(places, own, other, layout, shapes, name):
    first = unpack(places, own, (), layout, shapes, name + "_own")
    return unpack(places, other, tuple(first), layout, shapes, name + "_other")


def largest(count, most):
    return max(n for n in range(1, most + 1) if count % n == 0)


def per_device(
    patches,
    out_grad,
    score_grad,
    crop_size,
    frozen,
    attn_gain,
    attn_shift,
    qkv_weight,
    qkv_bias,
    rel_table,
    proj_weight,
    proj_bias,
    mlp_gain,
    mlp_shift,
    hidden_weight,
    hidden_bias,
    output_weight,
    output_bias,
    prototypes,
):
    rows, width = patches.shape
    padded = -(-rows // 16) * 16
    parts = lax.axis_size("tensor")
    groups = lax.axis_size("dp")
    heads = qkv_weight.shape[1]
    head_size = qkv_weight.shape[2] // 3
    hidden = hidden_weight.shape[1]
    inner = heads * head_size
    group_crops = crop_size.shape[0]
    crops = group_crops // parts
    slots = -(-crops // 16) * 16
    protos = prototypes.shape[0]
    all_rows = parts * padded
    half = parts // 2
    tensor_rank, dp_rank = lax.axis_index("tensor"), lax.axis_index("dp")
    ids = jnp.stack([tensor_rank, dp_rank, dp_rank * parts + tensor_rank]).astype(jnp.int32)
    chunks = groups
    while (width // chunks) % 16 or (hidden // chunks) % 16 or (4 * inner // chunks) % 16:
        chunks //= 2
    pairs = chunks // 2
    scatter = [b for b in bits_of(chunks) if b > 1]
    rest_bits = [b for b in bits_of(groups) if b >= chunks]
    orders_a = (scatter, scatter[1:2] + scatter[:1] + scatter[2:])
    orders_b = orders_a
    vector = whole((width,))

    x0, x1 = gather_halves(patches, "tensor")
    g0, g1 = gather_halves(out_grad, "tensor")

    proto_step = min(1024, protos)
    crop_bits = bits_of(groups)[1:]
    crop_rows = -(-group_crops // 8) * 8
    crop_shape = (groups // 2, crop_rows, width)
    def crop_step(kept, other, bit, *after):
        kept, other = (lax.optimization_barrier((v, after))[0] for v in (kept, other))
        half = kept.shape[0] // 2
        total = kept + other.astype(F32)
        return total[:half], swap(total[half:].astype(BF), "dp", bit)

    w_t = jnp.transpose(qkv_weight, (1, 2, 0)).reshape(3 * inner, width)
    wp = proj_weight.reshape(inner, width)
    unroll = largest(heads, 12)
    unroll_first = largest(heads, 6)
    block3 = lambda a, b: pl.BlockSpec((1, a, b), lambda i, *_: (i, 0, 0))
    halves3 = lambda a, b, dtype: (sds((half, a, b), dtype), block3(a, b))

    def attend(first, x, ids):
        dims = (first, rows, padded, heads, head_size, crops, unroll_first)
        return call(
            functools.partial(attend_kernel, dims),
            (half,),
            [
                block3(rows, width),
                vector,
                vector,
                whole(w_t.shape),
                whole(qkv_bias.shape),
                whole(tables.shape),
                whole(wp.shape),
            ],
            [
                halves3(padded, width, BF),
                halves3(padded, width, BF),
                halves3(3 * inner, padded, BF),
                (
                    sds((half, heads, padded, padded), BF),
                    pl.BlockSpec((1, heads, padded, padded), lambda i, *_: (i, 0, 0, 0)),
                ),
                halves3(inner, padded, BF),
                halves3(padded, width, BF),
            ],
            [
                pltpu.VMEM((padded, width), F32),
                pltpu.VMEM((heads * 2 * SLOTS, padded), BF),
                pltpu.VMEM((padded, padded), F32),
            ],
            2,
            (ids, crop_size, x, attn_gain, attn_shift, w_t, qkv_bias, tables, wp),
            "attend",
            all_rows * 4 * inner * width,
            20,
        )

    crop_keep, crop_send = call(
        functools.partial(crop_grad_kernel, groups, group_crops, crop_bits),
        (protos // proto_step,),
        [
            pl.BlockSpec((score_grad.shape[0], proto_step), lambda i, s: (0, i)),
            pl.BlockSpec((proto_step, width), lambda i, s: (i, 0)),
        ],
        [(sds(crop_shape, F32), whole(crop_shape)), (sds(crop_shape, F32), whole(crop_shape))],
        [pltpu.VMEM((score_grad.shape[0], width), F32)],
        1,
        (ids, score_grad, prototypes),
        "crop_grads",
        2 * score_grad.shape[0] * protos * width,
        24,
    )
    crop_other = swap(tie(crop_send, x1), "dp", 1)
    tables = call(
        functools.partial(table_kernel, heads, head_size**0.5),
        (1,),
        [whole(rel_table.shape)],
        [(sds((heads * 2 * SLOTS, LANES), BF), whole((heads * 2 * SLOTS, LANES)))],
        [],
        1,
        (tie(ids, crop_send), rel_table),
        "tables",
        0,
        8,
    )[0]
    crop_held = crop_step(crop_keep, crop_other, crop_bits[0], tables)
    xf0, h1_0, qkv0, pt0, ot0, a0 = attend(0, x0, tie(ids, crop_send))
    a0, g1 = lax.optimization_barrier((a0, g1))
    b0 = swap(a0, "tensor", 1)
    crop_held = crop_step(*crop_held, crop_bits[1], a0)
    xf1, h1_1, qkv1, pt1, ot1, a1 = attend(half, x1, tie(ids, crop_held[0]))
    b1 = swap(a1, "tensor", 1)
    if parts > 2:
        a_all, b_all = sum_halves(jnp.concatenate([a0, a1]), "tensor")
        a0, a1, b0, b1 = a_all[:half], a_all[half:], b_all[:half], b_all[half:]
    for bit in crop_bits[2:-1]:
        crop_held = crop_step(*crop_held, bit, a1)
    kept, other = (tie(v, a1) for v in crop_held)
    total = kept + other.astype(F32)
    kept, sent = total[:1].astype(BF), total[1:].astype(BF)
    far = crop_bits[-1] * parts
    crop_terms = [total[:1], swap(sent, ("dp", "tensor"), far)]
    for move in range(1, parts):
        crop_terms += [
            swap(kept, ("dp", "tensor"), move),
            swap(sent, ("dp", "tensor"), far + move),
        ]

    crops_slots = -(-group_crops // 16) * 16
    full = whole((parts, padded, width))
    columns = lambda a: whole((a, hidden))
    y1, gy, h2, gz, m, gu, gh2_near, gh2_far, ob, hb = call(
        functools.partial(hidden_kernel, (parts, rows, padded, crops, group_crops)),
        (1,),
        [
            *[whole((half, padded, width))] * 6,
            whole(g0.shape),
            whole(g1.shape),
            *[whole(kept.shape)] * len(crop_terms),
            vector,
            vector,
            vector,
            columns(width),
            columns(1),
            whole((hidden, width)),
        ],
        [
            (sds((parts, padded, width), F32), full),
            (sds((parts, padded, width), F32), full),
            (sds((all_rows, width), BF), whole((all_rows, width))),
            (sds((all_rows, width), BF), whole((all_rows, width))),
            (sds((all_rows, hidden), BF), columns(all_rows)),
            (sds((all_rows, hidden), BF), columns(all_rows)),
            (sds((half, padded, width), BF), whole((half, padded, width))),
            (sds((half, padded, width), BF), whole((half, padded, width))),
            (sds((1, width), F32), whole((1, width))),
            (sds((1, hidden), F32), columns(1)),
        ],
        [
            pltpu.VMEM((padded, width), F32),
            pltpu.VMEM((crops_slots, width), F32),
            pltpu.VMEM((all_rows, width), F32),
        ],
        2,
        (
            ids, crop_size, xf0, xf1, a0, a1, b0, b1, g0, g1, *crop_terms, proj_bias, mlp_gain, mlp_shift,
            hidden_weight, hidden_bias.reshape(1, hidden), output_weight,
        ),
        "hidden",
        6 * all_rows * hidden * width,
        40,
    )
    near_other = swap(gh2_near, "tensor", half)

    chunks_step = chunks
    wide = min(hidden, width)
    n1, n2 = width // chunks, hidden // chunks
    rows_a = (n1 * hidden + n2 * width) // wide
    chunk_a = whole((pairs, rows_a, wide))
    keep_a, send_a = call(
        functools.partial(hidden_grad_kernel, (chunks, chunks_step, wide, orders_a)),
        (1,),
        [
            whole((all_rows, width)),
            whole((all_rows, width)),
            pl.BlockSpec((all_rows, hidden), lambda i, s: (0, i)),
            pl.BlockSpec((all_rows, hidden), lambda i, s: (0, i)),
        ],
        [
            (sds((pairs, rows_a, wide), BF), chunk_a),
            (sds((pairs, rows_a, wide), BF), chunk_a),
        ],
        [pltpu.VMEM((width, all_rows), BF)],
        1,
        (ids, h2, gz, m, gu),
        "hidden_grads",
        4 * all_rows * hidden * width,
        30,
    )
    if parts > 2:
        e_all, f_all = sum_halves(jnp.concatenate([gh2_near, gh2_far]), "tensor")
        gh2_near, gh2_far = e_all[:half], e_all[half:]
        near_other, far_other = f_all[:half], f_all[half:]
    else:
        far_other = swap(tie(gh2_far, near_other), "tensor", half)
    send_a = tie(send_a, near_other)
    cut = pairs // 2
    core_high = swap(send_a[cut:], "dp", 1)
    core_low = swap(send_a[:cut], "dp", 1)

    n_b = 4 * inner // chunks
    chunk_b = whole((pairs, n_b, width))

    def attend_back(first, e0, e1, xf, qkv, pt, ids):
        dims = (first, rows, padded, heads, head_size, crops, unroll)
        at = lambda a, b: pl.BlockSpec((1, a, b), lambda i, *_: (first + i, 0, 0))
        return call(
            functools.partial(attend_back_kernel, dims),
            (half,),
            [
                at(padded, width),
                at(padded, width),
                block3(padded, width),
                block3(padded, width),
                vector,
                block3(padded, width),
                block3(3 * inner, padded),
                pl.BlockSpec((1, heads, padded, padded), lambda i, *_: (i, 0, 0, 0)),
                whole(wp.shape),
                whole(w_t.shape),
            ],
            [
                (sds((half, padded, width), F32), block3(padded, width)),
                (sds((half, padded, width), BF), block3(padded, width)),
                (sds((half, padded, width), BF), block3(padded, width)),
                (sds((half, 3 * inner, padded), BF), block3(3 * inner, padded)),
                (sds((8, width), F32), whole((8, width))),
                (sds((8, 3 * inner), F32), whole((8, 3 * inner))),
                (sds((heads * SLOTS, LANES), F32), whole((heads * SLOTS, LANES))),
            ],
            [pltpu.VMEM((inner, padded), BF), pltpu.VMEM((heads * SLOTS, padded), F32)],
            2,
            (ids, crop_size, y1, gy, e0, e1, mlp_gain, xf, qkv, pt, wp, w_t),
            "attend_back",
            2 * all_rows * 4 * inner * width,
            22,
        )

    z_part = call(
        functools.partial(share_kernel, parts, padded),
        (1,),
        [whole((all_rows, hidden)), whole((hidden, width))],
        [(sds((parts, padded, width), BF), full)],
        [pltpu.VMEM((all_rows, width), F32)],
        0,
        (tie(m, keep_a), output_weight),
        "share",
        2 * all_rows * hidden * width,
        16,
    )[0]
    sent_a = add_low(keep_a[cut:], core_high)
    other_a = mixed_swap(sent_a, list(zip(*orders_a))[0])
    _, gh1_far, ga1, gq1, sums1, qb1, tt1 = attend_back(
        half, gh2_far, near_other, xf1, qkv1, pt1, tie(ids, sent_a)
    )
    gh1_far, core_low = lax.optimization_barrier((gh1_far, core_low))
    kept_a = add_low(tie(keep_a[:cut], gh1_far), core_low)
    z0, z1 = scatter_halves(tie(z_part, gh1_far), "tensor")
    g_own, gh1_near, ga0, gq0, sums0, qb0, tt0 = attend_back(
        0, gh2_near, far_other, xf0, qkv0, pt0, tie(ids, gh1_far)
    )
    small_rows = 6 + -(-3 * inner // width) + -(-hidden // width) + -(-heads // (width // (2 * LANES)))
    small_rows = -(-small_rows // 8) * 8
    args = (ot0, ot1, ga0, ga1, gq0, gq1, h1_0, h1_1, sums0, sums1, qb0, qb1, tt0, tt1, ob, hb)
    keep_b, send_b, small = call(
        functools.partial(attend_grad_kernel, (parts, heads, chunks, orders_b)),
        (1,),
        [whole(v.shape) for v in args],
        [
            (sds((pairs, n_b, width), BF), chunk_b),
            (sds((pairs, n_b, width), BF), chunk_b),
            (sds((small_rows, width), F32), whole((small_rows, width))),
        ],
        [pltpu.VMEM((inner, width), F32), pltpu.VMEM((3 * inner, width), F32)],
        1,
        (ids, *args),
        "attend_grads",
        2 * all_rows * 4 * inner * width,
        30,
    )

    one = whole((1, padded, width))

    def places_of(orders):
        spots = pair_spots(jnp.arange(pairs, dtype=jnp.int32), dp_rank & (chunks - 1), orders)
        return jnp.concatenate([(dp_rank & 1)[None], *spots]).astype(jnp.int32)

    def all_sum(kept, other, orders, begin, cuts):
        stages = list(zip(*orders))
        for stage in stages[begin:-1]:
            kept, sent = add_halves(kept, other)
            kept, other = yield kept, mixed_swap(sent, stage)
        held = add_low(kept, other)
        for bits in [stages[-1], *[(bit, bit) for bit in rest_bits]]:
            size = held.shape[0] // cuts
            pieces = [held[i * size : (i + 1) * size] for i in range(cuts)]
            for i in range(cuts):
                pieces[i], pieces[i + 1 :], other = yield (
                    pieces[i],
                    pieces[i + 1 :],
                    mixed_swap(pieces[i], bits),
                )
                pieces[i] = add_low(pieces[i], other)
            held = jnp.concatenate(pieces, axis=0) if cuts > 1 else pieces[0]
        for stage in stages[-2::-1]:
            held = jnp.concatenate((yield held, mixed_swap(held, stage)), axis=0)
        return held, swap(held, "dp", 1)

    def hidden_sum():
        kept, other = yield kept_a, other_a
        held, other = yield from all_sum(kept, other, orders_a, 1, 2)
        layout = (
            (0, pairs, 0, n1, hidden // wide),
            (0, pairs, rows_a - n2 * width // wide, n2, width // wide),
        )
        shapes = ((width, hidden), (hidden, width))
        return (yield unpack_both(places_of(orders_a), held, other, layout, shapes, "unpack_hidden"))

    def attend_sum():
        kept, sent = yield keep_b, send_b
        kept, other = yield kept, swap(sent, "dp", 1)
        held, other = yield from all_sum(kept, other, orders_b, 0, 1)
        edge = inner // (2 * n_b)
        layout = ((0, edge, 0, n_b, 1), (edge, pairs, 0, n_b, 1))
        shapes = ((inner, width), (3 * inner, width))
        return unpack_both(places_of(orders_b), held, other, layout, shapes, "unpack_attend")

    def patch():
        yield ()
        near, far = gh1_near, gh1_far
        if half > 1:
            near, far = yield near, swap(far, "tensor", half)
            near, far = scatter_halves(add_low(near, far), "tensor", half)
        else:
            far = swap(far, "tensor", 1)
        near, far = yield near, far
        return (yield call(
            functools.partial(patch_grad_kernel, rows),
            (1,),
            [one, one, one, one, vector],
            [(sds((rows, width), F32), whole((rows, width)))],
            [],
            0,
            (g_own, near, far, xf0, attn_gain),
            "patch_grads",
            0,
            24,
        )[0])

    def head():
        own, other, held = yield z0, z1, small
        block_out, pooled = call(
            functools.partial(result_kernel, (rows, padded, crops)),
            (1,),
            [one, one, one, vector],
            [
                (sds((rows, width), BF), whole((rows, width))),
                (sds((1, slots, width), BF), whole((1, slots, width))),
            ],
            [],
            2,
            (ids, crop_size, y1, own, other, output_bias),
            "result",
            0,
            24,
        )
        steps = [[b * parts] for b in (bits_of(groups)[:2:-1] + bits_of(groups)[1:3])]
        steps += [[1, parts]] if parts == 2 else [[b] for b in [*bits_of(parts), parts]]
        weights = [weight for step in steps for weight in step]
        pooled = pooled[0]
        first = lax.broadcasted_iota(jnp.int32, (small_rows, 1), 0) < 2
        for step in steps:
            count = pooled.shape[0]
            high = lax.reduce_precision(held, 8, 7)
            payload = jnp.concatenate([pooled, high.astype(BF), (held - high).astype(BF)], axis=0)
            moves = [sum(w for k, w in enumerate(step) if i >> k & 1) for i in range(1, 2 ** len(step))]
            pooled, held, *others = yield (
                pooled,
                held,
                *[swap(payload, ("dp", "tensor"), move) for move in moves],
            )
            for move, other in zip(moves, others):
                high = other[count : count + small_rows].astype(F32)
                part = high + other[count + small_rows :].astype(F32)
                held = held + (jnp.where(first, part, 0.0) if move % parts else part)
            pooled = jnp.concatenate([pooled, *[other[:count] for other in others]], axis=0)
        step_spec = pl.BlockSpec((proto_step, width), lambda i, s: (i, 0))
        prototype_grad = call(
            functools.partial(proto_grad_kernel, (crops, slots, weights)),
            (protos // proto_step,),
            [
                pl.BlockSpec((score_grad.shape[0], proto_step), lambda i, s: (0, i)),
                whole(pooled.shape),
                step_spec,
                pl.BlockSpec((1, proto_step), lambda i, s: (0, i)),
            ],
            [(sds((protos, width), F32), step_spec)],
            [pltpu.VMEM((score_grad.shape[0], width), BF)],
            1,
            (ids, score_grad, pooled, prototypes, frozen.reshape(1, protos)),
            "proto_grads",
            2 * score_grad.shape[0] * protos * width,
            40,
        )[0]
        finished = call(
            functools.partial(finish_kernel, (heads, head_size, hidden)),
            (1,),
            [whole(held.shape)],
            [
                *[(sds((width,), F32), whole((width,)))] * 6,
                (sds((heads, 2 * head_size), F32), whole((heads, 2 * head_size))),
                (sds(rel_table.shape, F32), whole(rel_table.shape)),
                (sds((hidden,), F32), whole((hidden,))),
            ],
            [],
            0,
            (held,),
            "finish",
            0,
            8,
        )
        prototype_grad, finished = yield prototype_grad, finished
        return block_out, prototype_grad, finished

    threads = {"A": hidden_sum(), "B": attend_sum(), "H": head(), "P": patch()}
    done = rounds(threads)
    out_w1, out_w2 = done["A"]
    proj_weight_grad, qkv_weight_grad = done["B"]
    block_out, prototype_grad, (*small, qb, rel, hb) = done["H"]
    return (
        block_out,
        done["P"],
        small[0],
        small[1],
        jnp.transpose(qkv_weight_grad.reshape(heads, 3 * head_size, width), (2, 0, 1)),
        qb,
        rel,
        proj_weight_grad.reshape(heads, head_size, width),
        small[4],
        small[2],
        small[3],
        out_w1,
        hb,
        out_w2,
        small[5],
        prototype_grad,
    )


def solution(mesh):
    both = ("dp", "tensor")
    return jax.shard_map(
        per_device,
        mesh=mesh,
        in_specs=(
            P(both, None),
            P(both, None),
            P(None, both),
            P("dp"),
            P(both),
            P(),
            P(),
            P(None, "tensor", None),
            P("tensor", None),
            P("tensor", None),
            P("tensor", None, None),
            P(),
            P(),
            P(),
            P(None, "tensor"),
            P("tensor"),
            P("tensor", None),
            P(),
            P(both, None),
        ),
        out_specs=(
            P(both, None),
            P(both, None),
            P(),
            P(),
            P(None, "tensor", None),
            P("tensor", None),
            P("tensor", None),
            P("tensor", None, None),
            P(),
            P(),
            P(),
            P(None, "tensor"),
            P("tensor"),
            P("tensor", None),
            P(),
            P(both, None),
        ),
        check_vma=False,
    )
```

```python
import functools

import jax
import jax.numpy as jnp
import numpy as np
from jax import lax
from jax.experimental import pallas as pl
from jax.experimental.pallas import tpu as pltpu
from jax.sharding import PartitionSpec as P

EPS = 1e-05
BF = jnp.bfloat16
F32 = jnp.float32
HIGH = lax.Precision.HIGHEST
SIDE = 7
PLACES = SIDE * SIDE
OFFSETS = 2 * SIDE - 1
LAST = (SIDE - 1) * (OFFSETS + 1)
SLOTS = 96
LANES = 128
COST = 0.01


def nn(a, b):
    return jnp.dot(a, b, preferred_element_type=F32)


def nt(a, b):
    return lax.dot_general(a, b, (((1,), (1,)), ((), ())), preferred_element_type=F32)


def split(v):
    high = v.astype(BF)
    return high, (v - high.astype(F32)).astype(BF)


def line(ref):
    return ref[...].reshape(1, -1)


def normalize(v):
    center = v - jnp.mean(v, axis=-1, keepdims=True)
    spread = jnp.mean(center * center, axis=-1, keepdims=True)
    inverse = lax.rsqrt(spread + EPS)
    return center * inverse, inverse


def norm_back(hat, inverse, gain, grad):
    scaled = grad * gain
    first = jnp.mean(scaled, axis=-1, keepdims=True)
    second = jnp.mean(scaled * hat, axis=-1, keepdims=True)
    return (scaled - first - hat * second) * inverse


def row_layout(sizes_ref, base, crops, rows, padded, axis):
    shape = (padded, 1) if axis == 0 else (1, padded)
    position = lax.broadcasted_iota(jnp.int32, shape, axis)
    start = jnp.int32(0)
    segment = jnp.zeros(shape, jnp.int32)
    first = jnp.zeros(shape, jnp.int32)
    length = jnp.zeros(shape, jnp.int32)
    for crop in range(crops):
        size = sizes_ref[base + crop]
        reached = position >= start
        segment = jnp.where(reached, crop, segment)
        first = jnp.where(reached, start, first)
        length = jnp.where(reached, size, length)
        start = start + size
    offset = position - first
    by_seven = offset + ((offset * 37) >> 8) * (OFFSETS - SIDE)
    by_three = offset + ((offset * 11) >> 5) * (OFFSETS - 3)
    place = jnp.where(length == PLACES, by_seven, by_three)
    real = position < rows
    segment = jnp.where(real, segment, crops)
    place = jnp.where(real, place, 2 * LANES)
    return segment, place, jnp.where(real, length, 1).astype(F32)


def call(body, grid, ins, outs, scratch, prefetch, args, name, flops, vmem):
    moved = sum(int(np.prod(a.shape)) * a.dtype.itemsize for a in args)
    moved += sum(int(np.prod(s.shape)) * s.dtype.itemsize for s, _ in outs)
    return pl.pallas_call(
        body,
        grid_spec=pltpu.PrefetchScalarGridSpec(
            num_scalar_prefetch=prefetch,
            grid=grid,
            in_specs=ins,
            out_specs=[spec for _, spec in outs],
            scratch_shapes=scratch,
        ),
        out_shape=[shape for shape, _ in outs],
        compiler_params=pltpu.CompilerParams(
            dimension_semantics=("arbitrary",) * len(grid), vmem_limit_bytes=vmem * 2**20
        ),
        cost_estimate=pl.CostEstimate(
            flops=int(flops * COST), bytes_accessed=int(moved * COST), transcendentals=0
        ),
        name=name,
    )(*args)


def whole(shape):
    zeros = (0,) * len(shape)
    return pl.BlockSpec(tuple(shape), lambda *_: zeros)


def sds(shape, dtype):
    return jax.ShapeDtypeStruct(tuple(shape), dtype)


def crop_grad_kernel(groups, crops, bits, ids, score, proto, keep, send, total):
    step = pl.program_id(0)

    @pl.when(step == 0)
    def _():
        total[...] = jnp.zeros_like(total)

    p = proto[...].astype(F32)
    unit = p * lax.rsqrt(jnp.sum(p * p, axis=1, keepdims=True) + 1e-06)
    total[...] += nn(score[...], unit.astype(BF))

    @pl.when(step == pl.num_programs(0) - 1)
    def _():
        odd = (ids[1] & 1) == 1
        for pair in range(groups // 2):
            at = 0
            for bit in bits:
                at = 2 * at + (((pair ^ (ids[1] >> 1)) >> (bit.bit_length() - 2)) & 1)
            first = total[2 * pair * crops : (2 * pair + 1) * crops, :]
            second = total[(2 * pair + 1) * crops : (2 * pair + 2) * crops, :]
            keep[at, 0:crops, :] = jnp.where(odd, second, first)
            send[at, 0:crops, :] = jnp.where(odd, first, second)
            if keep.shape[1] > crops:
                tail = jnp.zeros((keep.shape[1] - crops, keep.shape[2]), F32)
                keep[at, crops:, :] = tail
                send[at, crops:, :] = tail


def table_kernel(heads, scale, ids, rel, tables):
    for h in range(heads):
        line = jnp.concatenate(
            [rel[h : h + 1, :], jnp.zeros((1, 2 * LANES - rel.shape[1]), F32)], axis=1
        )
        line = jnp.broadcast_to(line * scale, (8, 2 * LANES))
        line = pltpu.roll(line, 2 * LANES - LAST % 8, 1)
        line = jnp.broadcast_to(line[0:1, :], (SLOTS, 2 * LANES))
        slid = pltpu.roll(line, 2 * LANES - LAST // 8 * 8, 1, stride=1, stride_axis=0)
        high, low = split(slid[:, 0:LANES])
        tables[2 * h * SLOTS : (2 * h + 1) * SLOTS, :] = high
        tables[(2 * h + 1) * SLOTS : (2 * h + 2) * SLOTS, :] = low


def attend_kernel(
    dims, ids, sizes, x0, gain, shift, w, bias, tables, wp, xo, ho, qo, po, oo, ao, xs, rr, hide
):
    first, rows, padded, heads, head_size, crops, unroll = dims
    wide = 3 * head_size
    step = pl.program_id(0)
    base = ((first + step) ^ ids[0]) * crops
    tail = padded - 8
    xs[tail:padded, :] = jnp.zeros((padded - tail, xs.shape[1]), F32)
    xs[0:rows, :] = x0[0].astype(F32)
    x = xs[...]
    xo[0] = x.astype(BF)
    hat, _ = normalize(x)
    h1 = (hat * line(gain) + line(shift)).astype(BF)
    ho[0] = h1
    mixed = nt(w[...], h1)
    bias_cols = jnp.transpose(bias[...])
    for h in range(heads):
        low = h * wide
        qo[0, low : low + head_size, :] = (
            mixed[low : low + head_size] + bias_cols[0:head_size, h : h + 1]
        ).astype(BF)
        qo[0, low + head_size : low + 2 * head_size, :] = mixed[
            low + head_size : low + 2 * head_size
        ].astype(BF)
        qo[0, low + 2 * head_size : low + wide, :] = (
            mixed[low + 2 * head_size : low + wide] + bias_cols[head_size : 2 * head_size, h : h + 1]
        ).astype(BF)
    seg_row, place_row, _ = row_layout(sizes, base, crops, rows, padded, 1)
    seg_col, place_col, _ = row_layout(sizes, base, crops, rows, padded, 0)
    hide[...] = jnp.where(seg_col == seg_row, 0.0, -jnp.inf).astype(F32)
    lane = lax.broadcasted_iota(jnp.int32, (padded, LANES), 1)
    hot = (lane == place_col).astype(F32).astype(BF)
    slot = lax.broadcasted_iota(jnp.int32, (LANES, padded), 0)
    hot_t = (slot == place_row).astype(F32).astype(BF)

    rr[...] = nn(tables[...], hot_t).astype(BF)
    zeros = jnp.zeros((2 * LANES - 2 * SLOTS - head_size, padded), BF)

    def some_heads(i, carry):
        for u in range(unroll):
            h = i * unroll + u
            slab = qo[0, pl.ds(pl.multiple_of(h * wide, 32), wide), :]
            q = slab[0:head_size]
            v = slab[2 * head_size : wide]
            k = slab[head_size : 2 * head_size]
            left_t = jnp.transpose(jnp.concatenate([k, hot_t[0:SLOTS]], axis=0))
            left = jnp.concatenate([left_t, hot], axis=1)
            biases = rr[pl.ds(pl.multiple_of(h * 2 * SLOTS, 64), 2 * SLOTS), :]
            right = jnp.concatenate([q, biases, zeros], axis=0)
            s = nn(left, right) * (head_size**-0.5) + hide[...]
            e = jnp.exp(s - jnp.max(s, axis=0, keepdims=True))
            p = (e * (1.0 / jnp.sum(e, axis=0, keepdims=True))).astype(BF)
            po[0, h] = p
            oo[0, pl.ds(pl.multiple_of(h * head_size, 32), head_size), :] = nn(v, p).astype(BF)
        return carry

    lax.fori_loop(0, heads // unroll, some_heads, 0)
    ao[0] = nn(jnp.transpose(oo[0]), wp[...]).astype(BF)


def hidden_kernel(
    dims, ids, sizes, x0, x1, a0, a1, b0, b1, g0, g1, *rest,
):
    parts, rows, padded, crops, group_crops = dims
    terms, rest = rest[: 2 * parts], rest[2 * parts :]
    pb, gain, shift, w1, bias1, w2 = rest[:6]
    y1o, gyo, h2o, gzo, mo, guo, gh0, gh1, obo, hbo, gs, cs, total = rest[6:]
    step = pl.program_id(0)

    @pl.when(step == 0)
    def _():
        cs[...] = jnp.zeros_like(cs)
        cs[0 : terms[0].shape[1], :] = sum(term[0].astype(F32) for term in terms)
        high, low = split(cs[...])
        bias_sum = jnp.zeros((1, gs.shape[1]), F32)
        tail, half = padded - 8, parts // 2
        for r in range(parts):
            x, own, other, g = (x0, a0, b1, g0) if r < half else (x1, a1, b0, g1)
            k = r % half
            y1 = x[k].astype(F32) + (own[k].astype(F32) + other[k].astype(F32)) + line(pb)
            y1o[r] = y1
            hat, _ = normalize(y1)
            h2o[r * padded : (r + 1) * padded, :] = (hat * line(gain) + line(shift)).astype(BF)
            base = (ids[0] ^ r) * crops
            segment, _, length = row_layout(sizes, base, crops, rows, padded, 0)
            lane = lax.broadcasted_iota(jnp.int32, (padded, cs.shape[0]), 1)
            mine = (lane == segment + base) & (segment < crops)
            hot = mine.astype(F32).astype(BF)
            gs[tail:padded, :] = jnp.zeros((padded - tail, gs.shape[1]), F32)
            gs[0:rows, :] = g[k].astype(F32)
            gy = gs[...] + (nn(hot, high) + nn(hot, low)) / length
            gyo[r] = gy
            gzo[r * padded : (r + 1) * padded, :] = gy.astype(BF)
            bias_sum = bias_sum + jnp.sum(gy, axis=0, keepdims=True)
        obo[...] = bias_sum
        total[...] = jnp.zeros_like(total)

    u = nn(h2o[...], w1[...]) + bias1[...]
    spread = 0.5 * (1.0 + lax.erf(u * np.float32(np.sqrt(0.5))))
    mo[...] = (u * spread).astype(BF)
    slope = spread + u * (jnp.exp(-0.5 * u * u) * np.float32(1.0 / np.sqrt(2.0 * np.pi)))
    gu = (nt(gzo[...], w2[...]) * slope).astype(BF)
    guo[...] = gu
    hbo[...] = jnp.sum(gu.astype(F32), axis=0, keepdims=True)
    total[...] += nt(gu, w1[...])

    @pl.when(step == pl.num_programs(0) - 1)
    def _():
        half = parts // 2
        for r in range(parts):
            gho = gh0 if r < half else gh1
            gho[r % half] = total[r * padded : (r + 1) * padded, :].astype(BF)


def spot(pair, mine, core, orders):
    spots = []
    for order in orders:
        at = 0
        for bit in order:
            source = pair if bit == order[-1] else pair ^ mine
            at = 2 * at + ((source >> (bit.bit_length() - 2)) & 1)
        spots.append(at)
    return jnp.where(core == 1, spots[1], spots[0])


def put_chunk(keep, send, spots, odd, first, second, at):
    rows = pl.ds(at, first.shape[0])
    keep[spots[0], rows, :] = jnp.where(odd, second, first).astype(BF)
    send[spots[1], rows, :] = jnp.where(odd, first, second).astype(BF)


def pair_spots(pair, rank, orders):
    core, mine = rank & 1, rank >> 1
    return spot(pair, mine, core, orders), spot(pair, mine, 1 - core, orders)


def hidden_grad_kernel(dims, ids, h2, gz, m, gu, keep, send, h2t):
    chunks, chunks_step, wide, orders = dims
    step = pl.program_id(0)
    rank = ids[1] & (chunks - 1)
    odd = (rank & 1) == 1

    @pl.when(step == 0)
    def _():
        h2t[...] = jnp.transpose(h2[...])

    d1 = nn(h2t[...], gu[...])
    n1 = d1.shape[0] // chunks
    steps = d1.shape[1] // wide
    for pair in range(chunks // 2):
        spots = pair_spots(pair, rank, orders)
        for part in range(steps):
            piece = d1[2 * pair * n1 : (2 * pair + 2) * n1, part * wide : (part + 1) * wide]
            at = pl.multiple_of((step * steps + part) * n1, 16)
            put_chunk(keep, send, spots, odd, piece[:n1], piece[n1:], at)
    d2 = nn(jnp.transpose(m[...]), gz[...])
    n2 = d2.shape[0] // chunks_step
    base = keep.shape[1] - d2.shape[1] // wide * n2
    for pair in range(chunks_step // 2):
        spots = pair_spots(step * (chunks_step // 2) + pair, rank, orders)
        for part in range(d2.shape[1] // wide):
            piece = d2[2 * pair * n2 : (2 * pair + 2) * n2, part * wide : (part + 1) * wide]
            put_chunk(keep, send, spots, odd, piece[:n2], piece[n2:], base + part * n2)


def share_kernel(parts, padded, m, w2, zo, total):
    step = pl.program_id(0)

    @pl.when(step == 0)
    def _():
        total[...] = jnp.zeros_like(total)

    total[...] += nn(m[...], w2[...])

    @pl.when(step == pl.num_programs(0) - 1)
    def _():
        for r in range(parts):
            zo[r] = total[r * padded : (r + 1) * padded, :].astype(BF)


def result_kernel(dims, ids, sizes, y1, z0, z1, bias, out, pooled):
    rows, padded, crops = dims
    y = y1[0] + (z0[0].astype(F32) + z1[0].astype(F32)) + line(bias)
    out[...] = y[0:rows, :].astype(BF)
    segment, _, _ = row_layout(sizes, ids[0] * crops, crops, rows, padded, 1)
    crop = lax.broadcasted_iota(jnp.int32, (pooled.shape[1], padded), 0)
    member = ((crop == segment) & (crop < crops)).astype(F32)
    high, low = split(y)
    hot = member.astype(BF)
    count = jnp.maximum(jnp.sum(member, axis=1, keepdims=True), 1.0)
    pooled[0] = ((nn(hot, high) + nn(hot, low)) / count).astype(BF)


def attend_back_kernel(
    dims, ids, sizes, y1, gy, e0, e1, gain, x, qkv, pt, wp, w, g1o, gho, gao, gqo, sums, qb, tt, go, by
):
    first, rows, padded, heads, head_size, crops, unroll = dims
    wide = 3 * head_size
    step = pl.program_id(0)
    base = ((first + step) ^ ids[0]) * crops

    @pl.when(step == 0)
    def _():
        sums[...] = jnp.zeros_like(sums)
        qb[...] = jnp.zeros_like(qb)
        tt[...] = jnp.zeros_like(tt)

    hat2, inv2 = normalize(y1[0])
    grad2 = e0[0].astype(F32) + e1[0].astype(F32)
    gy1 = gy[0] + norm_back(hat2, inv2, line(gain), grad2)
    g1o[0] = gy1
    ga = gy1.astype(BF)
    gao[0] = ga
    sums[2:3, :] += jnp.sum(grad2 * hat2, axis=0, keepdims=True)
    sums[3:4, :] += jnp.sum(grad2, axis=0, keepdims=True)
    sums[4:5, :] += jnp.sum(gy1, axis=0, keepdims=True)
    go[...] = nt(wp[...], ga).astype(BF)
    _, place_row, _ = row_layout(sizes, base, crops, rows, padded, 1)
    _, place_col, _ = row_layout(sizes, base, crops, rows, padded, 0)
    slot = lax.broadcasted_iota(jnp.int32, (SLOTS, padded), 0)
    hot_t = (slot == LAST - place_row).astype(F32).astype(BF)
    lane = lax.broadcasted_iota(jnp.int32, (padded, LANES), 1)
    hot = (lane == place_col).astype(F32).astype(BF)
    zeros_a = jnp.zeros((LANES - wide, padded), BF)
    zeros_b = jnp.zeros((2 * head_size, padded), BF)
    scale = head_size**-0.5

    def some_heads(i, carry):
        for u in range(unroll):
            h = i * unroll + u
            at = pl.multiple_of(h * wide, 32)
            slab = qkv[0, pl.ds(at, wide), :]
            q = slab[0:head_size]
            k = slab[head_size : 2 * head_size]
            goh = go[pl.ds(pl.multiple_of(h * head_size, 32), head_size), :]
            p = pt[0, h]
            slab_t = jnp.transpose(jnp.concatenate([slab, zeros_a], axis=0))
            gp = nn(slab_t, jnp.concatenate([zeros_b, goh, zeros_a], axis=0))
            pf = p.astype(F32)
            both = pf * gp
            gs = (both - pf * jnp.sum(both, axis=0, keepdims=True)).astype(BF)
            gv = nt(goh, p)
            gk = nt(q, gs)
            gqe = nn(jnp.concatenate([k, hot_t], axis=0), gs)
            gqo[0, pl.ds(at, head_size), :] = (gqe[0:head_size] * scale).astype(BF)
            gqo[0, pl.ds(at + head_size, head_size), :] = (gk * scale).astype(BF)
            gqo[0, pl.ds(at + 2 * head_size, head_size), :] = gv.astype(BF)
            by[pl.ds(pl.multiple_of(h * SLOTS, 32), SLOTS), :] = gqe[head_size:]
        return carry

    lax.fori_loop(0, heads // unroll, some_heads, 0)
    high, low = split(by[...])
    tt[...] += nn(high, hot) + nn(low, hot)
    g = gqo[0]
    qb[...] += nt(jnp.ones((8, padded), BF), g)
    gh1 = nn(jnp.transpose(g), w[...])
    gho[0] = gh1.astype(BF)
    hat1, _ = normalize(x[0].astype(F32))
    sums[0:1, :] += jnp.sum(gh1 * hat1, axis=0, keepdims=True)
    sums[1:2, :] += jnp.sum(gh1, axis=0, keepdims=True)


def attend_grad_kernel(
    dims, ids, o0, o1, ga0, ga1, gq0, gq1, h0, h1, u0, u1, q0, q1, t0, t1, ob, hb, keep, send, small, dp, dq
):
    parts, heads, chunks, orders = dims
    half = parts // 2
    dp[...] = jnp.zeros_like(dp)
    dq[...] = jnp.zeros_like(dq)
    for r in range(parts):
        o, ga, gq, h = (o0, ga0, gq0, h0) if r < half else (o1, ga1, gq1, h1)
        dp[...] += nn(o[r % half], ga[r % half])
        dq[...] += nn(gq[r % half], h[r % half])
    n = (dp.shape[0] + dq.shape[0]) // chunks
    edge = dp.shape[0] // n
    rank = ids[1] & (chunks - 1)
    for pair in range(chunks // 2):
        source, at = (dp, 2 * pair * n) if 2 * pair < edge else (dq, (2 * pair - edge) * n)
        put_chunk(
            keep, send, pair_spots(pair, rank, orders), (rank & 1) == 1,
            source[at : at + n, :], source[at + n : at + 2 * n, :], 0,
        )
    width = small.shape[1]
    small[...] = jnp.zeros_like(small)
    small[0:5, :] = u0[0:5, :] + u1[0:5, :]
    small[5:6, :] = ob[...]
    at = 6
    for line in (q0[0:1, :] + q1[0:1, :], hb[...]):
        for low in range(0, line.shape[1], width):
            high = min(low + width, line.shape[1])
            small[at : at + 1, 0 : high - low] = line[:, low:high]
            at += 1
    held = width // (2 * LANES)
    for h in range(heads):
        block = t0[h * SLOTS : (h + 1) * SLOTS, :] + t1[h * SLOTS : (h + 1) * SLOTS, :]
        block = jnp.concatenate([block, jnp.zeros((SLOTS, LANES), F32)], axis=1)
        slid = pltpu.roll(block, 0, 1, stride=1, stride_axis=0)
        low = h % held * 2 * LANES
        small[at + h // held : at + h // held + 1, low : low + 2 * LANES] = jnp.sum(
            slid, axis=0, keepdims=True
        )


def patch_grad_kernel(rows, g1, e0, e1, x, gain, out):
    hat, inv = normalize(x[0].astype(F32))
    grad = g1[0] + norm_back(hat, inv, line(gain), e0[0].astype(F32) + e1[0].astype(F32))
    out[...] = grad[0:rows, :]


def proto_grad_kernel(dims, ids, score, pooled, proto, frozen, out, ordered):
    crops, slots, weights = dims

    @pl.when(pl.program_id(0) == 0)
    def _():
        count = pooled.shape[0]
        column = lax.broadcasted_iota(jnp.int32, (1, count), 1)
        block = column // slots
        device = jnp.zeros((1, count), jnp.int32)
        for k, weight in enumerate(weights):
            device = device + ((block >> k) & 1) * weight
        inside = column - block * slots
        target = jnp.where(inside < crops, (device ^ ids[2]) * crops + inside, -1)
        row = lax.broadcasted_iota(jnp.int32, (ordered.shape[0], count), 0)
        hot = (row == target).astype(F32).astype(BF)
        ordered[...] = nn(hot, pooled[...]).astype(BF)

    keep = (1 - frozen[...]).astype(F32).astype(BF)
    grad = nn(jnp.transpose(score[...] * keep), ordered[...])
    p = proto[...].astype(F32)
    inverse = lax.rsqrt(jnp.sum(p * p, axis=1, keepdims=True) + 1e-06)
    unit = p * inverse
    out[...] = (grad - unit * jnp.sum(unit * grad, axis=1, keepdims=True)) * inverse


def unpack_kernel(layout, own, places, held, *refs):
    count = len(layout)
    outs, wides, sems = refs[-2 * count - 1 : -count - 1], refs[-count - 1 : -1], refs[-1]
    pairs, _, wide = held.shape
    core = places[0] if own else 1 - places[0]
    copies = []
    for pair in range(pairs):
        at = places[(1 if own else 1 + pairs) + pair]
        for k, (first, last, low, n, parts) in enumerate(layout):
            if not first <= pair < last:
                continue
            buffer = wides[k].at[pair - first]
            for part in range(parts):
                rows = slice(low + part * n, low + (part + 1) * n)
                buffer[:, part * wide : (part + 1) * wide] = held[at, rows, :].astype(F32)
            start = pl.multiple_of((2 * (pair - first) + core) * n, n)
            copies.append(
                pltpu.make_async_copy(buffer, outs[k].at[pl.ds(start, n), :], sems.at[k, pair])
            )
            copies[-1].start()
    for copy in copies:
        copy.wait()


def tie(v, *after):
    return lax.optimization_barrier((v, *after))[0]


def rounds(threads):
    done, waiting = {}, {name: next(thread) for name, thread in threads.items()}
    while waiting:
        ready = lax.optimization_barrier(waiting)
        waiting = {}
        for name, value in ready.items():
            try:
                waiting[name] = threads[name].send(value)
            except StopIteration as stop:
                done[name] = stop.value
    return done


def finish_kernel(dims, small, *outs):
    heads, head_size, hidden = dims
    width = small.shape[1]
    wide = 3 * head_size
    for i in range(6):
        outs[i][...] = small[i, :]
    at = 6
    for h in range(heads):
        row, low = at + h * wide // width, h * wide % width
        line = small[row : row + 1, low : low + wide]
        outs[6][h : h + 1, 0:head_size] = line[:, 0:head_size]
        outs[6][h : h + 1, head_size:] = line[:, 2 * head_size :]
    at += -(-heads * wide // width)
    for low in range(0, hidden, width):
        high = min(low + width, hidden)
        outs[8][low:high] = small[at, 0 : high - low]
        at += 1
    held = width // (2 * LANES)
    for h in range(heads):
        low = h % held * 2 * LANES
        row = at + h // held
        outs[7][h : h + 1, :] = small[row : row + 1, low : low + outs[7].shape[1]]


def partner(axis, bit):
    return [(i, i ^ bit) for i in range(lax.axis_size(axis))]


def swap(v, axis, bit):
    return lax.ppermute(v, axis, partner(axis, bit))


def bits_of(count):
    return [1 << i for i in range(count.bit_length() - 1)]


def add_low(a, b):
    return (a.astype(F32) + b.astype(F32)).astype(a.dtype)


def gather_halves(v, axis):
    held = v[None]
    bits = bits_of(lax.axis_size(axis))
    for bit in bits[:-1]:
        held = jnp.concatenate([held, swap(held, axis, bit)], axis=0)
    return held, swap(held, axis, bits[-1])


def sum_halves(v, axis):
    bits = bits_of(lax.axis_size(axis))
    for bit in bits[:-1]:
        other = swap(v, axis, bit)
        shape = other.shape
        other = other.reshape((shape[0] // (2 * bit), 2, bit) + shape[1:])[:, ::-1].reshape(shape)
        v = add_low(v, other)
    return v, swap(v, axis, bits[-1])


def scatter_halves(v, axis, count=None):
    bits = bits_of(count or lax.axis_size(axis))
    for bit in bits[:0:-1]:
        v = add_low(v[:bit], swap(v[bit:], axis, bit))
    return v[:1], swap(v[1:], axis, 1)


def gather_all(v, steps):
    for axis, bit in steps:
        v = jnp.concatenate([v, swap(v, axis, bit)], axis=0)
    return v


def mixed_swap(v, bits):
    size = lax.axis_size("dp")
    return lax.ppermute(v, "dp", [(i, i ^ bits[i & 1]) for i in range(size)])


def add_halves(kept, other):
    half = kept.shape[0] // 2
    return add_low(kept[:half], other[:half]), add_low(kept[half:], other[half:])


def unpack(places, held, before, layout, shapes, name):
    own = not before
    anywhere = pl.BlockSpec(memory_space=pl.ANY)
    return pl.pallas_call(
        functools.partial(unpack_kernel, layout, own),
        grid_spec=pltpu.PrefetchScalarGridSpec(
            num_scalar_prefetch=1,
            grid=(1,),
            in_specs=[whole(held.shape)] + [anywhere] * len(before),
            out_specs=[anywhere] * len(shapes),
            scratch_shapes=[
                *[
                    pltpu.VMEM((last - first, n, shape[1]), F32)
                    for (first, last, _, n, _), shape in zip(layout, shapes)
                ],
                pltpu.SemaphoreType.DMA((len(layout), held.shape[0])),
            ],
        ),
        out_shape=[sds(shape, F32) for shape in shapes],
        input_output_aliases={2 + i: i for i in range(len(before))},
        compiler_params=pltpu.CompilerParams(
            dimension_semantics=("arbitrary",), vmem_limit_bytes=20 * 2**20
        ),
        name=name,
    )(places, held, *before)


def unpack_both(places, own, other, layout, shapes, name):
    first = unpack(places, own, (), layout, shapes, name + "_own")
    return unpack(places, other, tuple(first), layout, shapes, name + "_other")


def largest(count, most):
    return max(n for n in range(1, most + 1) if count % n == 0)


def per_device(
    patches,
    out_grad,
    score_grad,
    crop_size,
    frozen,
    attn_gain,
    attn_shift,
    qkv_weight,
    qkv_bias,
    rel_table,
    proj_weight,
    proj_bias,
    mlp_gain,
    mlp_shift,
    hidden_weight,
    hidden_bias,
    output_weight,
    output_bias,
    prototypes,
):
    rows, width = patches.shape
    padded = -(-rows // 16) * 16
    parts = lax.axis_size("tensor")
    groups = lax.axis_size("dp")
    heads = qkv_weight.shape[1]
    head_size = qkv_weight.shape[2] // 3
    hidden = hidden_weight.shape[1]
    inner = heads * head_size
    group_crops = crop_size.shape[0]
    crops = group_crops // parts
    slots = -(-crops // 16) * 16
    protos = prototypes.shape[0]
    all_rows = parts * padded
    half = parts // 2
    tensor_rank, dp_rank = lax.axis_index("tensor"), lax.axis_index("dp")
    ids = jnp.stack([tensor_rank, dp_rank, dp_rank * parts + tensor_rank]).astype(jnp.int32)
    chunks = groups
    while (width // chunks) % 16 or (hidden // chunks) % 16 or (4 * inner // chunks) % 16:
        chunks //= 2
    pairs = chunks // 2
    scatter = [b for b in bits_of(chunks) if b > 1]
    rest_bits = [b for b in bits_of(groups) if b >= chunks]
    orders_a = (scatter, scatter[1:2] + scatter[:1] + scatter[2:])
    orders_b = orders_a
    vector = whole((width,))

    x0, x1 = gather_halves(patches, "tensor")
    g0, g1 = gather_halves(out_grad, "tensor")

    proto_step = min(1024, protos)
    crop_bits = bits_of(groups)[1:]
    crop_rows = -(-group_crops // 8) * 8
    crop_shape = (groups // 2, crop_rows, width)
    def crop_step(kept, other, bit, *after):
        kept, other = (lax.optimization_barrier((v, after))[0] for v in (kept, other))
        half = kept.shape[0] // 2
        total = kept + other.astype(F32)
        return total[:half], swap(total[half:].astype(BF), "dp", bit)

    w_t = jnp.transpose(qkv_weight, (1, 2, 0)).reshape(3 * inner, width)
    wp = proj_weight.reshape(inner, width)
    unroll = largest(heads, 12)
    unroll_first = largest(heads, 6)
    block3 = lambda a, b: pl.BlockSpec((1, a, b), lambda i, *_: (i, 0, 0))
    halves3 = lambda a, b, dtype: (sds((half, a, b), dtype), block3(a, b))

    def attend(first, x, ids):
        dims = (first, rows, padded, heads, head_size, crops, unroll_first)
        return call(
            functools.partial(attend_kernel, dims),
            (half,),
            [
                block3(rows, width),
                vector,
                vector,
                whole(w_t.shape),
                whole(qkv_bias.shape),
                whole(tables.shape),
                whole(wp.shape),
            ],
            [
                halves3(padded, width, BF),
                halves3(padded, width, BF),
                halves3(3 * inner, padded, BF),
                (
                    sds((half, heads, padded, padded), BF),
                    pl.BlockSpec((1, heads, padded, padded), lambda i, *_: (i, 0, 0, 0)),
                ),
                halves3(inner, padded, BF),
                halves3(padded, width, BF),
            ],
            [
                pltpu.VMEM((padded, width), F32),
                pltpu.VMEM((heads * 2 * SLOTS, padded), BF),
                pltpu.VMEM((padded, padded), F32),
            ],
            2,
            (ids, crop_size, x, attn_gain, attn_shift, w_t, qkv_bias, tables, wp),
            "attend",
            all_rows * 4 * inner * width,
            20,
        )

    crop_keep, crop_send = call(
        functools.partial(crop_grad_kernel, groups, group_crops, crop_bits),
        (protos // proto_step,),
        [
            pl.BlockSpec((score_grad.shape[0], proto_step), lambda i, s: (0, i)),
            pl.BlockSpec((proto_step, width), lambda i, s: (i, 0)),
        ],
        [(sds(crop_shape, F32), whole(crop_shape)), (sds(crop_shape, F32), whole(crop_shape))],
        [pltpu.VMEM((score_grad.shape[0], width), F32)],
        1,
        (ids, score_grad, prototypes),
        "crop_grads",
        2 * score_grad.shape[0] * protos * width,
        24,
    )
    crop_other = swap(tie(crop_send, x1), "dp", 1)
    tables = call(
        functools.partial(table_kernel, heads, head_size**0.5),
        (1,),
        [whole(rel_table.shape)],
        [(sds((heads * 2 * SLOTS, LANES), BF), whole((heads * 2 * SLOTS, LANES)))],
        [],
        1,
        (tie(ids, crop_send), rel_table),
        "tables",
        0,
        8,
    )[0]
    crop_held = crop_step(crop_keep, crop_other, crop_bits[0], tables)
    xf0, h1_0, qkv0, pt0, ot0, a0 = attend(0, x0, tie(ids, crop_send))
    a0, g1 = lax.optimization_barrier((a0, g1))
    b0 = swap(a0, "tensor", 1)
    crop_held = crop_step(*crop_held, crop_bits[1], a0)
    xf1, h1_1, qkv1, pt1, ot1, a1 = attend(half, x1, tie(ids, crop_held[0]))
    b1 = swap(a1, "tensor", 1)
    if parts > 2:
        a_all, b_all = sum_halves(jnp.concatenate([a0, a1]), "tensor")
        a0, a1, b0, b1 = a_all[:half], a_all[half:], b_all[:half], b_all[half:]
    for bit in crop_bits[2:-1]:
        crop_held = crop_step(*crop_held, bit, a1)
    kept, other = (tie(v, a1) for v in crop_held)
    total = kept + other.astype(F32)
    kept, sent = total[:1].astype(BF), total[1:].astype(BF)
    far = crop_bits[-1] * parts
    crop_terms = [total[:1], swap(sent, ("dp", "tensor"), far)]
    for move in range(1, parts):
        crop_terms += [
            swap(kept, ("dp", "tensor"), move),
            swap(sent, ("dp", "tensor"), far + move),
        ]

    crops_slots = -(-group_crops // 16) * 16
    full = whole((parts, padded, width))
    columns = lambda a: whole((a, hidden))
    y1, gy, h2, gz, m, gu, gh2_near, gh2_far, ob, hb = call(
        functools.partial(hidden_kernel, (parts, rows, padded, crops, group_crops)),
        (1,),
        [
            *[whole((half, padded, width))] * 6,
            whole(g0.shape),
            whole(g1.shape),
            *[whole(kept.shape)] * len(crop_terms),
            vector,
            vector,
            vector,
            columns(width),
            columns(1),
            whole((hidden, width)),
        ],
        [
            (sds((parts, padded, width), F32), full),
            (sds((parts, padded, width), F32), full),
            (sds((all_rows, width), BF), whole((all_rows, width))),
            (sds((all_rows, width), BF), whole((all_rows, width))),
            (sds((all_rows, hidden), BF), columns(all_rows)),
            (sds((all_rows, hidden), BF), columns(all_rows)),
            (sds((half, padded, width), BF), whole((half, padded, width))),
            (sds((half, padded, width), BF), whole((half, padded, width))),
            (sds((1, width), F32), whole((1, width))),
            (sds((1, hidden), F32), columns(1)),
        ],
        [
            pltpu.VMEM((padded, width), F32),
            pltpu.VMEM((crops_slots, width), F32),
            pltpu.VMEM((all_rows, width), F32),
        ],
        2,
        (
            ids, crop_size, xf0, xf1, a0, a1, b0, b1, g0, g1, *crop_terms, proj_bias, mlp_gain, mlp_shift,
            hidden_weight, hidden_bias.reshape(1, hidden), output_weight,
        ),
        "hidden",
        6 * all_rows * hidden * width,
        40,
    )
    near_other = swap(gh2_near, "tensor", half)

    chunks_step = chunks
    wide = min(hidden, width)
    n1, n2 = width // chunks, hidden // chunks
    rows_a = (n1 * hidden + n2 * width) // wide
    chunk_a = whole((pairs, rows_a, wide))
    keep_a, send_a = call(
        functools.partial(hidden_grad_kernel, (chunks, chunks_step, wide, orders_a)),
        (1,),
        [
            whole((all_rows, width)),
            whole((all_rows, width)),
            pl.BlockSpec((all_rows, hidden), lambda i, s: (0, i)),
            pl.BlockSpec((all_rows, hidden), lambda i, s: (0, i)),
        ],
        [
            (sds((pairs, rows_a, wide), BF), chunk_a),
            (sds((pairs, rows_a, wide), BF), chunk_a),
        ],
        [pltpu.VMEM((width, all_rows), BF)],
        1,
        (ids, h2, gz, m, gu),
        "hidden_grads",
        4 * all_rows * hidden * width,
        30,
    )
    if parts > 2:
        e_all, f_all = sum_halves(jnp.concatenate([gh2_near, gh2_far]), "tensor")
        gh2_near, gh2_far = e_all[:half], e_all[half:]
        near_other, far_other = f_all[:half], f_all[half:]
    else:
        far_other = swap(tie(gh2_far, near_other), "tensor", half)
    send_a = tie(send_a, near_other)
    cut = pairs // 2
    core_high = swap(send_a[cut:], "dp", 1)
    core_low = swap(send_a[:cut], "dp", 1)

    n_b = 4 * inner // chunks
    chunk_b = whole((pairs, n_b, width))

    def attend_back(first, e0, e1, xf, qkv, pt, ids):
        dims = (first, rows, padded, heads, head_size, crops, unroll)
        at = lambda a, b: pl.BlockSpec((1, a, b), lambda i, *_: (first + i, 0, 0))
        return call(
            functools.partial(attend_back_kernel, dims),
            (half,),
            [
                at(padded, width),
                at(padded, width),
                block3(padded, width),
                block3(padded, width),
                vector,
                block3(padded, width),
                block3(3 * inner, padded),
                pl.BlockSpec((1, heads, padded, padded), lambda i, *_: (i, 0, 0, 0)),
                whole(wp.shape),
                whole(w_t.shape),
            ],
            [
                (sds((half, padded, width), F32), block3(padded, width)),
                (sds((half, padded, width), BF), block3(padded, width)),
                (sds((half, padded, width), BF), block3(padded, width)),
                (sds((half, 3 * inner, padded), BF), block3(3 * inner, padded)),
                (sds((8, width), F32), whole((8, width))),
                (sds((8, 3 * inner), F32), whole((8, 3 * inner))),
                (sds((heads * SLOTS, LANES), F32), whole((heads * SLOTS, LANES))),
            ],
            [pltpu.VMEM((inner, padded), BF), pltpu.VMEM((heads * SLOTS, padded), F32)],
            2,
            (ids, crop_size, y1, gy, e0, e1, mlp_gain, xf, qkv, pt, wp, w_t),
            "attend_back",
            2 * all_rows * 4 * inner * width,
            22,
        )

    z_part = call(
        functools.partial(share_kernel, parts, padded),
        (1,),
        [whole((all_rows, hidden)), whole((hidden, width))],
        [(sds((parts, padded, width), BF), full)],
        [pltpu.VMEM((all_rows, width), F32)],
        0,
        (tie(m, keep_a), output_weight),
        "share",
        2 * all_rows * hidden * width,
        16,
    )[0]
    sent_a = add_low(keep_a[cut:], core_high)
    other_a = mixed_swap(sent_a, list(zip(*orders_a))[0])
    _, gh1_far, ga1, gq1, sums1, qb1, tt1 = attend_back(
        half, gh2_far, near_other, xf1, qkv1, pt1, tie(ids, sent_a)
    )
    gh1_far, core_low = lax.optimization_barrier((gh1_far, core_low))
    kept_a = add_low(tie(keep_a[:cut], gh1_far), core_low)
    z0, z1 = scatter_halves(tie(z_part, gh1_far), "tensor")
    g_own, gh1_near, ga0, gq0, sums0, qb0, tt0 = attend_back(
        0, gh2_near, far_other, xf0, qkv0, pt0, tie(ids, gh1_far)
    )
    small_rows = 6 + -(-3 * inner // width) + -(-hidden // width) + -(-heads // (width // (2 * LANES)))
    small_rows = -(-small_rows // 8) * 8
    args = (ot0, ot1, ga0, ga1, gq0, gq1, h1_0, h1_1, sums0, sums1, qb0, qb1, tt0, tt1, ob, hb)
    keep_b, send_b, small = call(
        functools.partial(attend_grad_kernel, (parts, heads, chunks, orders_b)),
        (1,),
        [whole(v.shape) for v in args],
        [
            (sds((pairs, n_b, width), BF), chunk_b),
            (sds((pairs, n_b, width), BF), chunk_b),
            (sds((small_rows, width), F32), whole((small_rows, width))),
        ],
        [pltpu.VMEM((inner, width), F32), pltpu.VMEM((3 * inner, width), F32)],
        1,
        (ids, *args),
        "attend_grads",
        2 * all_rows * 4 * inner * width,
        30,
    )

    one = whole((1, padded, width))

    def places_of(orders):
        spots = pair_spots(jnp.arange(pairs, dtype=jnp.int32), dp_rank & (chunks - 1), orders)
        return jnp.concatenate([(dp_rank & 1)[None], *spots]).astype(jnp.int32)

    def all_sum(kept, other, orders, begin, cuts):
        stages = list(zip(*orders))
        for stage in stages[begin:-1]:
            kept, sent = add_halves(kept, other)
            kept, other = yield kept, mixed_swap(sent, stage)
        held = add_low(kept, other)
        for bits in [stages[-1], *[(bit, bit) for bit in rest_bits]]:
            size = held.shape[0] // cuts
            pieces = [held[i * size : (i + 1) * size] for i in range(cuts)]
            for i in range(cuts):
                pieces[i], pieces[i + 1 :], other = yield (
                    pieces[i],
                    pieces[i + 1 :],
                    mixed_swap(pieces[i], bits),
                )
                pieces[i] = add_low(pieces[i], other)
            held = jnp.concatenate(pieces, axis=0) if cuts > 1 else pieces[0]
        for stage in stages[-2::-1]:
            held = jnp.concatenate((yield held, mixed_swap(held, stage)), axis=0)
        return held, swap(held, "dp", 1)

    def hidden_sum():
        kept, other = yield kept_a, other_a
        held, other = yield from all_sum(kept, other, orders_a, 1, 2)
        layout = (
            (0, pairs, 0, n1, hidden // wide),
            (0, pairs, rows_a - n2 * width // wide, n2, width // wide),
        )
        shapes = ((width, hidden), (hidden, width))
        return (yield unpack_both(places_of(orders_a), held, other, layout, shapes, "unpack_hidden"))

    def attend_sum():
        kept, sent = yield keep_b, send_b
        kept, other = yield kept, swap(sent, "dp", 1)
        held, other = yield from all_sum(kept, other, orders_b, 0, 1)
        edge = inner // (2 * n_b)
        layout = ((0, edge, 0, n_b, 1), (edge, pairs, 0, n_b, 1))
        shapes = ((inner, width), (3 * inner, width))
        return unpack_both(places_of(orders_b), held, other, layout, shapes, "unpack_attend")

    def patch():
        yield ()
        yield ()
        near, far = gh1_near, gh1_far
        if half > 1:
            near, far = yield near, swap(far, "tensor", half)
            near, far = scatter_halves(add_low(near, far), "tensor", half)
        else:
            far = swap(far, "tensor", 1)
        near, far = yield near, far
        return (yield call(
            functools.partial(patch_grad_kernel, rows),
            (1,),
            [one, one, one, one, vector],
            [(sds((rows, width), F32), whole((rows, width)))],
            [],
            0,
            (g_own, near, far, xf0, attn_gain),
            "patch_grads",
            0,
            24,
        )[0])

    def head():
        own, other, held = yield z0, z1, small
        block_out, pooled = call(
            functools.partial(result_kernel, (rows, padded, crops)),
            (1,),
            [one, one, one, vector],
            [
                (sds((rows, width), BF), whole((rows, width))),
                (sds((1, slots, width), BF), whole((1, slots, width))),
            ],
            [],
            2,
            (ids, crop_size, y1, own, other, output_bias),
            "result",
            0,
            24,
        )
        steps = [[b * parts] for b in (bits_of(groups)[:2:-1] + bits_of(groups)[1:3])]
        steps += [[1, parts]] if parts == 2 else [[b] for b in [*bits_of(parts), parts]]
        weights = [weight for step in steps for weight in step]
        pooled = pooled[0]
        first = lax.broadcasted_iota(jnp.int32, (small_rows, 1), 0) < 2
        for step in steps:
            count = pooled.shape[0]
            high = lax.reduce_precision(held, 8, 7)
            payload = jnp.concatenate([pooled, high.astype(BF), (held - high).astype(BF)], axis=0)
            moves = [sum(w for k, w in enumerate(step) if i >> k & 1) for i in range(1, 2 ** len(step))]
            pooled, held, *others = yield (
                pooled,
                held,
                *[swap(payload, ("dp", "tensor"), move) for move in moves],
            )
            for move, other in zip(moves, others):
                high = other[count : count + small_rows].astype(F32)
                part = high + other[count + small_rows :].astype(F32)
                held = held + (jnp.where(first, part, 0.0) if move % parts else part)
            pooled = jnp.concatenate([pooled, *[other[:count] for other in others]], axis=0)
        step_spec = pl.BlockSpec((proto_step, width), lambda i, s: (i, 0))
        prototype_grad = call(
            functools.partial(proto_grad_kernel, (crops, slots, weights)),
            (protos // proto_step,),
            [
                pl.BlockSpec((score_grad.shape[0], proto_step), lambda i, s: (0, i)),
                whole(pooled.shape),
                step_spec,
                pl.BlockSpec((1, proto_step), lambda i, s: (0, i)),
            ],
            [(sds((protos, width), F32), step_spec)],
            [pltpu.VMEM((score_grad.shape[0], width), BF)],
            1,
            (ids, score_grad, pooled, prototypes, frozen.reshape(1, protos)),
            "proto_grads",
            2 * score_grad.shape[0] * protos * width,
            40,
        )[0]
        finished = call(
            functools.partial(finish_kernel, (heads, head_size, hidden)),
            (1,),
            [whole(held.shape)],
            [
                *[(sds((width,), F32), whole((width,)))] * 6,
                (sds((heads, 2 * head_size), F32), whole((heads, 2 * head_size))),
                (sds(rel_table.shape, F32), whole(rel_table.shape)),
                (sds((hidden,), F32), whole((hidden,))),
            ],
            [],
            0,
            (held,),
            "finish",
            0,
            8,
        )
        prototype_grad, finished = yield prototype_grad, finished
        return block_out, prototype_grad, finished

    threads = {"A": hidden_sum(), "B": attend_sum(), "H": head(), "P": patch()}
    done = rounds(threads)
    out_w1, out_w2 = done["A"]
    proj_weight_grad, qkv_weight_grad = done["B"]
    block_out, prototype_grad, (*small, qb, rel, hb) = done["H"]
    return (
        block_out,
        done["P"],
        small[0],
        small[1],
        jnp.transpose(qkv_weight_grad.reshape(heads, 3 * head_size, width), (2, 0, 1)),
        qb,
        rel,
        proj_weight_grad.reshape(heads, head_size, width),
        small[4],
        small[2],
        small[3],
        out_w1,
        hb,
        out_w2,
        small[5],
        prototype_grad,
    )


def solution(mesh):
    both = ("dp", "tensor")
    return jax.shard_map(
        per_device,
        mesh=mesh,
        in_specs=(
            P(both, None),
            P(both, None),
            P(None, both),
            P("dp"),
            P(both),
            P(),
            P(),
            P(None, "tensor", None),
            P("tensor", None),
            P("tensor", None),
            P("tensor", None, None),
            P(),
            P(),
            P(),
            P(None, "tensor"),
            P("tensor"),
            P("tensor", None),
            P(),
            P(both, None),
        ),
        out_specs=(
            P(both, None),
            P(both, None),
            P(),
            P(),
            P(None, "tensor", None),
            P("tensor", None),
            P("tensor", None),
            P("tensor", None, None),
            P(),
            P(),
            P(),
            P(None, "tensor"),
            P("tensor"),
            P("tensor", None),
            P(),
            P(both, None),
        ),
        check_vma=False,
    )
```
